32 devices in a mesh: img: 2 (over y), row: 4 (over x, core), col: 4 (over z).
Axes of the slice: x: 2, y: 2, z: 4, core: 2. Of those that a mesh axis runs over, the one named last changes fastest.
Arguments:
- latents: bfloat16 [4, 64, 32, 16], P('img', 'row', 'col'), may hold values from -6 to 6
- skip: bfloat16 [4, 64, 32, 1408], P('img', 'row', 'col'), may hold values from -6 to 6
- temb: bfloat16 [4, 1408], P('img'), may hold values from -6 to 6
- text: bfloat16 [4, 333, 1024], P('img'), may hold values from -6 to 6
- text_len: int32 [4, 2], P('img'), may hold values from 1 to 256, as said below
- extent: int32 [4, 2], P('img'), may hold values from 16 to 64, as said below
- embed_weight: bfloat16 [144, 1408], P(None, ('row', 'col')), may hold values from -0.5 to 0.5
- skip_weight: bfloat16 [2816, 1408], P(('row', 'col')), may hold values from -0.109375 to 0.109375
- shift_weight: bfloat16 [1408, 1408], P(('row', 'col')), may hold values from -0.15625 to 0.15625
- qkv_weight: bfloat16 [1408, 4224], P(('row', 'col')), may hold values from -0.15625 to 0.15625
- out_weight: bfloat16 [1408, 1408], P(('row', 'col')), may hold values from -4 to 4
- cross_query: bfloat16 [1408, 1408], P(('row', 'col')), may hold values from -0.15625 to 0.15625
- cross_keys: bfloat16 [1024, 2816], P(None, ('row', 'col')), may hold values from -0.1875 to 0.1875
- cross_out: bfloat16 [1408, 1408], P(('row', 'col')), may hold values from -1.25 to 1.25
- up_weight: bfloat16 [1408, 6144], P(('row', 'col')), may hold values from -0.15625 to 0.15625
- down_weight: bfloat16 [6144, 1408], P(('row', 'col')), may hold values from -0.15625 to 0.15625
- final_weight: bfloat16 [1408, 144], P(('row', 'col')), may hold values from -0.0546875 to 0.0546875
- norm_gain: bfloat16 [3, 1408], P(None, ('row', 'col')), may hold values from 0.5 to 1.5
- norm_shift: bfloat16 [3, 1408], P(None, ('row', 'col')), may hold values from -1.75 to 1.75
- skip_gain: bfloat16 [2816], P(('row', 'col')), may hold values from 0.5 to 1.5
- skip_shift: bfloat16 [2816], P(('row', 'col')), may hold values from -1.75 to 1.75
- head_gain: bfloat16 [352], P(('row', 'col')), may hold values from 0.5 to 1.5
- head_shift: bfloat16 [352], P(('row', 'col')), may hold values from -1.75 to 1.75
- front_biases: bfloat16 [8448], P(('row', 'col')), may hold values from -1.75 to 1.75
- all_biases: bfloat16 [11776], P(('row', 'col')), may hold values from -1.75 to 1.75
- cross_bias: bfloat16 [2816], P(('row', 'col')), may hold values from -1.75 to 1.75
- cotangent: bfloat16 [4, 64, 32, 16], P('img', 'row', 'col'), may hold values from -6 to 6
Outputs:
- out_latents: float32 [4, 64, 32, 16], P('img', 'row', 'col')
- grad_latents: float32 [4, 64, 32, 16], P('img', 'row', 'col')
- grad_skip: float32 [4, 64, 32, 1408], P('img', 'row', 'col')
- grad_embed: float32 [144, 1408], P(None, ('row', 'col'))
- grad_skip_weight: float32 [2816, 1408], P(('row', 'col'))
- grad_shift: float32 [1408, 1408], P(('row', 'col'))
- grad_qkv: float32 [1408, 4224], P(('row', 'col'))
- grad_out: float32 [1408, 1408], P(('row', 'col'))
- grad_cross_query: float32 [1408, 1408], P(('row', 'col'))
- grad_cross_keys: float32 [1024, 2816], P(None, ('row', 'col'))
- grad_cross_out: float32 [1408, 1408], P(('row', 'col'))
- grad_up: float32 [1408, 6144], P(('row', 'col'))
- grad_down: float32 [6144, 1408], P(('row', 'col'))
- grad_final: float32 [1408, 144], P(('row', 'col'))
- grad_norm_gain: float32 [3, 1408], P(None, ('row', 'col'))
- grad_norm_shift: float32 [3, 1408], P(None, ('row', 'col'))
- grad_skip_gain: float32 [2816], P(('row', 'col'))
- grad_skip_shift: float32 [2816], P(('row', 'col'))
- grad_head_gain: float32 [352], P(('row', 'col'))
- grad_head_shift: float32 [352], P(('row', 'col'))
- grad_front_biases: float32 [8448], P(('row', 'col'))
- grad_biases: float32 [11776], P(('row', 'col'))
- grad_cross_bias: float32 [2816], P(('row', 'col'))
The draws below stay inside these ranges and needn't reach their ends.
Inputs may be any that keep to these rules, and one draw needn't show every extreme that they name: `text_len`: column 0 counts live 77 slots (at most 77), column 1 live mT5 slots; some image has 77 and 256 live tokens, some image a single live 77 token. Each image's extent is either (64, 32) or (32, 16); every aligned block of 2 images holds at least one image of full extent, and some image is of half extent.
All inputs are finite; a program needn't handle non-finite values.
Results may differ from the reference program's by a relative error of at most 0.033.
Values may be sent and summed in bfloat16 or wider, within the bound.
A program may use at most 448 MiB of HBM per device.

```python
import math
import jax
import jax.numpy as jnp
from jax import lax

D = 1408
HEADS = 16
HD = 88
FF = 6144
TD = 1024
CH = 16
CLIP = 77
MT5 = 256
IMG_GRP = 2
TEXT = 333
NB = 144
GH = 64
GW = 32
SEQ = 2048
IMAGES = 4


def draw_text_len(key, part):
    clip_draw = jax.random.randint(jax.random.fold_in(key, 21), (IMAGES,), 1, CLIP + 1)
    long_draw = jax.random.randint(jax.random.fold_in(key, 22), (IMAGES,), 1, MT5 + 1)
    longest = jax.random.randint(jax.random.fold_in(key, 23), (), 0, IMAGES)
    slots = jnp.arange(IMAGES, dtype=jnp.int32)
    clip_len = jnp.where(slots == longest, CLIP, jnp.where(slots == (longest + 1) % IMAGES, 1, clip_draw))
    long_len = jnp.where(slots == longest, MT5, long_draw)
    return jnp.stack([clip_len, long_len], axis=1).astype(jnp.int32)


def draw_extent(key, part):
    slots = jnp.arange(IMAGES, dtype=jnp.int32)
    full_slot = jnp.repeat(jax.random.randint(jax.random.fold_in(key, 11), (IMAGES // IMG_GRP,), 0, IMG_GRP), IMG_GRP)
    coin_draw = jax.random.randint(jax.random.fold_in(key, 12), (IMAGES,), 0, 3)
    forced_half = slots == (full_slot[0] + 1) % IMG_GRP
    is_full = (slots % IMG_GRP == full_slot) | (coin_draw == 0) & jnp.logical_not(forced_half)
    row_extent = jnp.where(is_full, GH, GH // 2)
    col_extent = jnp.where(is_full, GW, GW // 2)
    return jnp.stack([row_extent, col_extent], axis=1).astype(jnp.int32)


def levels(key, shape, shards, low, top_value):
    def one(dim, parts):
        draws = jax.random.uniform(jax.random.fold_in(jax.random.fold_in(key, 6), dim), (parts,), jnp.float32, low / len(shards), top_value / len(shards))
        return jnp.repeat(jnp.exp(draws), shape[dim] // parts).reshape((-1,) + (1,) * (len(shape) - dim - 1))

    loudness = one(*shards[0])
    for cut in shards[1:]:
        loudness = loudness * one(*cut)
    return loudness


def noise(key, shape, scale, limit, shards=(), held_as=jnp.bfloat16):
    factor_of = levels(key, shape, shards, -0.22, 0.18) if shards else 1.0
    entries = jax.random.normal(key, shape, jnp.float32) * scale * factor_of
    return jnp.minimum(jnp.maximum(entries, -limit), limit).astype(held_as)


def setup_inputs(seed: int = 0) -> dict:
    key_of = jax.random.split(jax.random.key(seed), 28)
    latents = noise(key_of[0], (IMAGES, GH, GW, CH), 1.0, 6.0, ((0, 2), (1, 4), (2, 4)))
    skip = noise(key_of[1], (IMAGES, GH, GW, D), 1.0, 6.0, ((0, 2), (1, 4), (2, 4)))
    temb = noise(key_of[2], (IMAGES, D), 1.0, 6.0, ((0, 2),))
    text = noise(key_of[3], (IMAGES, TEXT, TD), 1.0, 6.0, ((0, 2),))
    text_len = draw_text_len(jax.random.fold_in(key_of[27], 71), 0)
    extent = draw_extent(jax.random.fold_in(key_of[27], 71), 0)
    embed_weight = noise(key_of[6], (NB, D), NB ** -0.5, 0.5, ((1, 16),))
    skip_weight = noise(key_of[7], (2 * D, D), (2 * D) ** -0.5, 0.109375, ((0, 16),))
    shift_weight = noise(key_of[8], (D, D), D ** -0.5, 0.15625, ((0, 16),))
    qkv_weight = noise(key_of[9], (D, 3 * D), D ** -0.5, 0.15625, ((0, 16),))
    out_weight = noise(key_of[10], (D, D), (max(1, 4 * D // SEQ)) ** -0.5, 4.0, ((0, 16),))
    cross_query = noise(key_of[11], (D, D), D ** -0.5, 0.15625, ((0, 16),))
    cross_keys = noise(key_of[12], (TD, 2 * D), TD ** -0.5, 0.1875, ((1, 16),))
    cross_out = noise(key_of[13], (D, D), (max(1, D // 64)) ** -0.5, 1.25, ((0, 16),))
    up_weight = noise(key_of[14], (D, FF), D ** -0.5, 0.15625, ((0, 16),))
    down_weight = noise(key_of[15], (FF, D), (FF // 4) ** -0.5, 0.15625, ((0, 16),))
    final_weight = noise(key_of[16], (D, NB), (9 * D) ** -0.5, 0.0546875, ((0, 16),))
    norm_gain = jnp.clip(1.0 + 0.1 * jax.random.normal(key_of[17], (3, D), jnp.float32), 0.5, 1.5).astype(jnp.bfloat16)
    norm_shift = noise(key_of[18], (3, D), 0.3, 1.75, ((1, 16),))
    skip_gain = jnp.clip(1.0 + 0.1 * jax.random.normal(key_of[19], (2 * D,), jnp.float32), 0.5, 1.5).astype(jnp.bfloat16)
    skip_shift = noise(key_of[20], (2 * D,), 0.3, 1.75, ((0, 16),))
    head_gain = jnp.clip(1.0 + 0.1 * jax.random.normal(key_of[21], (4 * HD,), jnp.float32), 0.5, 1.5).astype(jnp.bfloat16)
    head_shift = noise(key_of[22], (4 * HD,), 0.3, 1.75, ((0, 16),))
    front_biases = noise(key_of[23], (6 * D,), 0.3, 1.75, ((0, 16),))
    all_biases = noise(key_of[24], (4 * D + FF,), 0.3, 1.75, ((0, 16),))
    cross_bias = noise(key_of[25], (2 * D,), 0.3, 1.75, ((0, 16),))
    cotangent = noise(key_of[26], (IMAGES, GH, GW, CH), 1.0, 6.0, ((0, 2), (1, 4), (2, 4)))
    return {"latents": latents, "skip": skip, "temb": temb, "text": text, "text_len": text_len, "extent": extent, "embed_weight": embed_weight, "skip_weight": skip_weight, "shift_weight": shift_weight, "qkv_weight": qkv_weight, "out_weight": out_weight, "cross_query": cross_query, "cross_keys": cross_keys, "cross_out": cross_out, "up_weight": up_weight, "down_weight": down_weight, "final_weight": final_weight, "norm_gain": norm_gain, "norm_shift": norm_shift, "skip_gain": skip_gain, "skip_shift": skip_shift, "head_gain": head_gain, "head_shift": head_shift, "front_biases": front_biases, "all_biases": all_biases, "cross_bias": cross_bias, "cotangent": cotangent}


@jax.custom_vjp
def low(v):
    return lax.optimization_barrier(v.astype(jnp.bfloat16)).astype(jnp.float32)

@jax.custom_vjp
def low_back(v):
    return v

def low_keep(v):
    return (low(v), None)

def low_pass(kept, grad):
    return (grad,)

def back_keep(v):
    return (v, None)

def back_low(kept, grad):
    return (low(grad),)
low.defvjp(low_keep, low_pass)
low_back.defvjp(back_keep, back_low)
HIGHEST = lax.Precision.HIGHEST
NORM_EPS = 1e-06
STEPS = ((-1, -1), (-1, 0), (-1, 1), (0, -1), (0, 0), (0, 1), (1, -1), (1, 0), (1, 1))

def product(former, latter):
    return jnp.matmul(former, latter, precision=HIGHEST)

def layer_norm(values, scales, offsets):
    centre = values - lax.optimization_barrier(jnp.mean(values, axis=-1, keepdims=True))
    spread = lax.optimization_barrier(jnp.mean(centre * centre, axis=-1, keepdims=True))
    return centre * lax.rsqrt(spread + NORM_EPS) * scales + offsets

def head_norm(values, scales, offsets):
    old_shape = values.shape
    per_head = values.reshape(old_shape[:-1] + (old_shape[-1] // HD, HD))
    return layer_norm(per_head, scales, offsets).reshape(old_shape)

def rope_tables(row_place, col_place):
    quarter = HD // 4
    pair_index = jnp.arange(HD, dtype=jnp.int32) // 2
    by_row = pair_index < quarter
    within = jnp.where(by_row, pair_index, pair_index - quarter).astype(jnp.float32)
    frequency = jnp.exp(-math.log(10000.0) * within / quarter)
    places = jnp.where(by_row[None, :], row_place[:, None], col_place[:, None])
    angles = jnp.tile(places * frequency[None, :], (1, HEADS))
    return (jnp.cos(angles), jnp.sin(angles))

def rotate(values, cosine_table, sine_table):
    is_even = jnp.arange(values.shape[-1], dtype=jnp.int32) % 2 == 0
    swapped = jnp.where(is_even, -jnp.roll(values, -1, axis=-1), jnp.roll(values, 1, axis=-1))
    return values * cosine_table + swapped * sine_table

def gather_near(padded, tall, broad):
    return jnp.concatenate([padded[..., 1 + step_row:1 + step_row + tall, 1 + step_col:1 + step_col + broad, :] for step_row, step_col in STEPS], axis=-1)

def spread_near(padded, tall, broad, channels):
    result = None
    for number, (step_row, step_col) in enumerate(STEPS):
        portion = padded[..., 1 - step_row:1 - step_row + tall, 1 - step_col:1 - step_col + broad, number * channels:(number + 1) * channels]
        result = portion if result is None else result + portion
    return result

def split_front(vector):
    cut_points = (0, D, 2 * D, 3 * D, 6 * D)
    return tuple((vector[cut_points[number]:cut_points[number + 1]] for number in range(4)))

def split_back(vector):
    cut_points = (0, D, 2 * D, 3 * D, 3 * D + FF, 4 * D + FF)
    return tuple((vector[cut_points[number]:cut_points[number + 1]] for number in range(5)))

def attend(queries, key_rows, value_rows, usable):
    row_count = queries.shape[0]
    block_rows = math.gcd(row_count, 512)
    score_scale = 1.0 / math.sqrt(HD)
    key_heads = key_rows.reshape(key_rows.shape[0], HEADS, HD)
    value_heads = value_rows.reshape(value_rows.shape[0], HEADS, HD)

    def one_block(query_block):
        query_heads = query_block.reshape(block_rows, HEADS, HD)
        scores = low_back(jnp.einsum('qhd,khd->hqk', query_heads, key_heads, precision=HIGHEST) * score_scale)
        scores = jnp.where(usable[None, None, :], scores, -1e+30)
        shifted = jnp.exp(scores - lax.optimization_barrier(jnp.max(scores, axis=-1, keepdims=True)))
        weights = low(shifted / lax.optimization_barrier(jnp.sum(shifted, axis=-1, keepdims=True)))
        mixed = jnp.einsum('hqk,khd->qhd', weights, value_heads, precision=HIGHEST)
        return mixed.reshape(block_rows, D)
    blocks = queries.reshape(row_count // block_rows, block_rows, D)
    return lax.map(jax.checkpoint(one_block), blocks).reshape(row_count, D)

def image_forward(params, latent_tile, skip_tile, time_vec, text_rows, lengths, extents):
    embed_weight, skip_weight, shift_weight, qkv_weight, out_weight, cross_query, cross_keys, cross_out, up_weight, down_weight, final_weight, norm_gain, norm_shift, skip_gain, skip_shift, head_gain, head_shift, front_biases, all_biases, cross_bias = params
    bias_embed, bias_skip, bias_shift, bias_qkv = split_front(front_biases)
    bias_out, bias_cross_q, bias_cross_o, bias_up, bias_down = split_back(all_biases)
    head_gains = head_gain.reshape(4, HD)
    head_offsets = head_shift.reshape(4, HD)
    grid_rows = jnp.arange(GH, dtype=jnp.int32)
    grid_cols = jnp.arange(GW, dtype=jnp.int32)
    inside = ((grid_rows[:, None] < extents[0]) & (grid_cols[None, :] < extents[1])).astype(jnp.float32)
    masked = latent_tile * inside[:, :, None]
    near = gather_near(jnp.pad(masked, ((1, 1), (1, 1), (0, 0))), GH, GW).reshape(SEQ, NB)
    embedded = low_back(product(near, embed_weight) + bias_embed)
    joined = jnp.concatenate([embedded, skip_tile.reshape(SEQ, D)], axis=-1)
    skip_in = low(layer_norm(joined, skip_gain, skip_shift))
    residual = low_back(product(skip_in, skip_weight) + bias_skip)
    shift_row = product(low(jax.nn.silu(time_vec))[None, :], shift_weight)[0] + bias_shift
    normed = low(layer_norm(residual, norm_gain[0], norm_shift[0]) + shift_row)
    qkv_rows = low_back(product(normed, qkv_weight) + bias_qkv)
    row_place = jnp.repeat(grid_rows, GW).astype(jnp.float32)
    col_place = jnp.tile(grid_cols, GH).astype(jnp.float32)
    cosine_table, sine_table = rope_tables(row_place, col_place)
    queries = low(rotate(head_norm(qkv_rows[:, :D], head_gains[0], head_offsets[0]), cosine_table, sine_table))
    key_rows = low(rotate(head_norm(qkv_rows[:, D:2 * D], head_gains[1], head_offsets[1]), cosine_table, sine_table))
    value_rows = low(qkv_rows[:, 2 * D:])
    usable = inside.reshape(SEQ) > 0.5
    attended = low(low_back(attend(queries, key_rows, value_rows, usable)))
    residual = residual + low_back(product(attended, out_weight) + bias_out)
    cross_in = low(layer_norm(residual, norm_gain[1], norm_shift[1]))
    cross_rows = low_back(product(cross_in, cross_query) + bias_cross_q)
    cross_queries = low(rotate(head_norm(cross_rows, head_gains[2], head_offsets[2]), cosine_table, sine_table))
    text_proj = low_back(product(text_rows, cross_keys) + cross_bias)
    text_keys = low(head_norm(text_proj[:, :D], head_gains[3], head_offsets[3]))
    text_values = low(text_proj[:, D:])
    places = jnp.arange(TEXT, dtype=jnp.int32)
    live = (places < lengths[0]) | (places >= CLIP) & (places < CLIP + lengths[1])
    cross_mixed = low(low_back(attend(cross_queries, text_keys, text_values, live)))
    residual = residual + low_back(product(cross_mixed, cross_out) + bias_cross_o)
    mlp_in = low(layer_norm(residual, norm_gain[2], norm_shift[2]))
    hidden = low_back(product(mlp_in, up_weight) + bias_up)
    residual = residual + low_back(product(low(jax.nn.gelu(hidden, approximate=True)), down_weight) + bias_down)
    emitted = low_back(product(low(residual), final_weight))
    emitted = (emitted * inside.reshape(SEQ, 1)).reshape(GH, GW, NB)
    return spread_near(jnp.pad(emitted, ((1, 1), (1, 1), (0, 0))), GH, GW, CH) * inside[:, :, None]

def reference(latents, skip, temb, text, text_len, extent, embed_weight, skip_weight, shift_weight, qkv_weight, out_weight, cross_query, cross_keys, cross_out, up_weight, down_weight, final_weight, norm_gain, norm_shift, skip_gain, skip_shift, head_gain, head_shift, front_biases, all_biases, cross_bias, cotangent):
    params = tuple((array_in.astype(jnp.float32) for array_in in (embed_weight, skip_weight, shift_weight, qkv_weight, out_weight, cross_query, cross_keys, cross_out, up_weight, down_weight, final_weight, norm_gain, norm_shift, skip_gain, skip_shift, head_gain, head_shift, front_biases, all_biases, cross_bias)))
    stacked = (latents.astype(jnp.float32), skip.astype(jnp.float32), temb.astype(jnp.float32), text.astype(jnp.float32), text_len, extent, cotangent.astype(jnp.float32))

    def one_image(totals, inputs):
        latent_tile, skip_tile, time_vec, text_rows, lengths, extents, cot_tile = inputs

        def forward(weights_in, latent_in, skip_in):
            return image_forward(weights_in, latent_in, skip_in, time_vec, text_rows, lengths, extents)
        result, pullback = jax.vjp(forward, params, latent_tile, skip_tile)
        grad_weights, grad_latent, grad_skip_in = pullback(cot_tile)
        totals = jax.tree.map(lambda former, latter: former + latter, totals, grad_weights)
        return (totals, (result, grad_latent, grad_skip_in))
    zero_sums = jax.tree.map(jnp.zeros_like, params)
    totals, (outputs, grad_latents, grad_skips) = lax.scan(one_image, zero_sums, stacked)
    return (outputs, grad_latents, grad_skips, totals[0], totals[1], totals[2], totals[3], totals[4], totals[5], totals[6], totals[7], totals[8], totals[9], totals[10], totals[11], totals[12], totals[13], totals[14], totals[15], totals[16], totals[17], totals[18], totals[19])
```

```python
import functools
import math

import jax
import jax.numpy as jnp
import numpy as np
from jax import lax
from jax.experimental import pallas as pl
from jax.experimental.pallas import tpu as pltpu
from jax.sharding import PartitionSpec as P

D = 1408
HEADS = 16
HD = 88
FF = 6144
CLIP = 77
NORM_EPS = 1e-06
NEG_FILL = -1e30
STEPS = ((-1, -1), (-1, 0), (-1, 1), (0, -1), (0, 0), (0, 1), (1, -1), (1, 0), (1, 1))
GROUP = ("row", "col")
F32 = jnp.float32
BF = jnp.bfloat16
SCALE = 1.0 / math.sqrt(HD)
LOG2E = math.log2(math.e)
NT = (((1,), (1,)), ((), ()))
KEY_BLOCK = 256
QUERY_CHUNK = 1024


def with_halo(block, sides, width):
    for axis, dim in sides:
        count = lax.axis_size(axis)
        forward = [(i, i + 1) for i in range(count - 1)]
        backward = [(target, source) for source, target in forward]
        low = lax.ppermute(
            lax.slice_in_dim(block, block.shape[dim] - width, None, axis=dim), axis, forward
        )
        high = lax.ppermute(lax.slice_in_dim(block, 0, width, axis=dim), axis, backward)
        block = jnp.concatenate([low, block, high], axis=dim)
    return block


def dot(former, latter, former_dims, latter_dims):
    return lax.dot_general(
        former, latter, ((former_dims, latter_dims), ((), ())), preferred_element_type=F32
    )


def matmul(former, latter):
    return dot(former, latter, (former.ndim - 1,), (0,))


def matmul_back(former, latter):
    return dot(former, latter, (former.ndim - 1,), (1,))


def weight_grad(inputs, grads):
    lead = tuple(range(inputs.ndim - 1))
    return dot(inputs, grads, lead, lead)


def column_sum(grads):
    return jnp.sum(grads.astype(F32), axis=tuple(range(grads.ndim - 1)))


def layer_norm(values, scales, offsets):
    centre = values - jnp.mean(values, axis=-1, keepdims=True)
    spread = jnp.mean(centre * centre, axis=-1, keepdims=True)
    return centre * lax.rsqrt(spread + NORM_EPS) * scales + offsets


def angles_of(row_place, col_place):
    pair_index = np.arange(HD) // 2
    quarter = HD // 4
    within = np.where(pair_index < quarter, pair_index, pair_index - quarter).astype(np.float32)
    frequency = np.exp(np.float32(-math.log(10000.0)) * within / np.float32(quarter))
    by_row = jnp.asarray(pair_index < quarter)
    places = jnp.where(by_row[:, None], row_place[None, :], col_place[None, :])
    return places.astype(F32) * jnp.asarray(frequency.astype(np.float32))[:, None]


def gather_near(padded, tall, broad):
    return jnp.concatenate(
        [
            padded[..., 1 + step_row : 1 + step_row + tall, 1 + step_col : 1 + step_col + broad, :]
            for step_row, step_col in STEPS
        ],
        axis=-1,
    )


def spread_near(padded, tall, broad, channels):
    result = None
    for number, (step_row, step_col) in enumerate(STEPS):
        portion = padded[
            ...,
            1 - step_row : 1 - step_row + tall,
            1 - step_col : 1 - step_col + broad,
            number * channels : (number + 1) * channels,
        ]
        result = portion if result is None else result + portion
    return result


def cuts(vector, widths):
    ends = np.cumsum((0,) + widths)
    return [vector[..., ends[i] : ends[i + 1]] for i in range(len(widths))]


def swap_images(values, bit):
    count = lax.axis_size("img")
    return lax.ppermute(values, "img", [(i, i ^ bit) for i in range(count)])


def images_gather(values):
    blocks = values[None]
    while blocks.shape[0] < lax.axis_size("img"):
        blocks = jnp.concatenate([blocks, swap_images(blocks, blocks.shape[0])])
    return blocks


def images_scatter(parts):
    while parts.shape[0] > 1:
        half = parts.shape[0] // 2
        parts = parts[:half] + swap_images(parts[half:].astype(BF), half).astype(F32)
    return parts[0]


def images_sum(values, sent):
    bit = 1
    while bit < lax.axis_size("img"):
        values = values.astype(sent)
        values = values.astype(F32) + swap_images(values, bit).astype(F32)
        bit *= 2
    return values.astype(F32)


def exchange(values, axis, bit):
    size = lax.axis_size(axis)
    return lax.ppermute(values, axis, [(i, i ^ bit) for i in range(size)])


def halves(values, dim, bit):
    keep = lax.dynamic_index_in_dim(values, bit, dim, keepdims=False)
    return keep, lax.dynamic_index_in_dim(values, 1 - bit, dim, keepdims=False)


def core_features(values, dim, core):
    rows = lax.axis_size("row")
    block = values.shape[dim] // rows
    return jnp.concatenate(
        [
            lax.dynamic_slice_in_dim(values, (2 * i + core) * block, block, dim)
            for i in range(rows // 2)
        ],
        axis=dim,
    )


def row_first():
    rows, cols = lax.axis_size("row"), lax.axis_size("col")
    row_bits = [("row", 1 << i) for i in range(1, rows.bit_length() - 1)]
    return row_bits + [("col", 1 << i) for i in range(cols.bit_length() - 1)]


def col_first():
    return sorted(row_first())


def shard_sum(order, after, inputs, grads, input_lead, grad_lead, feature):
    core = lax.axis_index("row") % 2
    give = dot(core_features(inputs, feature, 1 - core), grads, input_lead, grad_lead)
    got = yield exchange(give.astype(BF), "row", 1)
    keep = dot(core_features(inputs, feature, core), grads, input_lead, grad_lead)
    part = yield from scatter_sum(order, keep + got.astype(F32))
    part = yield from after(part)
    return part


def image_parts(grads, dim):
    groups, me = lax.axis_size("img"), lax.axis_index("img")
    width = grads.shape[dim] // groups
    return [
        lax.dynamic_slice_in_dim(grads, (me ^ i) * width, width, dim) for i in range(groups)
    ]


def image_first_sum(order, after, inputs, grads, input_lead, grad_lead, feature, grad_feature):
    core = lax.axis_index("row") % 2
    parts = image_parts(grads, grad_feature)
    given = core_features(inputs, feature, 1 - core)
    gots = yield [
        exchange(dot(given, part, input_lead, grad_lead).astype(BF), "row", 1) for part in parts
    ]
    kept = core_features(inputs, feature, core)
    sums = [
        dot(kept, part, input_lead, grad_lead) + got.astype(F32) for part, got in zip(parts, gots)
    ]
    while len(sums) > 1:
        half = len(sums) // 2
        gots = yield [swap_images(part.astype(BF), half) for part in sums[half:]]
        sums = [part + got.astype(F32) for part, got in zip(sums, gots)]
    part = yield from scatter_sum(order, sums[0])
    part = yield from after(part)
    return part


def row_sum(order, after, values):
    rows = lax.axis_size("row")
    split = values.reshape(rows // 2, 2, -1, values.shape[-1])
    keep, give = halves(split, 1, lax.axis_index("row") % 2)
    got = yield exchange(give, "row", 1)
    part = yield from scatter_sum(order, keep.astype(F32) + got.astype(F32))
    part = yield from after(part)
    return part


def scatter_sum(order, part):
    dims = [d for d in reversed(row_first()) if d[0] == "row"]
    dims += [d for d in reversed(row_first()) if d[0] == "col"]
    width = part.shape[-1]
    part = part.reshape((2,) * len(dims) + (-1, width))
    for axis, bit in order:
        at = dims.index((axis, bit))
        keep, give = halves(part, at, lax.axis_index(axis) // bit % 2)
        del dims[at]
        got = yield exchange(give.astype(BF), axis, bit)
        part = keep + got.astype(F32)
    return part.reshape(-1, width)


def alone(part):
    return part
    yield


def over_images(part):
    bit = 1
    while bit < lax.axis_size("img"):
        part = part.astype(BF)
        got = yield swap_images(part, bit)
        part = part.astype(F32) + got.astype(F32)
        bit *= 2
    return part


def all_images(part):
    bit, blocks = 1, part.astype(BF)[None]
    while bit < lax.axis_size("img"):
        got = yield swap_images(blocks, bit)
        blocks = placed(blocks, got, lax.axis_index("img") // bit % 2, 0)
        blocks = blocks.reshape((-1,) + part.shape)
        bit *= 2
    return blocks


def placed(mine, other, bit, dim):
    first = lax.select(jnp.broadcast_to(bit == 0, mine.shape), mine, other)
    last = lax.select(jnp.broadcast_to(bit == 0, mine.shape), other, mine)
    return jnp.stack([first, last], axis=dim)


def gather_rows(values):
    rows, cols = lax.axis_size("row"), lax.axis_size("col")
    row_index, col_index = lax.axis_index("row"), lax.axis_index("col")
    tail = values.shape
    bit, blocks = cols // 2, values[None]
    while bit >= 1:
        blocks = placed(blocks, exchange(blocks, "col", bit), col_index // bit % 2, 1)
        blocks = blocks.reshape((-1,) + tail)
        bit //= 2
    blocks = blocks[None]
    bit = rows // 2
    while bit >= 1:
        blocks = placed(blocks, exchange(blocks, "row", bit), row_index // bit % 2, 1)
        blocks = blocks.reshape((-1, cols) + tail)
        bit //= 2
    return blocks.reshape((-1,) + tail[1:])


class Sums:
    def __init__(self):
        self.running = {}
        self.done = {}

    def begin(self, name, *work, order=None, after=over_images):
        kind = {1: row_sum, 5: shard_sum, 6: image_first_sum}[len(work)]
        maker = kind(order or row_first(), after, *work)
        self.running[name] = (maker, next(maker))

    def step(self, value, *names):
        names = [name for name in names if name in self.running]
        if not names:
            return value
        tied = lax.optimization_barrier((value, *[self.running[name][1] for name in names]))
        for name, got in zip(names, tied[1:]):
            self.move(name, got)
        return tied[0]

    def move(self, name, got):
        maker = self.running[name][0]
        try:
            self.running[name] = (maker, maker.send(got))
        except StopIteration as stop:
            del self.running[name]
            self.done[name] = stop.value

    def finish(self):
        while self.running:
            for name in list(self.running):
                self.move(name, self.running[name][1])
        return self.done


def unit_rows(values):
    centre = values - jnp.mean(values, axis=0, keepdims=True)
    rstd = lax.rsqrt(jnp.mean(centre * centre, axis=0, keepdims=True) + NORM_EPS)
    return centre * rstd, rstd


def swap_pairs(values, back):
    rows = values.shape[0]
    even = lax.broadcasted_iota(jnp.int32, values.shape, 0) % 2 == 0
    up = pltpu.roll(values, rows - 1, 0)
    down = pltpu.roll(values, 1, 0)
    return jnp.where(even, up, -down) if back else jnp.where(even, -up, down)


def turn(values, cos, sin):
    return values * cos + swap_pairs(values, False) * sin


def turn_back(values, cos, sin):
    return values * cos + swap_pairs(values, True) * sin


def tiles(ref, part, count):
    return jnp.concatenate([ref[s, 0, part] for s in range(count)], axis=1)


def key_blocks(geo, ext_ref, job):
    count, tile_rows, tile_cols, col_tiles, block_tiles = geo
    rows = ext_ref[job, 0] // tile_rows
    groups = ext_ref[job, 1] // (block_tiles * tile_cols)

    def place(i):
        block = i // groups * (col_tiles // block_tiles) + i % groups
        return pl.multiple_of(block * KEY_BLOCK, KEY_BLOCK)

    return rows * groups, place


def attend_kernel(
    geo, ext_ref, qkv_ref, cos_ref, sin_ref, head_ref, out_ref, keep_ref, total_ref,
    q_s, kt_s, v_s, m_s, l_s,
):
    count = geo[0]
    cos, sin = cos_ref[...], sin_ref[...]
    unit, _ = unit_rows(tiles(qkv_ref, 0, count).astype(F32))
    q_s[...] = turn(unit * head_ref[:, 0:1] + head_ref[:, 1:2], cos, sin).astype(BF)
    unit, _ = unit_rows(tiles(qkv_ref, 1, count).astype(F32))
    kt_s[...] = turn(unit * head_ref[:, 2:3] + head_ref[:, 3:4], cos, sin).T.astype(BF)
    v_s[...] = tiles(qkv_ref, 2, count)
    block_count, place = key_blocks(geo, ext_ref, pl.program_id(0))
    width = q_s.shape[1]
    m_s[...] = jnp.full_like(m_s, NEG_FILL)
    l_s[...] = jnp.zeros_like(l_s)
    keep_ref[0] = jnp.zeros(keep_ref.shape[1:], F32)

    def key_step(i, carry):
        first = place(i)
        keys = kt_s[pl.ds(first, KEY_BLOCK), :]
        vals = v_s[:, pl.ds(first, KEY_BLOCK)]
        for part in range(width // QUERY_CHUNK):
            cut = slice(part * QUERY_CHUNK, (part + 1) * QUERY_CHUNK)
            scores = jnp.dot(keys, q_s[:, cut], preferred_element_type=F32)
            old = m_s[:, cut]
            new = jnp.maximum(old, jnp.max(scores, axis=0, keepdims=True))
            probs = jnp.exp2((scores - new) * (SCALE * LOG2E))
            factor = jnp.exp2((old - new) * (SCALE * LOG2E))
            m_s[:, cut] = new
            l_s[:, cut] = l_s[:, cut] * factor + jnp.sum(probs, axis=0, keepdims=True)
            keep_ref[0, :, cut] = keep_ref[0, :, cut] * factor + jnp.dot(
                vals, probs.astype(BF), preferred_element_type=F32
            )
        return carry

    lax.fori_loop(0, block_count, key_step, 0)
    total_ref[0] = m_s[...] * (SCALE * LOG2E) + jnp.log2(l_s[...])
    mixed = keep_ref[0] / l_s[...]
    keep_ref[0] = mixed
    low = mixed.astype(BF)
    tile = width // count
    for s in range(count):
        out_ref[s, 0] = low[:, s * tile : (s + 1) * tile]


def attend(ext_jobs, qkv, cos, sin, head, geo):
    count, jobs, _, _, tile = qkv.shape
    width = count * tile
    work = 4 * jobs * width * width * HD
    return pl.pallas_call(
        functools.partial(attend_kernel, geo),
        grid=(jobs,),
        in_specs=[
            pl.BlockSpec(memory_space=pltpu.SMEM),
            pl.BlockSpec((count, 1, 3, HD, tile), lambda j: (0, j, 0, 0, 0)),
            pl.BlockSpec((HD, width), lambda j: (0, 0)),
            pl.BlockSpec((HD, width), lambda j: (0, 0)),
            pl.BlockSpec((HD, 4), lambda j: (0, 0)),
        ],
        out_specs=[
            pl.BlockSpec((count, 1, HD, tile), lambda j: (0, j, 0, 0)),
            pl.BlockSpec((1, HD, width), lambda j: (j, 0, 0)),
            pl.BlockSpec((1, 1, width), lambda j: (j, 0, 0)),
        ],
        out_shape=[
            jax.ShapeDtypeStruct((count, jobs, HD, tile), BF),
            jax.ShapeDtypeStruct((jobs, HD, width), F32),
            jax.ShapeDtypeStruct((jobs, 1, width), F32),
        ],
        scratch_shapes=[
            pltpu.VMEM((HD, width), BF),
            pltpu.VMEM((width, HD), BF),
            pltpu.VMEM((HD, width), BF),
            pltpu.VMEM((1, width), F32),
            pltpu.VMEM((1, width), F32),
        ],
        compiler_params=pltpu.CompilerParams(vmem_limit_bytes=48 * 2**20),
        cost_estimate=pl.CostEstimate(
            flops=3 * work, bytes_accessed=6 * 2**20, transcendentals=jobs * width * width
        ),
    )(ext_jobs, qkv, cos, sin, head)


def attend_back_kernel(
    geo, ext_ref, qkv_ref, dout_ref, keep_ref, total_ref, cos_ref, sin_ref, head_ref,
    grad_ref, head_grad_ref, q_s, k_s, kt_s, vt_s, do_s, delta_s, dq_s, dk_s, dv_s,
):
    count = geo[0]
    cos, sin = cos_ref[...], sin_ref[...]
    unit, _ = unit_rows(tiles(qkv_ref, 0, count).astype(F32))
    q_s[...] = turn(unit * head_ref[:, 0:1] + head_ref[:, 1:2], cos, sin).astype(BF)
    unit, _ = unit_rows(tiles(qkv_ref, 1, count).astype(F32))
    keys = turn(unit * head_ref[:, 2:3] + head_ref[:, 3:4], cos, sin)
    k_s[...] = keys.astype(BF)
    kt_s[...] = keys.T.astype(BF)
    vt_s[...] = tiles(qkv_ref, 2, count).astype(F32).T.astype(BF)
    dout = jnp.concatenate([dout_ref[s, 0] for s in range(count)], axis=1)
    do_s[...] = dout
    delta_s[...] = jnp.sum(dout.astype(F32) * keep_ref[0], axis=0, keepdims=True)
    block_count, place = key_blocks(geo, ext_ref, pl.program_id(0))
    width = q_s.shape[1]
    dq_s[...] = jnp.zeros_like(dq_s)
    dk_s[...] = jnp.zeros_like(dk_s)
    dv_s[...] = jnp.zeros_like(dv_s)

    def key_step(i, carry):
        first = place(i)
        keys_t = kt_s[pl.ds(first, KEY_BLOCK), :]
        vals_t = vt_s[pl.ds(first, KEY_BLOCK), :]
        keys_n = k_s[:, pl.ds(first, KEY_BLOCK)]
        dk = jnp.zeros((HD, KEY_BLOCK), F32)
        dv = jnp.zeros((HD, KEY_BLOCK), F32)
        for part in range(width // QUERY_CHUNK):
            cut = slice(part * QUERY_CHUNK, (part + 1) * QUERY_CHUNK)
            queries = q_s[:, cut]
            douts = do_s[:, cut]
            scores = jnp.dot(keys_t, queries, preferred_element_type=F32)
            probs = jnp.exp2(scores * (SCALE * LOG2E) - total_ref[0, :, cut])
            dprob = jnp.dot(vals_t, douts, preferred_element_type=F32)
            dscore = (probs * (dprob - delta_s[:, cut])).astype(BF)
            dv = dv + lax.dot_general(douts, probs.astype(BF), NT, preferred_element_type=F32)
            dk = dk + lax.dot_general(queries, dscore, NT, preferred_element_type=F32)
            dq_s[:, cut] += jnp.dot(keys_n, dscore, preferred_element_type=F32)
        dk_s[:, pl.ds(first, KEY_BLOCK)] = dk
        dv_s[:, pl.ds(first, KEY_BLOCK)] = dv
        return carry

    lax.fori_loop(0, block_count, key_step, 0)
    tile = width // count

    def lift(part, turned, at):
        unit, rstd = unit_rows(tiles(qkv_ref, part, count).astype(F32))
        dy = turn_back(turned * SCALE, cos, sin)
        head_grad_ref[0, :, at : at + 1] = jnp.sum(dy * unit, axis=1, keepdims=True)
        head_grad_ref[0, :, at + 1 : at + 2] = jnp.sum(dy, axis=1, keepdims=True)
        dunit = dy * head_ref[:, at : at + 1]
        along = jnp.mean(dunit * unit, axis=0, keepdims=True)
        dx = (dunit - jnp.mean(dunit, axis=0, keepdims=True) - unit * along) * rstd
        low = dx.astype(BF)
        for s in range(count):
            grad_ref[s, 0, part] = low[:, s * tile : (s + 1) * tile]

    lift(0, dq_s[...], 0)
    lift(1, dk_s[...], 2)
    low = dv_s[...].astype(BF)
    for s in range(count):
        grad_ref[s, 0, 2] = low[:, s * tile : (s + 1) * tile]


def attend_back(ext_jobs, qkv, dout, keep, total, cos, sin, head, geo):
    count, jobs, _, _, tile = qkv.shape
    width = count * tile
    work = 10 * jobs * width * width * HD
    return pl.pallas_call(
        functools.partial(attend_back_kernel, geo),
        grid=(jobs,),
        in_specs=[
            pl.BlockSpec(memory_space=pltpu.SMEM),
            pl.BlockSpec((count, 1, 3, HD, tile), lambda j: (0, j, 0, 0, 0)),
            pl.BlockSpec((count, 1, HD, tile), lambda j: (0, j, 0, 0)),
            pl.BlockSpec((1, HD, width), lambda j: (j, 0, 0)),
            pl.BlockSpec((1, 1, width), lambda j: (j, 0, 0)),
            pl.BlockSpec((HD, width), lambda j: (0, 0)),
            pl.BlockSpec((HD, width), lambda j: (0, 0)),
            pl.BlockSpec((HD, 4), lambda j: (0, 0)),
        ],
        out_specs=[
            pl.BlockSpec((count, 1, 3, HD, tile), lambda j: (0, j, 0, 0, 0)),
            pl.BlockSpec((1, HD, 4), lambda j: (j, 0, 0)),
        ],
        out_shape=[
            jax.ShapeDtypeStruct((count, jobs, 3, HD, tile), BF),
            jax.ShapeDtypeStruct((jobs, HD, 4), F32),
        ],
        scratch_shapes=[
            pltpu.VMEM((HD, width), BF),
            pltpu.VMEM((HD, width), BF),
            pltpu.VMEM((width, HD), BF),
            pltpu.VMEM((width, HD), BF),
            pltpu.VMEM((HD, width), BF),
            pltpu.VMEM((1, width), F32),
            pltpu.VMEM((HD, width), F32),
            pltpu.VMEM((HD, width), F32),
            pltpu.VMEM((HD, width), F32),
        ],
        compiler_params=pltpu.CompilerParams(vmem_limit_bytes=56 * 2**20),
        cost_estimate=pl.CostEstimate(
            flops=3 * work, bytes_accessed=8 * 2**20, transcendentals=jobs * width * width
        ),
    )(ext_jobs, qkv, dout, keep, total, cos, sin, head)


TN = (((0,), (0,)), ((), ()))
CROSS_HEADS = 2


def text_scores(len_ref, keys, queries, image):
    scores = lax.dot_general(keys, queries, TN, preferred_element_type=F32) * (SCALE * LOG2E)
    place = lax.broadcasted_iota(jnp.int32, scores.shape, 0)
    live = (place < len_ref[image, 0]) | (
        (place >= CLIP) & (place < CLIP + len_ref[image, 1])
    )
    return jnp.where(live, scores, NEG_FILL)


def cross_kernel(images, len_ref, rows_ref, text_ref, cos_ref, sin_ref, head_ref, out_ref, total_ref):
    tile = rows_ref.shape[2] // images
    slots = text_ref.shape[3] // images
    for h in range(CROSS_HEADS):
        unit, _ = unit_rows(rows_ref[h])
        queries = turn(unit * head_ref[:, 0:1] + head_ref[:, 1:2], cos_ref[...], sin_ref[...])
        queries = queries.astype(BF)
        for i in range(images):
            own, slot = slice(i * tile, (i + 1) * tile), slice(i * slots, (i + 1) * slots)
            scores = text_scores(len_ref, text_ref[0, h, :, slot], queries[:, own], i)
            top = jnp.max(scores, axis=0, keepdims=True)
            probs = jnp.exp2(scores - top)
            weight = jnp.sum(probs, axis=0, keepdims=True)
            low = (probs / weight).astype(BF)
            mixed = jnp.dot(text_ref[1, h, :, slot], low, preferred_element_type=F32)
            out_ref[h, :, own] = mixed.astype(BF)
            total_ref[h, :, own] = top + jnp.log2(weight)


def cross_back_kernel(
    images, len_ref, rows_ref, text_ref, dout_ref, total_ref, cos_ref, sin_ref, head_ref,
    grad_ref, text_grad_ref, head_grad_ref,
):
    tile = rows_ref.shape[2] // images
    slots = text_ref.shape[3] // images
    cos, sin = cos_ref[...], sin_ref[...]
    gain_grad = jnp.zeros((HD, 1), F32)
    shift_grad = jnp.zeros((HD, 1), F32)
    for h in range(CROSS_HEADS):
        unit, rstd = unit_rows(rows_ref[h])
        queries = turn(unit * head_ref[:, 0:1] + head_ref[:, 1:2], cos, sin).astype(BF)
        turned = []
        for i in range(images):
            own, slot = slice(i * tile, (i + 1) * tile), slice(i * slots, (i + 1) * slots)
            keys = text_ref[0, h, :, slot]
            douts = dout_ref[h, :, own]
            scores = text_scores(len_ref, keys, queries[:, own], i)
            probs = jnp.exp2(scores - total_ref[h, :, own])
            dprob = lax.dot_general(
                text_ref[1, h, :, slot], douts, TN, preferred_element_type=F32
            )
            delta = jnp.sum(probs * dprob, axis=0, keepdims=True)
            dscore = (probs * (dprob - delta)).astype(BF)
            low = probs.astype(BF)
            dkeys = lax.dot_general(queries[:, own], dscore, NT, preferred_element_type=F32)
            text_grad_ref[0, h, :, slot] = (dkeys * SCALE).astype(BF)
            text_grad_ref[1, h, :, slot] = lax.dot_general(
                douts, low, NT, preferred_element_type=F32
            ).astype(BF)
            turned.append(jnp.dot(keys, dscore, preferred_element_type=F32))
        dy = turn_back(jnp.concatenate(turned, axis=1) * SCALE, cos, sin)
        gain_grad += jnp.sum(dy * unit, axis=1, keepdims=True)
        shift_grad += jnp.sum(dy, axis=1, keepdims=True)
        dunit = dy * head_ref[:, 0:1]
        along_unit = jnp.mean(dunit * unit, axis=0, keepdims=True)
        dx = (dunit - jnp.mean(dunit, axis=0, keepdims=True) - unit * along_unit) * rstd
        grad_ref[h] = dx.astype(BF)
    head_grad_ref[0, :, 0:1] = gain_grad
    head_grad_ref[0, :, 1:2] = shift_grad


def cross_specs(width, slots):
    return dict(
        smem=pl.BlockSpec(memory_space=pltpu.SMEM),
        rows=pl.BlockSpec((CROSS_HEADS, HD, width), lambda h: (h, 0, 0)),
        text=pl.BlockSpec((2, CROSS_HEADS, HD, slots), lambda h: (0, h, 0, 0)),
        table=pl.BlockSpec((HD, width), lambda h: (0, 0)),
        head=pl.BlockSpec((HD, 2), lambda h: (0, 0)),
        total=pl.BlockSpec((CROSS_HEADS, 1, width), lambda h: (h, 0, 0)),
        head_grad=pl.BlockSpec((1, HD, 2), lambda h: (h, 0, 0)),
    )


def cross_attend(lengths, rows, text, cos, sin, head):
    heads, _, width = rows.shape
    slots = text.shape[3]
    sp = cross_specs(width, slots)
    return pl.pallas_call(
        functools.partial(cross_kernel, lengths.shape[0]),
        grid=(heads // CROSS_HEADS,),
        in_specs=[sp["smem"], sp["rows"], sp["text"], sp["table"], sp["table"], sp["head"]],
        out_specs=[sp["rows"], sp["total"]],
        out_shape=[
            jax.ShapeDtypeStruct((heads, HD, width), BF),
            jax.ShapeDtypeStruct((heads, 1, width), F32),
        ],
        compiler_params=pltpu.CompilerParams(vmem_limit_bytes=32 * 2**20),
        cost_estimate=pl.CostEstimate(
            flops=2**32, bytes_accessed=10 * 2**20, transcendentals=heads * width * slots
        ),
    )(lengths, rows, text, cos, sin, head)


def cross_attend_back(lengths, rows, text, dout, total, cos, sin, head):
    heads, _, width = rows.shape
    slots = text.shape[3]
    sp = cross_specs(width, slots)
    return pl.pallas_call(
        functools.partial(cross_back_kernel, lengths.shape[0]),
        grid=(heads // CROSS_HEADS,),
        in_specs=[
            sp["smem"], sp["rows"], sp["text"], sp["rows"], sp["total"], sp["table"], sp["table"],
            sp["head"],
        ],
        out_specs=[sp["rows"], sp["text"], sp["head_grad"]],
        out_shape=[
            jax.ShapeDtypeStruct((heads, HD, width), BF),
            jax.ShapeDtypeStruct((2, heads, HD, slots), BF),
            jax.ShapeDtypeStruct((heads // CROSS_HEADS, HD, 2), F32),
        ],
        compiler_params=pltpu.CompilerParams(vmem_limit_bytes=32 * 2**20),
        cost_estimate=pl.CostEstimate(
            flops=2**33, bytes_accessed=16 * 2**20, transcendentals=heads * width * slots
        ),
    )(lengths, rows, text, dout, total, cos, sin, head)


def all_to_all(values):
    return lax.all_to_all(values, GROUP, split_axis=0, concat_axis=0, tiled=True)


def body(
    latents, skip, temb, text, text_len, extent, embed_weight, skip_weight, shift_weight,
    qkv_weight, out_weight, cross_query, cross_keys, cross_out, up_weight, down_weight,
    final_weight, norm_gain, norm_shift, skip_gain, skip_shift, head_gain, head_shift,
    front_biases, all_biases, cross_bias, cotangent,
):
    img_count, tile_rows, tile_cols, patch_vals = latents.shape
    tokens = tile_rows * tile_cols
    near_vals = 9 * patch_vals
    row_count = lax.axis_size("row")
    col_count = lax.axis_size("col")
    count = row_count * col_count
    groups = lax.axis_size("img")
    jobs = img_count * HEADS // count
    row_index = lax.axis_index("row")
    col_index = lax.axis_index("col")
    group_index = lax.axis_index("img")
    device = row_index * col_count + col_index
    shard = D // count
    hid_shard = FF // count
    hid_part = hid_shard // groups

    small_widths = (
        norm_gain.size, norm_shift.size, skip_gain.size, skip_shift.size,
        head_gain.size, head_shift.size, front_biases.size, all_biases.size,
    )
    small = jnp.concatenate(
        [
            embed_weight.T.reshape(-1), final_weight.reshape(-1), norm_gain.reshape(-1),
            norm_shift.reshape(-1), skip_gain, skip_shift, head_gain, head_shift,
            front_biases, all_biases,
        ]
    )
    small_len = small.size
    padded_len = -(-(small_len + img_count * D) // 2048) * 2048
    time_act = jax.nn.silu(temb.astype(F32)).astype(BF)
    time_own = lax.dynamic_slice_in_dim(time_act, device * shard, shard, 1)
    shift_share = matmul(time_own, shift_weight).astype(BF).reshape(-1)
    small = jnp.pad(jnp.concatenate([small, shift_share]), (0, padded_len - small_len - shift_share.size))
    small_all = all_to_all(jnp.broadcast_to(small.reshape(1, -1, 128), (count, padded_len // 128, 128)))
    small_all = small_all.reshape(count, padded_len)
    first_rows = jnp.concatenate(
        [skip_weight] + [qkv_weight[:, i * D : (i + 1) * D] for i in range(3)]
    )
    first_all = lax.all_gather(first_rows, GROUP, axis=0, tiled=False)
    skip_full = first_all[:, : 2 * shard].reshape(2 * D, D)
    qkv_full = jnp.concatenate(
        [first_all[:, (2 + i) * shard : (3 + i) * shard].reshape(D, D) for i in range(3)], axis=1
    )
    trio = lax.all_gather(
        jnp.stack([out_weight, cross_query, cross_out]), GROUP, axis=0, tiled=False
    )
    out_full, cross_q_full, cross_o_full = [trio[:, i].reshape(D, D) for i in range(3)]
    up_part = lax.dynamic_index_in_dim(
        up_weight.reshape(shard, count, groups, hid_part), group_index, 2, keepdims=False
    ).reshape(shard, count * hid_part)
    up_full = lax.all_gather(up_part, GROUP, axis=0, tiled=True)
    down_part = lax.dynamic_index_in_dim(
        down_weight.reshape(groups, hid_part, D), group_index, 0, keepdims=False
    )
    down_full = lax.all_gather(down_part, GROUP, axis=0, tiled=True)

    wide = shard * near_vals
    embed_t = small_all[:, :wide].reshape(D, near_vals)
    final_full = small_all[:, wide : 2 * wide].reshape(D, near_vals)
    vectors = cuts(small_all[:, 2 * wide : small_len].astype(F32), small_widths)
    gain_rows = jnp.transpose(vectors[0].reshape(count, 3, shard), (1, 0, 2)).reshape(3, D)
    offset_rows = jnp.transpose(vectors[1].reshape(count, 3, shard), (1, 0, 2)).reshape(3, D)
    skip_gains, skip_offsets = vectors[2].reshape(-1), vectors[3].reshape(-1)
    head_gains, head_offsets = vectors[4].reshape(4, HD), vectors[5].reshape(4, HD)
    bias_embed, bias_skip, bias_shift, bias_qkv = cuts(vectors[6].reshape(-1), (D, D, D, 3 * D))
    bias_out, bias_cross_q, bias_cross_o, bias_up, bias_down = cuts(
        vectors[7].reshape(-1), (D, D, D, FF, D)
    )
    bias_up_part = lax.dynamic_index_in_dim(
        bias_up.reshape(count, groups, hid_part), group_index, 1, keepdims=False
    ).reshape(-1)

    local_rows = row_index * tile_rows + jnp.arange(tile_rows, dtype=jnp.int32)
    local_cols = col_index * tile_cols + jnp.arange(tile_cols, dtype=jnp.int32)
    inside = (
        (local_rows[None, :, None] < extent[:, 0, None, None])
        & (local_cols[None, None, :] < extent[:, 1, None, None])
    ).astype(F32)
    token_inside = inside.reshape(img_count, tokens, 1)
    own_angle = angles_of(
        jnp.tile(jnp.repeat(local_rows, tile_cols), img_count),
        jnp.tile(jnp.tile(local_cols, tile_rows), img_count),
    )
    own_cos, own_sin = jnp.cos(own_angle), jnp.sin(own_angle)
    every = np.arange(count * tokens)
    every_row = every // tokens // col_count * tile_rows + every % tokens // tile_cols
    every_col = every // tokens % col_count * tile_cols + every % tile_cols
    every_angle = angles_of(jnp.asarray(every_row), jnp.asarray(every_col))
    every_cos, every_sin = jnp.cos(every_angle), jnp.sin(every_angle)
    job_images = (device * jobs + jnp.arange(jobs, dtype=jnp.int32)) % img_count
    ext_jobs = jnp.take(extent, job_images, axis=0)
    geo = (count, tile_rows, tile_cols, col_count, KEY_BLOCK // tokens)

    def gelu_tanh(values):
        return jax.nn.gelu(values, approximate=True)

    text_width = cross_keys.shape[1]
    text_count = -(-text.shape[1] // 128) * 128
    text_wide = jnp.pad(text, ((0, 0), (0, text_count - text.shape[1]), (0, 0)))
    is_key = device * text_width + jnp.arange(text_width, dtype=jnp.int32) < D

    def text_norm(values, scales, offsets):
        per_head = values.reshape(text_width // HD, HD, -1)
        centre = per_head - jnp.mean(per_head, axis=1, keepdims=True)
        spread = jnp.mean(centre * centre, axis=1, keepdims=True)
        unit = centre * lax.rsqrt(spread + NORM_EPS) * scales[:, None] + offsets[:, None]
        return jnp.where(is_key[:, None], unit.reshape(values.shape), values)

    text_part = dot(cross_keys, text_wide, (0,), (2,)).reshape(text_width, -1)
    text_part = text_part + cross_bias.astype(F32)[:, None]
    text_normed, text_pull = jax.vjp(text_norm, text_part, head_gains[3], head_offsets[3])
    text_both = lax.all_gather(text_normed.astype(BF), GROUP, axis=0, tiled=True)
    text_both = text_both.reshape(2, HEADS, HD, img_count * text_count)
    shift_sums = small_all[:, small_len : small_len + img_count * D].astype(F32)
    shift_rows = jnp.sum(shift_sums, axis=0).reshape(img_count, D) + bias_shift

    lat_masked = (latents * inside[..., None]).astype(BF)
    cot_masked = (cotangent * inside[..., None]).astype(BF)
    rims = with_halo(
        jnp.concatenate([lat_masked, cot_masked], axis=-1), (("row", 1), ("col", 2)), 1
    )
    rims = rims.astype(F32)
    near = gather_near(rims[..., :patch_vals], tile_rows, tile_cols)
    near = near.reshape(img_count, tokens, near_vals).astype(BF)
    cot_near = gather_near(rims[..., patch_vals:], tile_rows, tile_cols)
    cot_near = cot_near.reshape(img_count, tokens, near_vals)
    embedded = matmul_back(near, embed_t) + bias_embed
    joined_full = jnp.concatenate(
        [embedded, skip.reshape(img_count, tokens, D).astype(F32)], axis=-1
    )
    skip_normed, skip_norm_pull = jax.vjp(layer_norm, joined_full, skip_gains, skip_offsets)
    skip_in = skip_normed.astype(BF)
    resid_in = matmul(skip_in, skip_full) + bias_skip
    self_norm, self_norm_pull = jax.vjp(layer_norm, resid_in, gain_rows[0], offset_rows[0])
    normed = (self_norm + shift_rows[:, None, :]).astype(BF)

    qkv_t = dot(qkv_full, normed, (0,), (2,)) + bias_qkv[:, None, None]
    qkv_t = qkv_t.astype(BF).reshape(3, HEADS, HD, img_count, tokens)
    qkv_jobs = all_to_all(
        jnp.transpose(qkv_t, (1, 3, 0, 2, 4)).reshape(count, jobs, 3, HD, tokens)
    )
    head_cols = jnp.stack([head_gains[0], head_offsets[0], head_gains[1], head_offsets[1]], axis=1)
    mixed_jobs, keep, total = attend(ext_jobs, qkv_jobs, every_cos, every_sin, head_cols, geo)
    mixed = all_to_all(mixed_jobs).reshape(HEADS, img_count, HD, tokens)
    attended_t = jnp.transpose(mixed, (1, 0, 2, 3)).reshape(img_count, D, tokens)
    resid_self = resid_in + dot(attended_t, out_full, (1,), (0,)) + bias_out

    cross_norm, cross_norm_pull = jax.vjp(layer_norm, resid_self, gain_rows[1], offset_rows[1])
    cross_in = cross_norm.astype(BF)
    all_tokens = img_count * tokens
    cross_rows = dot(cross_q_full, cross_in.reshape(all_tokens, D), (0,), (1,))
    cross_rows = (cross_rows + bias_cross_q[:, None]).reshape(HEADS, HD, all_tokens)
    cross_cols = jnp.stack([head_gains[2], head_offsets[2]], axis=1)
    cross_mixed, cross_total = cross_attend(
        text_len, cross_rows, text_both, own_cos, own_sin, cross_cols
    )
    cross_low = cross_mixed.reshape(D, all_tokens)
    cross_out_rows = dot(cross_low, cross_o_full, (0,), (0,)).reshape(img_count, tokens, D)
    resid_cross = resid_self + cross_out_rows + bias_cross_o

    mlp_norm, mlp_norm_pull = jax.vjp(layer_norm, resid_cross, gain_rows[2], offset_rows[2])
    mlp_in = images_gather(mlp_norm.astype(BF))
    hidden = matmul(mlp_in, up_full) + bias_up_part
    gelu_out, gelu_pull = jax.vjp(gelu_tanh, hidden)
    activated = gelu_out.astype(BF)
    resid_out = resid_cross + images_scatter(matmul(activated, down_full)) + bias_down
    resid_low = resid_out.astype(BF)
    emitted = matmul(resid_low, final_full) * token_inside
    emit_rim = with_halo(
        emitted.reshape(img_count, tile_rows, tile_cols, near_vals), (("row", 1), ("col", 2)), 1
    )
    out_latents = spread_near(emit_rim, tile_rows, tile_cols, patch_vals) * inside[..., None]

    sums = Sums()
    lead = (0, 1)
    grad_emitted = (cot_near * token_inside).astype(BF)
    grad_final = weight_grad(resid_low, grad_emitted)
    grad_resid_out = matmul_back(grad_emitted, final_full)
    grad_down_low = grad_resid_out.astype(BF)
    bias_down_grad = column_sum(grad_down_low)
    grad_down_rows = images_gather(grad_down_low)
    every_lead = (0, 1, 2)
    activated, out_latents = lax.optimization_barrier((activated, out_latents))
    sums.begin(
        "down", activated, grad_down_rows, every_lead, every_lead, 3, after=all_images
    )
    grad_hidden = gelu_pull(matmul_back(grad_down_rows, down_full))[0].astype(BF)
    sums.begin("up", mlp_in, grad_hidden, every_lead, every_lead, 3, after=all_images)
    bias_up_grad = column_sum(grad_hidden)
    grad_mlp_in = sums.step(matmul_back(grad_hidden, up_full), "down")
    grad_mlp_in = sums.step(images_scatter(grad_mlp_in), "up")
    grad_from_mlp, gain_mlp_grad, shift_mlp_grad = mlp_norm_pull(grad_mlp_in)
    grad_resid_cross = grad_resid_out + grad_from_mlp

    grad_cross_low = grad_resid_cross.astype(BF)
    grad_cross_flat = grad_cross_low.reshape(all_tokens, D)
    sums.begin("cross_o", cross_low, grad_cross_flat, (1,), (0,), 0)
    bias_cross_o_grad = column_sum(grad_cross_low)
    grad_cross_mixed = dot(cross_o_full, grad_cross_flat, (1,), (1,)).astype(BF)
    grad_cross_mixed = sums.step(grad_cross_mixed, "cross_o")
    grad_cross_rows, grad_text, cross_head_grads = cross_attend_back(
        text_len, cross_rows, text_both, grad_cross_mixed.reshape(HEADS, HD, all_tokens),
        cross_total, own_cos, own_sin, cross_cols,
    )
    cross_head_grads = jnp.sum(cross_head_grads, axis=0)
    grad_cross_rows = grad_cross_rows.reshape(D, all_tokens)
    sums.begin("text", grad_text.reshape(2 * D, img_count * text_count), after=alone)
    sums.begin("cross_q", cross_in.reshape(all_tokens, D), grad_cross_rows, (0,), (1,), 1)
    bias_cross_q_grad = jnp.sum(grad_cross_rows.astype(F32), axis=1)
    grad_cross_in = dot(grad_cross_rows, cross_q_full, (0,), (1,))
    grad_cross_in = sums.step(grad_cross_in, "text", "cross_q", "down")
    grad_from_cross, gain_cross_grad, shift_cross_grad = cross_norm_pull(
        grad_cross_in.reshape(img_count, tokens, D)
    )
    grad_resid_self = grad_resid_cross + grad_from_cross

    grad_out_rows = grad_resid_self.astype(BF)
    sums.begin("out", attended_t, grad_out_rows, (0, 2), lead, 1)
    bias_out_grad = column_sum(grad_out_rows)
    grad_attended = dot(out_full, grad_out_rows, (1,), (2,)).astype(BF)
    grad_attended = jnp.transpose(
        grad_attended.reshape(HEADS, HD, img_count, tokens), (0, 2, 1, 3)
    )
    grad_mixed_jobs = all_to_all(grad_attended.reshape(count, jobs, HD, tokens))
    grad_mixed_jobs = sums.step(grad_mixed_jobs, "out", "up", "cross_o", "down")
    grad_jobs, head_grads = attend_back(
        ext_jobs, qkv_jobs, grad_mixed_jobs, keep, total, every_cos, every_sin, head_cols, geo
    )
    grad_jobs = sums.step(grad_jobs, "text", "cross_q", "up", "cross_o")
    grad_qkv_t = sums.step(all_to_all(grad_jobs), "out", "down").reshape(HEADS, img_count, 3, HD, tokens)
    grad_qkv_t = jnp.transpose(grad_qkv_t, (2, 0, 3, 1, 4)).reshape(3 * D, img_count, tokens)
    head_grads = jnp.sum(head_grads, axis=0)

    sums.begin("qkv", normed, grad_qkv_t, (0, 1), (1, 2), 2, 0, after=all_images)
    bias_qkv_grad = jnp.sum(grad_qkv_t.astype(F32), axis=(1, 2))
    grad_normed = sums.step(
        dot(grad_qkv_t, qkv_full, (0,), (1,)), "up", "cross_o", "text", "cross_q"
    )
    grad_shift_rows = jnp.sum(grad_normed, axis=1)
    bias_shift_grad = jnp.sum(grad_shift_rows, axis=0)
    grad_from_self, gain_self_grad, shift_self_grad = self_norm_pull(grad_normed)
    grad_resid_in = grad_resid_self + grad_from_self
    grad_merged = sums.step(grad_resid_in.astype(BF), "qkv", "out", "text")
    skip_cut = D // 256 * 128
    sums.begin("skip_a", skip_in, grad_merged[..., :-skip_cut], lead, lead, 2)
    sums.begin("skip_b", skip_in, grad_merged[..., -skip_cut:], lead, lead, 2, order=col_first())
    bias_skip_grad = column_sum(grad_merged)
    grad_skip_normed = sums.step(matmul_back(grad_merged, skip_full), "skip_a", "skip_b", "cross_q", "cross_o")
    grad_joined, skip_gain_grad, skip_shift_grad = skip_norm_pull(grad_skip_normed)
    grad_skip = grad_joined[..., D:].reshape(img_count, tile_rows, tile_cols, D)
    grad_embedded = sums.step(grad_joined[..., :D].astype(BF), "up", "out", "cross_q", "qkv")
    grad_embed_t = weight_grad(grad_embedded, near)
    bias_embed_grad = column_sum(grad_embedded)
    grad_near = matmul(grad_embedded, embed_t).reshape(
        img_count, tile_rows, tile_cols, near_vals
    )
    near_rim = with_halo(grad_near, (("row", 1), ("col", 2)), 1)
    grad_latents = spread_near(near_rim, tile_rows, tile_cols, patch_vals) * inside[..., None]

    shards = sums.finish()
    grad_text_lin, head_gain_ck_grad, head_shift_ck_grad = text_pull(shards["text"])
    grad_text_low = grad_text_lin.astype(BF)
    grad_cross_keys = images_sum(
        dot(
            text_wide, grad_text_low.reshape(text_width, img_count, text_count), (0, 1), (1, 2)
        ),
        BF,
    )
    grad_cross_bias = images_sum(jnp.sum(grad_text_low.astype(F32), axis=1), F32)

    def by_device(vector):
        return vector.reshape(count, -1)

    def rows_by_device(rows):
        return jnp.transpose(rows.reshape(3, count, shard), (1, 0, 2)).reshape(count, -1)

    bias_up_all = jnp.where(
        (jnp.arange(groups) == group_index)[None, :, None],
        bias_up_grad.reshape(count, 1, hid_part),
        0.0,
    ).reshape(-1)
    small_grads = jnp.concatenate(
        [
            by_device(grad_embed_t),
            by_device(grad_final),
            rows_by_device(jnp.stack([gain_self_grad, gain_cross_grad, gain_mlp_grad])),
            rows_by_device(jnp.stack([shift_self_grad, shift_cross_grad, shift_mlp_grad])),
            by_device(skip_gain_grad),
            by_device(skip_shift_grad),
            by_device(
                jnp.concatenate(
                    [head_grads[:, 0], head_grads[:, 2], cross_head_grads[:, 0], head_gain_ck_grad]
                )
            ),
            by_device(
                jnp.concatenate(
                    [head_grads[:, 1], head_grads[:, 3], cross_head_grads[:, 1], head_shift_ck_grad]
                )
            ),
            by_device(
                jnp.concatenate([bias_embed_grad, bias_skip_grad, bias_shift_grad, bias_qkv_grad])
            ),
            by_device(
                jnp.concatenate(
                    [
                        bias_out_grad, bias_cross_q_grad, bias_cross_o_grad, bias_up_all,
                        bias_down_grad,
                    ]
                )
            ),
        ],
        axis=1,
    )
    shift_share = jnp.broadcast_to(grad_shift_rows.reshape(1, -1), (count, img_count * D))
    small_grads = jnp.concatenate([small_grads, shift_share], axis=1).astype(BF)
    small_grads = jnp.pad(small_grads, ((0, 0), (0, padded_len - small_grads.shape[1])))
    small_got = all_to_all(small_grads.reshape(count, -1, 128)).astype(F32)
    small_got = jnp.sum(small_got, axis=0).reshape(-1)
    small_sum = images_sum(small_got[:small_len], F32)
    total_parts = cuts(small_sum, (wide, wide) + small_widths)
    grad_shift = lax.dot_general(
        time_own.astype(F32),
        small_got[small_len : small_len + img_count * D].reshape(img_count, D),
        (((0,), (0,)), ((), ())),
        precision=lax.Precision.HIGHEST,
    )

    total_up = jnp.transpose(
        shards["up"].reshape(groups, shard, count, hid_part), (1, 2, 0, 3)
    ).reshape(shard, FF)
    total_down = shards["down"].reshape(hid_shard, D)
    return (
        out_latents,
        grad_latents,
        grad_skip,
        total_parts[0].reshape(shard, near_vals).T,
        jnp.concatenate([shards["skip_a"], shards["skip_b"]], axis=1),
        images_sum(grad_shift, F32),
        jnp.concatenate([shards["qkv"][i] for i in range(groups)], axis=1).astype(F32),
        shards["out"],
        shards["cross_q"],
        grad_cross_keys,
        shards["cross_o"],
        total_up.astype(F32),
        total_down.astype(F32),
        total_parts[1].reshape(shard, near_vals),
        total_parts[2].reshape(3, shard),
        total_parts[3].reshape(3, shard),
        total_parts[4],
        total_parts[5],
        total_parts[6],
        total_parts[7],
        total_parts[8],
        total_parts[9],
        grad_cross_bias,
    )


def solution(mesh):
    tile = P("img", "row", "col", None)
    rows = P(GROUP, None)
    columns = P(None, GROUP)
    vector = P(GROUP)
    return jax.shard_map(
        body,
        mesh=mesh,
        in_specs=(
            tile, tile, P("img", None), P("img", None, None), P("img", None), P("img", None),
            columns, rows, rows, rows, rows, rows, columns, rows, rows, rows, rows,
            columns, columns, vector, vector, vector, vector, vector, vector, vector, tile,
        ),
        out_specs=(
            tile, tile, tile, columns, rows, rows, rows, rows, rows, columns, rows, rows, rows,
            rows, columns, columns, vector, vector, vector, vector, vector, vector, vector,
        ),
        check_vma=False,
    )
```

```python
import functools
import math

import jax
import jax.numpy as jnp
import numpy as np
from jax import lax
from jax.experimental import pallas as pl
from jax.experimental.pallas import tpu as pltpu
from jax.sharding import PartitionSpec as P

D = 1408
HEADS = 16
HD = 88
FF = 6144
CLIP = 77
NORM_EPS = 1e-06
NEG_FILL = -1e30
STEPS = ((-1, -1), (-1, 0), (-1, 1), (0, -1), (0, 0), (0, 1), (1, -1), (1, 0), (1, 1))
GROUP = ("row", "col")
F32 = jnp.float32
BF = jnp.bfloat16
SCALE = 1.0 / math.sqrt(HD)
LOG2E = math.log2(math.e)
NT = (((1,), (1,)), ((), ()))
KEY_BLOCK = 256
QUERY_CHUNK = 1024


def with_halo(block, sides, width):
    for axis, dim in sides:
        count = lax.axis_size(axis)
        forward = [(i, i + 1) for i in range(count - 1)]
        backward = [(target, source) for source, target in forward]
        low = lax.ppermute(
            lax.slice_in_dim(block, block.shape[dim] - width, None, axis=dim), axis, forward
        )
        high = lax.ppermute(lax.slice_in_dim(block, 0, width, axis=dim), axis, backward)
        block = jnp.concatenate([low, block, high], axis=dim)
    return block


def dot(former, latter, former_dims, latter_dims):
    return lax.dot_general(
        former, latter, ((former_dims, latter_dims), ((), ())), preferred_element_type=F32
    )


def matmul(former, latter):
    return dot(former, latter, (former.ndim - 1,), (0,))


def matmul_back(former, latter):
    return dot(former, latter, (former.ndim - 1,), (1,))


def weight_grad(inputs, grads):
    lead = tuple(range(inputs.ndim - 1))
    return dot(inputs, grads, lead, lead)


def column_sum(grads):
    return jnp.sum(grads.astype(F32), axis=tuple(range(grads.ndim - 1)))


def layer_norm(values, scales, offsets):
    centre = values - jnp.mean(values, axis=-1, keepdims=True)
    spread = jnp.mean(centre * centre, axis=-1, keepdims=True)
    return centre * lax.rsqrt(spread + NORM_EPS) * scales + offsets


def angles_of(row_place, col_place):
    pair_index = np.arange(HD) // 2
    quarter = HD // 4
    within = np.where(pair_index < quarter, pair_index, pair_index - quarter).astype(np.float32)
    frequency = np.exp(np.float32(-math.log(10000.0)) * within / np.float32(quarter))
    by_row = jnp.asarray(pair_index < quarter)
    places = jnp.where(by_row[:, None], row_place[None, :], col_place[None, :])
    return places.astype(F32) * jnp.asarray(frequency.astype(np.float32))[:, None]


def gather_near(padded, tall, broad):
    return jnp.concatenate(
        [
            padded[..., 1 + step_row : 1 + step_row + tall, 1 + step_col : 1 + step_col + broad, :]
            for step_row, step_col in STEPS
        ],
        axis=-1,
    )


def spread_near(padded, tall, broad, channels):
    result = None
    for number, (step_row, step_col) in enumerate(STEPS):
        portion = padded[
            ...,
            1 - step_row : 1 - step_row + tall,
            1 - step_col : 1 - step_col + broad,
            number * channels : (number + 1) * channels,
        ]
        result = portion if result is None else result + portion
    return result


def cuts(vector, widths):
    ends = np.cumsum((0,) + widths)
    return [vector[..., ends[i] : ends[i + 1]] for i in range(len(widths))]


def swap_images(values, bit):
    count = lax.axis_size("img")
    return lax.ppermute(values, "img", [(i, i ^ bit) for i in range(count)])


def images_gather(values):
    blocks = values[None]
    while blocks.shape[0] < lax.axis_size("img"):
        blocks = jnp.concatenate([blocks, swap_images(blocks, blocks.shape[0])])
    return blocks


def images_scatter(parts):
    while parts.shape[0] > 1:
        half = parts.shape[0] // 2
        parts = parts[:half] + swap_images(parts[half:].astype(BF), half).astype(F32)
    return parts[0]


def images_sum(values, sent):
    bit = 1
    while bit < lax.axis_size("img"):
        values = values.astype(sent)
        values = values.astype(F32) + swap_images(values, bit).astype(F32)
        bit *= 2
    return values.astype(F32)


def exchange(values, axis, bit):
    if bit is None:
        return lax.psum_scatter(values, axis, scatter_dimension=0, tiled=True)
    size = lax.axis_size(axis)
    return lax.ppermute(values, axis, [(i, i ^ bit) for i in range(size)])


def halves(values, dim, bit):
    keep = lax.dynamic_index_in_dim(values, bit, dim, keepdims=False)
    return keep, lax.dynamic_index_in_dim(values, 1 - bit, dim, keepdims=False)


def core_features(values, dim, core):
    rows = lax.axis_size("row")
    block = values.shape[dim] // rows
    return jnp.concatenate(
        [
            lax.dynamic_slice_in_dim(values, (2 * i + core) * block, block, dim)
            for i in range(rows // 2)
        ],
        axis=dim,
    )


def row_first():
    rows, cols = lax.axis_size("row"), lax.axis_size("col")
    row_bits = [("row", 1 << i) for i in range(1, rows.bit_length() - 1)]
    return row_bits + [("col", 1 << i) for i in range(cols.bit_length() - 1)]


def shard_sum(order, after, inputs, grads, input_lead, grad_lead, feature):
    core = lax.axis_index("row") % 2
    give = dot(core_features(inputs, feature, 1 - core), grads, input_lead, grad_lead)
    (got,) = yield [give.astype(BF)], "row", 1
    keep = dot(core_features(inputs, feature, core), grads, input_lead, grad_lead)
    part = yield from scatter_sum(order, keep + got.astype(F32))
    part = yield from after(part)
    return part


def offload_sum(after, part):
    (got,) = yield [part.astype(BF)], GROUP, None
    part = yield from after(got.astype(F32))
    return part


def scatter_sum(order, part):
    dims = [d for d in reversed(row_first()) if d[0] == "row"]
    dims += [d for d in reversed(row_first()) if d[0] == "col"]
    width = part.shape[-1]
    part = part.reshape((2,) * len(dims) + (-1, width))
    for axis, bit in order:
        at = dims.index((axis, bit))
        keep, give = halves(part, at, lax.axis_index(axis) // bit % 2)
        del dims[at]
        (got,) = yield [give.astype(BF)], axis, bit
        part = keep + got.astype(F32)
    return part.reshape(-1, width)


def alone(part):
    return part
    yield


def all_images(part):
    bit, blocks = 1, part.astype(BF)[None]
    while bit < lax.axis_size("img"):
        (got,) = yield [blocks], "img", bit
        blocks = placed(blocks, got, lax.axis_index("img") // bit % 2, 0)
        blocks = blocks.reshape((-1,) + part.shape)
        bit *= 2
    return blocks


def placed(mine, other, bit, dim):
    first = lax.select(jnp.broadcast_to(bit == 0, mine.shape), mine, other)
    last = lax.select(jnp.broadcast_to(bit == 0, mine.shape), other, mine)
    return jnp.stack([first, last], axis=dim)


class Moves:
    def __init__(self):
        self.running = {}
        self.done = {}

    def begin(self, value, **makers):
        return self.launch(value, {name: (maker, next(maker)) for name, maker in makers.items()})

    def launch(self, value, wanted):
        if not wanted:
            return value
        gives = {name: request[0] for name, (_, request) in wanted.items()}
        value, gives = lax.optimization_barrier((value, gives))
        for name, (maker, (_, axis, bit)) in wanted.items():
            self.running[name] = (maker, [exchange(give, axis, bit) for give in gives[name]])
        return value

    def step(self, value, *names):
        names = [name for name in names if name in self.running]
        if not names:
            return value
        value, gots = lax.optimization_barrier(
            (value, {name: self.running[name][1] for name in names})
        )
        wanted = {}
        for name in names:
            maker = self.running.pop(name)[0]
            try:
                wanted[name] = (maker, maker.send(gots[name]))
            except StopIteration as stop:
                self.done[name] = stop.value
        return self.launch(value, wanted)

    def finish(self, *names):
        waiting = [name for name in names if name in self.running]
        while waiting:
            for name in waiting:
                maker, gots = self.running.pop(name)
                try:
                    gives, axis, bit = maker.send(gots)
                    self.running[name] = (maker, [exchange(give, axis, bit) for give in gives])
                except StopIteration as stop:
                    self.done[name] = stop.value
            waiting = [name for name in names if name in self.running]


def unit_rows(values):
    centre = values - jnp.mean(values, axis=0, keepdims=True)
    rstd = lax.rsqrt(jnp.mean(centre * centre, axis=0, keepdims=True) + NORM_EPS)
    return centre * rstd, rstd


def swap_pairs(values, back):
    rows = values.shape[0]
    even = lax.broadcasted_iota(jnp.int32, values.shape, 0) % 2 == 0
    up = pltpu.roll(values, rows - 1, 0)
    down = pltpu.roll(values, 1, 0)
    return jnp.where(even, up, -down) if back else jnp.where(even, -up, down)


def turn(values, cos, sin):
    return values * cos + swap_pairs(values, False) * sin


def turn_back(values, cos, sin):
    return values * cos + swap_pairs(values, True) * sin


def tiles(ref, part, count):
    return jnp.concatenate([ref[s, 0, part] for s in range(count)], axis=1)


def key_blocks(geo, ext_ref, job):
    count, tile_rows, tile_cols, col_tiles, block_tiles = geo
    rows = ext_ref[job, 0] // tile_rows
    groups = ext_ref[job, 1] // (block_tiles * tile_cols)

    def place(i):
        block = i // groups * (col_tiles // block_tiles) + i % groups
        return pl.multiple_of(block * KEY_BLOCK, KEY_BLOCK)

    return rows * groups, place


def attend_kernel(
    geo, ext_ref, qkv_ref, cos_ref, sin_ref, head_ref, out_ref, keep_ref, total_ref,
    q_s, kt_s, v_s, m_s, l_s,
):
    count = geo[0]
    cos, sin = cos_ref[...], sin_ref[...]
    unit, _ = unit_rows(tiles(qkv_ref, 0, count).astype(F32))
    q_s[...] = turn(unit * head_ref[:, 0:1] + head_ref[:, 1:2], cos, sin).astype(BF)
    unit, _ = unit_rows(tiles(qkv_ref, 1, count).astype(F32))
    kt_s[...] = turn(unit * head_ref[:, 2:3] + head_ref[:, 3:4], cos, sin).T.astype(BF)
    v_s[...] = tiles(qkv_ref, 2, count)
    block_count, place = key_blocks(geo, ext_ref, pl.program_id(0))
    width = q_s.shape[1]
    m_s[...] = jnp.full_like(m_s, NEG_FILL)
    l_s[...] = jnp.zeros_like(l_s)
    keep_ref[0] = jnp.zeros(keep_ref.shape[1:], F32)

    def key_step(i, carry):
        first = place(i)
        keys = kt_s[pl.ds(first, KEY_BLOCK), :]
        vals = v_s[:, pl.ds(first, KEY_BLOCK)]
        for part in range(width // QUERY_CHUNK):
            cut = slice(part * QUERY_CHUNK, (part + 1) * QUERY_CHUNK)
            scores = jnp.dot(keys, q_s[:, cut], preferred_element_type=F32)
            old = m_s[:, cut]
            new = jnp.maximum(old, jnp.max(scores, axis=0, keepdims=True))
            probs = jnp.exp2((scores - new) * (SCALE * LOG2E))
            factor = jnp.exp2((old - new) * (SCALE * LOG2E))
            m_s[:, cut] = new
            l_s[:, cut] = l_s[:, cut] * factor + jnp.sum(probs, axis=0, keepdims=True)
            keep_ref[0, :, cut] = keep_ref[0, :, cut] * factor + jnp.dot(
                vals, probs.astype(BF), preferred_element_type=F32
            )
        return carry

    lax.fori_loop(0, block_count, key_step, 0)
    total_ref[0] = m_s[...] * (SCALE * LOG2E) + jnp.log2(l_s[...])
    mixed = keep_ref[0] / l_s[...]
    keep_ref[0] = mixed
    low = mixed.astype(BF)
    tile = width // count
    for s in range(count):
        out_ref[s, 0] = low[:, s * tile : (s + 1) * tile]


def attend(ext_jobs, qkv, cos, sin, head, geo):
    count, jobs, _, _, tile = qkv.shape
    width = count * tile
    work = 4 * jobs * width * width * HD
    return pl.pallas_call(
        functools.partial(attend_kernel, geo),
        grid=(jobs,),
        in_specs=[
            pl.BlockSpec(memory_space=pltpu.SMEM),
            pl.BlockSpec((count, 1, 3, HD, tile), lambda j: (0, j, 0, 0, 0)),
            pl.BlockSpec((HD, width), lambda j: (0, 0)),
            pl.BlockSpec((HD, width), lambda j: (0, 0)),
            pl.BlockSpec((HD, 4), lambda j: (0, 0)),
        ],
        out_specs=[
            pl.BlockSpec((count, 1, HD, tile), lambda j: (0, j, 0, 0)),
            pl.BlockSpec((1, HD, width), lambda j: (j, 0, 0)),
            pl.BlockSpec((1, 1, width), lambda j: (j, 0, 0)),
        ],
        out_shape=[
            jax.ShapeDtypeStruct((count, jobs, HD, tile), BF),
            jax.ShapeDtypeStruct((jobs, HD, width), F32),
            jax.ShapeDtypeStruct((jobs, 1, width), F32),
        ],
        scratch_shapes=[
            pltpu.VMEM((HD, width), BF),
            pltpu.VMEM((width, HD), BF),
            pltpu.VMEM((HD, width), BF),
            pltpu.VMEM((1, width), F32),
            pltpu.VMEM((1, width), F32),
        ],
        compiler_params=pltpu.CompilerParams(vmem_limit_bytes=48 * 2**20),
        cost_estimate=pl.CostEstimate(
            flops=3 * work, bytes_accessed=6 * 2**20, transcendentals=jobs * width * width
        ),
    )(ext_jobs, qkv, cos, sin, head)


def attend_back_kernel(
    geo, ext_ref, qkv_ref, dout_ref, keep_ref, total_ref, cos_ref, sin_ref, head_ref,
    grad_ref, head_grad_ref, q_s, k_s, kt_s, vt_s, do_s, delta_s, dq_s, dk_s, dv_s,
):
    count = geo[0]
    cos, sin = cos_ref[...], sin_ref[...]
    unit, _ = unit_rows(tiles(qkv_ref, 0, count).astype(F32))
    q_s[...] = turn(unit * head_ref[:, 0:1] + head_ref[:, 1:2], cos, sin).astype(BF)
    unit, _ = unit_rows(tiles(qkv_ref, 1, count).astype(F32))
    keys = turn(unit * head_ref[:, 2:3] + head_ref[:, 3:4], cos, sin)
    k_s[...] = keys.astype(BF)
    kt_s[...] = keys.T.astype(BF)
    vt_s[...] = tiles(qkv_ref, 2, count).astype(F32).T.astype(BF)
    dout = jnp.concatenate([dout_ref[s, 0] for s in range(count)], axis=1)
    do_s[...] = dout
    delta_s[...] = jnp.sum(dout.astype(F32) * keep_ref[0], axis=0, keepdims=True)
    block_count, place = key_blocks(geo, ext_ref, pl.program_id(0))
    width = q_s.shape[1]
    dq_s[...] = jnp.zeros_like(dq_s)
    dk_s[...] = jnp.zeros_like(dk_s)
    dv_s[...] = jnp.zeros_like(dv_s)

    def key_step(i, carry):
        first = place(i)
        keys_t = kt_s[pl.ds(first, KEY_BLOCK), :]
        vals_t = vt_s[pl.ds(first, KEY_BLOCK), :]
        keys_n = k_s[:, pl.ds(first, KEY_BLOCK)]
        dk = jnp.zeros((HD, KEY_BLOCK), F32)
        dv = jnp.zeros((HD, KEY_BLOCK), F32)
        for part in range(width // QUERY_CHUNK):
            cut = slice(part * QUERY_CHUNK, (part + 1) * QUERY_CHUNK)
            queries = q_s[:, cut]
            douts = do_s[:, cut]
            scores = jnp.dot(keys_t, queries, preferred_element_type=F32)
            probs = jnp.exp2(scores * (SCALE * LOG2E) - total_ref[0, :, cut])
            dprob = jnp.dot(vals_t, douts, preferred_element_type=F32)
            dscore = (probs * (dprob - delta_s[:, cut])).astype(BF)
            dv = dv + lax.dot_general(douts, probs.astype(BF), NT, preferred_element_type=F32)
            dk = dk + lax.dot_general(queries, dscore, NT, preferred_element_type=F32)
            dq_s[:, cut] += jnp.dot(keys_n, dscore, preferred_element_type=F32)
        dk_s[:, pl.ds(first, KEY_BLOCK)] = dk
        dv_s[:, pl.ds(first, KEY_BLOCK)] = dv
        return carry

    lax.fori_loop(0, block_count, key_step, 0)
    tile = width // count

    def lift(part, turned, at):
        unit, rstd = unit_rows(tiles(qkv_ref, part, count).astype(F32))
        dy = turn_back(turned * SCALE, cos, sin)
        head_grad_ref[0, :, at : at + 1] = jnp.sum(dy * unit, axis=1, keepdims=True)
        head_grad_ref[0, :, at + 1 : at + 2] = jnp.sum(dy, axis=1, keepdims=True)
        dunit = dy * head_ref[:, at : at + 1]
        along = jnp.mean(dunit * unit, axis=0, keepdims=True)
        dx = (dunit - jnp.mean(dunit, axis=0, keepdims=True) - unit * along) * rstd
        low = dx.astype(BF)
        for s in range(count):
            grad_ref[s, 0, part] = low[:, s * tile : (s + 1) * tile]

    lift(0, dq_s[...], 0)
    lift(1, dk_s[...], 2)
    low = dv_s[...].astype(BF)
    for s in range(count):
        grad_ref[s, 0, 2] = low[:, s * tile : (s + 1) * tile]


def attend_back(ext_jobs, qkv, dout, keep, total, cos, sin, head, geo):
    count, jobs, _, _, tile = qkv.shape
    width = count * tile
    work = 10 * jobs * width * width * HD
    return pl.pallas_call(
        functools.partial(attend_back_kernel, geo),
        grid=(jobs,),
        in_specs=[
            pl.BlockSpec(memory_space=pltpu.SMEM),
            pl.BlockSpec((count, 1, 3, HD, tile), lambda j: (0, j, 0, 0, 0)),
            pl.BlockSpec((count, 1, HD, tile), lambda j: (0, j, 0, 0)),
            pl.BlockSpec((1, HD, width), lambda j: (j, 0, 0)),
            pl.BlockSpec((1, 1, width), lambda j: (j, 0, 0)),
            pl.BlockSpec((HD, width), lambda j: (0, 0)),
            pl.BlockSpec((HD, width), lambda j: (0, 0)),
            pl.BlockSpec((HD, 4), lambda j: (0, 0)),
        ],
        out_specs=[
            pl.BlockSpec((count, 1, 3, HD, tile), lambda j: (0, j, 0, 0, 0)),
            pl.BlockSpec((1, HD, 4), lambda j: (j, 0, 0)),
        ],
        out_shape=[
            jax.ShapeDtypeStruct((count, jobs, 3, HD, tile), BF),
            jax.ShapeDtypeStruct((jobs, HD, 4), F32),
        ],
        scratch_shapes=[
            pltpu.VMEM((HD, width), BF),
            pltpu.VMEM((HD, width), BF),
            pltpu.VMEM((width, HD), BF),
            pltpu.VMEM((width, HD), BF),
            pltpu.VMEM((HD, width), BF),
            pltpu.VMEM((1, width), F32),
            pltpu.VMEM((HD, width), F32),
            pltpu.VMEM((HD, width), F32),
            pltpu.VMEM((HD, width), F32),
        ],
        compiler_params=pltpu.CompilerParams(vmem_limit_bytes=56 * 2**20),
        cost_estimate=pl.CostEstimate(
            flops=3 * work, bytes_accessed=8 * 2**20, transcendentals=jobs * width * width
        ),
    )(ext_jobs, qkv, dout, keep, total, cos, sin, head)


TN = (((0,), (0,)), ((), ()))
CROSS_HEADS = 2


def text_scores(len_ref, keys, queries, image):
    scores = lax.dot_general(keys, queries, TN, preferred_element_type=F32) * (SCALE * LOG2E)
    place = lax.broadcasted_iota(jnp.int32, scores.shape, 0)
    live = (place < len_ref[image, 0]) | (
        (place >= CLIP) & (place < CLIP + len_ref[image, 1])
    )
    return jnp.where(live, scores, NEG_FILL)


def cross_kernel(images, len_ref, rows_ref, text_ref, cos_ref, sin_ref, head_ref, out_ref, total_ref):
    tile = rows_ref.shape[2] // images
    slots = text_ref.shape[3] // images
    for h in range(CROSS_HEADS):
        unit, _ = unit_rows(rows_ref[h])
        queries = turn(unit * head_ref[:, 0:1] + head_ref[:, 1:2], cos_ref[...], sin_ref[...])
        queries = queries.astype(BF)
        for i in range(images):
            own, slot = slice(i * tile, (i + 1) * tile), slice(i * slots, (i + 1) * slots)
            scores = text_scores(len_ref, text_ref[0, h, :, slot], queries[:, own], i)
            top = jnp.max(scores, axis=0, keepdims=True)
            probs = jnp.exp2(scores - top)
            weight = jnp.sum(probs, axis=0, keepdims=True)
            low = (probs / weight).astype(BF)
            mixed = jnp.dot(text_ref[1, h, :, slot], low, preferred_element_type=F32)
            out_ref[h, :, own] = mixed.astype(BF)
            total_ref[h, :, own] = top + jnp.log2(weight)


def cross_back_kernel(
    images, len_ref, rows_ref, text_ref, dout_ref, total_ref, cos_ref, sin_ref, head_ref,
    grad_ref, text_grad_ref, head_grad_ref,
):
    tile = rows_ref.shape[2] // images
    slots = text_ref.shape[3] // images
    cos, sin = cos_ref[...], sin_ref[...]
    gain_grad = jnp.zeros((HD, 1), F32)
    shift_grad = jnp.zeros((HD, 1), F32)
    for h in range(CROSS_HEADS):
        unit, rstd = unit_rows(rows_ref[h])
        queries = turn(unit * head_ref[:, 0:1] + head_ref[:, 1:2], cos, sin).astype(BF)
        turned = []
        for i in range(images):
            own, slot = slice(i * tile, (i + 1) * tile), slice(i * slots, (i + 1) * slots)
            keys = text_ref[0, h, :, slot]
            douts = dout_ref[h, :, own]
            scores = text_scores(len_ref, keys, queries[:, own], i)
            probs = jnp.exp2(scores - total_ref[h, :, own])
            dprob = lax.dot_general(
                text_ref[1, h, :, slot], douts, TN, preferred_element_type=F32
            )
            delta = jnp.sum(probs * dprob, axis=0, keepdims=True)
            dscore = (probs * (dprob - delta)).astype(BF)
            low = probs.astype(BF)
            dkeys = lax.dot_general(queries[:, own], dscore, NT, preferred_element_type=F32)
            text_grad_ref[0, h, :, slot] = (dkeys * SCALE).astype(BF)
            text_grad_ref[1, h, :, slot] = lax.dot_general(
                douts, low, NT, preferred_element_type=F32
            ).astype(BF)
            turned.append(jnp.dot(keys, dscore, preferred_element_type=F32))
        dy = turn_back(jnp.concatenate(turned, axis=1) * SCALE, cos, sin)
        gain_grad += jnp.sum(dy * unit, axis=1, keepdims=True)
        shift_grad += jnp.sum(dy, axis=1, keepdims=True)
        dunit = dy * head_ref[:, 0:1]
        along_unit = jnp.mean(dunit * unit, axis=0, keepdims=True)
        dx = (dunit - jnp.mean(dunit, axis=0, keepdims=True) - unit * along_unit) * rstd
        grad_ref[h] = dx.astype(BF)
    head_grad_ref[0, :, 0:1] = gain_grad
    head_grad_ref[0, :, 1:2] = shift_grad


def cross_specs(width, slots):
    return dict(
        smem=pl.BlockSpec(memory_space=pltpu.SMEM),
        rows=pl.BlockSpec((CROSS_HEADS, HD, width), lambda h: (h, 0, 0)),
        text=pl.BlockSpec((2, CROSS_HEADS, HD, slots), lambda h: (0, h, 0, 0)),
        table=pl.BlockSpec((HD, width), lambda h: (0, 0)),
        head=pl.BlockSpec((HD, 2), lambda h: (0, 0)),
        total=pl.BlockSpec((CROSS_HEADS, 1, width), lambda h: (h, 0, 0)),
        head_grad=pl.BlockSpec((1, HD, 2), lambda h: (h, 0, 0)),
    )


def cross_attend(lengths, rows, text, cos, sin, head):
    heads, _, width = rows.shape
    slots = text.shape[3]
    sp = cross_specs(width, slots)
    return pl.pallas_call(
        functools.partial(cross_kernel, lengths.shape[0]),
        grid=(heads // CROSS_HEADS,),
        in_specs=[sp["smem"], sp["rows"], sp["text"], sp["table"], sp["table"], sp["head"]],
        out_specs=[sp["rows"], sp["total"]],
        out_shape=[
            jax.ShapeDtypeStruct((heads, HD, width), BF),
            jax.ShapeDtypeStruct((heads, 1, width), F32),
        ],
        compiler_params=pltpu.CompilerParams(vmem_limit_bytes=32 * 2**20),
        cost_estimate=pl.CostEstimate(
            flops=2**32, bytes_accessed=10 * 2**20, transcendentals=heads * width * slots
        ),
    )(lengths, rows, text, cos, sin, head)


def cross_attend_back(lengths, rows, text, dout, total, cos, sin, head):
    heads, _, width = rows.shape
    slots = text.shape[3]
    sp = cross_specs(width, slots)
    return pl.pallas_call(
        functools.partial(cross_back_kernel, lengths.shape[0]),
        grid=(heads // CROSS_HEADS,),
        in_specs=[
            sp["smem"], sp["rows"], sp["text"], sp["rows"], sp["total"], sp["table"], sp["table"],
            sp["head"],
        ],
        out_specs=[sp["rows"], sp["text"], sp["head_grad"]],
        out_shape=[
            jax.ShapeDtypeStruct((heads, HD, width), BF),
            jax.ShapeDtypeStruct((2, heads, HD, slots), BF),
            jax.ShapeDtypeStruct((heads // CROSS_HEADS, HD, 2), F32),
        ],
        compiler_params=pltpu.CompilerParams(vmem_limit_bytes=32 * 2**20),
        cost_estimate=pl.CostEstimate(
            flops=2**33, bytes_accessed=16 * 2**20, transcendentals=heads * width * slots
        ),
    )(lengths, rows, text, dout, total, cos, sin, head)


MESH = pl.DeviceIdType.MESH


def sum_plan(sizes, rows_first):
    groups, row_count, cols = sizes
    count, height = row_count * cols // 2, 16 * groups
    image_bits = [("img", 1 << i) for i in range(groups.bit_length() - 1)]
    row_bits = [("row", 1 << i) for i in range(1, row_count.bit_length() - 1)]
    col_bits = [("col", 1 << i) for i in range(cols.bit_length() - 1)]
    plan = []
    for axis, bit in (row_bits + image_bits if rows_first else image_bits + row_bits) + col_bits:
        if axis == "img":
            height //= 2
        else:
            count //= 2
        plan.append((axis, bit, count, height))
    return plan


def sum_kernel(sizes, steps, grads_ref, out_ref, *scratch):
    groups, row_count, cols = sizes
    height = 16 * groups
    first_count = row_count * cols // 2
    places = {axis: lax.axis_index(axis) for axis in ("img", "row", "col")}
    plans = [sum_plan(sizes, False), sum_plan(sizes, True)]
    stages = len(plans[0])
    image_stages = groups.bit_length() - 1
    held = [scratch[: stages + 1], scratch[stages + 1 : 2 * stages + 2]]
    own, send_sem, recv_sem, spread_sem, spread_recv, own_sem, out_sem = scratch[2 * stages + 2 :]
    core = places["row"] % 2

    def partner(axis, bit):
        place = dict(places)
        part = place[axis] // bit % 2
        place[axis] = place[axis] + bit - 2 * bit * part
        return tuple(place[name] for name in ("img", "row", "col"))

    def bit_of(axis, bit):
        return places[axis] // bit % 2

    def chunk_rows(kind, chunk):
        return pl.multiple_of((2 * chunk + kind) * height, 16)

    def first_copies(kind, chunk):
        rows = pl.ds(chunk_rows(kind, chunk), height)
        for i in range(row_count // 2):
            shards = pl.ds((2 * i + 1 - core) * cols, cols)
            yield pltpu.make_async_remote_copy(
                src_ref=grads_ref.at[shards, rows],
                dst_ref=held[kind][0].at[chunk, pl.ds(i * cols, cols)],
                send_sem=send_sem.at[kind, 0, chunk],
                recv_sem=recv_sem.at[kind, 0, chunk],
                device_id=partner("row", 1),
                device_id_type=MESH,
            )

    def own_copies(kind, chunk):
        rows = pl.ds(chunk_rows(kind, chunk), height)
        for i in range(row_count // 2):
            shards = pl.ds((2 * i + core) * cols, cols)
            yield pltpu.make_async_copy(
                grads_ref.at[shards, rows],
                own.at[kind, lax.rem(chunk, 2), pl.ds(i * cols, cols)],
                own_sem.at[kind, lax.rem(chunk, 2)],
            )

    def split(kind, stage):
        axis, bit, count, rows = plans[kind][stage]
        part = bit_of(axis, bit)
        if axis == "img":
            return (
                [((pl.ds(0, count), pl.ds(pl.multiple_of((1 - part) * rows, 16), rows)), pl.ds(0, count))],
                lambda i: (i, pl.ds(pl.multiple_of(part * rows, 16), rows)),
            )
        if axis == "row":
            return (
                [((pl.ds((1 - part) * count, count), pl.ds(0, rows)), pl.ds(0, count))],
                lambda i: (part * count + i, pl.ds(0, rows)),
            )
        return (
            [((pl.ds(2 * i + 1 - part, 1), pl.ds(0, rows)), pl.ds(i, 1)) for i in range(count)],
            lambda i: (2 * i + part, pl.ds(0, rows)),
        )

    def stage_copies(kind, stage, chunk):
        axis, bit, count, rows = plans[kind][stage]
        for (shards, lines), target in split(kind, stage)[0]:
            yield pltpu.make_async_remote_copy(
                src_ref=held[kind][stage].at[chunk, shards, lines],
                dst_ref=held[kind][stage + 1].at[chunk, target],
                send_sem=send_sem.at[kind, stage + 1, chunk],
                recv_sem=recv_sem.at[kind, stage + 1, chunk],
                device_id=partner(axis, bit),
                device_id_type=MESH,
            )

    def whole(kind, stage, chunk):
        buffer = held[kind][stage].at[chunk]
        return pltpu.make_async_remote_copy(
            src_ref=buffer,
            dst_ref=buffer,
            send_sem=send_sem.at[kind, stage, chunk],
            recv_sem=recv_sem.at[kind, stage, chunk],
            device_id=partner("row", 1),
            device_id_type=MESH,
        )

    last_rows = plans[0][-1][3]

    def out_rows(kind, chunk):
        return pl.ds(pl.multiple_of(chunk_rows(kind, chunk) + image_place() * last_rows, 16), last_rows)

    def image_place():
        place = 0
        for i in range(image_stages):
            place = place + bit_of("img", 1 << i) * (1 << (image_stages - 1 - i))
        return place

    def spread_copies(kind, chunk):
        for i in range(1, groups):
            place = dict(places)
            place["img"] = lax.rem(places["img"] + i, groups)
            yield pltpu.make_async_remote_copy(
                src_ref=held[kind][stages].at[chunk, 0],
                dst_ref=out_ref.at[out_rows(kind, chunk)],
                send_sem=spread_sem.at[kind, i, chunk],
                recv_sem=spread_recv.at[kind, i, chunk],
                device_id=tuple(place[name] for name in ("img", "row", "col")),
                device_id_type=MESH,
            )

    def home_copy(kind, chunk):
        return pltpu.make_async_copy(
            held[kind][stages].at[chunk, 0],
            out_ref.at[out_rows(kind, chunk)],
            out_sem.at[kind, chunk],
        )

    def start(copies):
        for copy in copies:
            copy.start()

    barrier = pltpu.get_barrier_semaphore()
    near = [partner("row", 1)] + [partner(a, b) for a, b, _, _ in plans[0] if a != "img"]
    for i in range(1, groups):
        place = dict(places)
        place["img"] = lax.rem(places["img"] + i, groups)
        near.append(tuple(place[name] for name in ("img", "row", "col")))
    for other in near:
        pl.semaphore_signal(barrier, inc=1, device_id=other, device_id_type=MESH)
    pl.semaphore_wait(barrier, len(near))

    def begin(chunk):
        for kind in range(2):
            start(first_copies(kind, chunk))
            start(own_copies(kind, chunk))

    begin(0)

    def time_step(t, carry):
        for stage in range(stages, -1, -1):
            chunk = t - stage

            @pl.when(jnp.logical_and(chunk >= 0, chunk < steps))
            def _(stage=stage, chunk=chunk):
                if stage == 0:

                    @pl.when(chunk + 1 < steps)
                    def _():
                        begin(chunk + 1)

                for kind in range(2):
                    buffer = held[kind][stage]
                    whole(kind, stage, chunk).wait_recv()
                    if stage == 0:
                        for copy in own_copies(kind, chunk):
                            copy.wait()
                        count = first_count

                        def add(i, carry, buffer=buffer, kind=kind):
                            mine = own[kind, lax.rem(chunk, 2), i].astype(F32)
                            buffer[chunk, i] = (buffer[chunk, i].astype(F32) + mine).astype(BF)
                            return carry
                    else:
                        count = plans[kind][stage - 1][2]
                        kept = split(kind, stage - 1)[1]
                        before = held[kind][stage - 1]

                        def add(i, carry, buffer=buffer, before=before, kept=kept):
                            shard, lines = kept(i)
                            mine = before[chunk, shard, lines].astype(F32)
                            buffer[chunk, i] = (buffer[chunk, i].astype(F32) + mine).astype(BF)
                            return carry

                    lax.fori_loop(0, count, add, 0)
                    if stage < stages:
                        start(stage_copies(kind, stage, chunk))
                    else:
                        start(spread_copies(kind, chunk))
                        home_copy(kind, chunk).start()

        return carry

    lax.fori_loop(0, steps + stages, time_step, 0)

    def drain(chunk, carry):
        for kind in range(2):
            for stage in range(stages + 1):
                whole(kind, stage, chunk).wait_send()
            for copy in spread_copies(kind, chunk):
                copy.wait()
            home_copy(kind, chunk).wait()
        return carry

    lax.fori_loop(0, steps, drain, 0)


def sum_everywhere(grads, sizes):
    groups, row_count, cols = sizes
    count, rows, width = grads.shape
    height = 16 * groups
    steps = rows // (2 * height)
    first_count = count // 2
    buffers = []
    for kind in range(2):
        plan = sum_plan(sizes, bool(kind))
        buffers.append(pltpu.VMEM((steps, first_count, height, width), BF))
        buffers += [pltpu.VMEM((steps, c, h, width), BF) for _, _, c, h in plan]
    stages = len(sum_plan(sizes, False))
    return pl.pallas_call(
        functools.partial(sum_kernel, sizes, steps),
        out_shape=jax.ShapeDtypeStruct((rows, width), BF),
        in_specs=[pl.BlockSpec(memory_space=pl.ANY)],
        out_specs=pl.BlockSpec(memory_space=pl.ANY),
        scratch_shapes=buffers
        + [
            pltpu.VMEM((2, 2, first_count, height, width), BF),
            pltpu.SemaphoreType.DMA((2, stages + 1, steps)),
            pltpu.SemaphoreType.DMA((2, stages + 1, steps)),
            pltpu.SemaphoreType.DMA((2, groups, steps)),
            pltpu.SemaphoreType.DMA((2, groups, steps)),
            pltpu.SemaphoreType.DMA((2, 2)),
            pltpu.SemaphoreType.DMA((2, steps)),
        ],
        compiler_params=pltpu.CompilerParams(
            collective_id=1, has_side_effects=True, vmem_limit_bytes=56 * 2**20
        ),
        cost_estimate=pl.CostEstimate(flops=2**28, bytes_accessed=2**28, transcendentals=0),
    )(grads)


def all_to_all(values):
    return lax.all_to_all(values, GROUP, split_axis=0, concat_axis=0, tiled=True)


def body(
    latents, skip, temb, text, text_len, extent, embed_weight, skip_weight, shift_weight,
    qkv_weight, out_weight, cross_query, cross_keys, cross_out, up_weight, down_weight,
    final_weight, norm_gain, norm_shift, skip_gain, skip_shift, head_gain, head_shift,
    front_biases, all_biases, cross_bias, cotangent,
):
    img_count, tile_rows, tile_cols, patch_vals = latents.shape
    tokens = tile_rows * tile_cols
    near_vals = 9 * patch_vals
    row_count = lax.axis_size("row")
    col_count = lax.axis_size("col")
    count = row_count * col_count
    groups = lax.axis_size("img")
    jobs = img_count * HEADS // count
    row_index = lax.axis_index("row")
    col_index = lax.axis_index("col")
    group_index = lax.axis_index("img")
    device = row_index * col_count + col_index
    shard = D // count
    hid_shard = FF // count
    hid_part = hid_shard // groups

    small_widths = (
        norm_gain.size, norm_shift.size, skip_gain.size, skip_shift.size,
        head_gain.size, head_shift.size, front_biases.size, all_biases.size,
    )
    small = jnp.concatenate(
        [
            embed_weight.T.reshape(-1), final_weight.reshape(-1), norm_gain.reshape(-1),
            norm_shift.reshape(-1), skip_gain, skip_shift, head_gain, head_shift,
            front_biases, all_biases,
        ]
    )
    small_len = small.size
    padded_len = -(-(small_len + img_count * D) // 2048) * 2048
    time_act = jax.nn.silu(temb.astype(F32)).astype(BF)
    time_own = lax.dynamic_slice_in_dim(time_act, device * shard, shard, 1)
    shift_share = matmul(time_own, shift_weight).astype(BF).reshape(-1)
    small = jnp.pad(jnp.concatenate([small, shift_share]), (0, padded_len - small_len - shift_share.size))
    small_all = all_to_all(jnp.broadcast_to(small.reshape(1, -1, 128), (count, padded_len // 128, 128)))
    small_all = small_all.reshape(count, padded_len)
    def beside(values, parts):
        return jnp.concatenate(jnp.split(values, parts, axis=0), axis=1)

    def below(values, parts):
        width = values.shape[1] // parts
        blocks = [values[:, i * width : (i + 1) * width] for i in range(parts)]
        return jnp.stack([b.reshape(count, -1, width) for b in blocks], axis=1).reshape(-1, width)

    first_all = lax.all_gather(
        jnp.concatenate([beside(skip_weight, 2), qkv_weight], axis=1), GROUP, axis=0, tiled=True
    )
    skip_full = below(first_all[:, : 2 * D], 2)
    qkv_full = first_all[:, 2 * D :]
    folds = hid_part // shard
    fold_rows = hid_part // folds
    up_part = lax.dynamic_index_in_dim(
        up_weight.reshape(shard, count, groups, hid_part), group_index, 2, keepdims=False
    ).reshape(shard, count * hid_part)
    down_part = lax.dynamic_index_in_dim(
        down_weight.reshape(groups, hid_part, D), group_index, 0, keepdims=False
    )
    third = jnp.concatenate(
        [jnp.pad(up_part, ((0, fold_rows - shard), (0, 0))), beside(down_part, folds)], axis=1
    )

    wide = shard * near_vals
    embed_t = small_all[:, :wide].reshape(D, near_vals)
    final_full = small_all[:, wide : 2 * wide].reshape(D, near_vals)
    vectors = cuts(small_all[:, 2 * wide : small_len].astype(F32), small_widths)
    gain_rows = jnp.transpose(vectors[0].reshape(count, 3, shard), (1, 0, 2)).reshape(3, D)
    offset_rows = jnp.transpose(vectors[1].reshape(count, 3, shard), (1, 0, 2)).reshape(3, D)
    skip_gains, skip_offsets = vectors[2].reshape(-1), vectors[3].reshape(-1)
    head_gains, head_offsets = vectors[4].reshape(4, HD), vectors[5].reshape(4, HD)
    bias_embed, bias_skip, bias_shift, bias_qkv = cuts(vectors[6].reshape(-1), (D, D, D, 3 * D))
    bias_out, bias_cross_q, bias_cross_o, bias_up, bias_down = cuts(
        vectors[7].reshape(-1), (D, D, D, FF, D)
    )
    bias_up_part = lax.dynamic_index_in_dim(
        bias_up.reshape(count, groups, hid_part), group_index, 1, keepdims=False
    ).reshape(-1)

    local_rows = row_index * tile_rows + jnp.arange(tile_rows, dtype=jnp.int32)
    local_cols = col_index * tile_cols + jnp.arange(tile_cols, dtype=jnp.int32)
    inside = (
        (local_rows[None, :, None] < extent[:, 0, None, None])
        & (local_cols[None, None, :] < extent[:, 1, None, None])
    ).astype(F32)
    token_inside = inside.reshape(img_count, tokens, 1)
    own_angle = angles_of(
        jnp.tile(jnp.repeat(local_rows, tile_cols), img_count),
        jnp.tile(jnp.tile(local_cols, tile_rows), img_count),
    )
    own_cos, own_sin = jnp.cos(own_angle), jnp.sin(own_angle)
    every = np.arange(count * tokens)
    every_row = every // tokens // col_count * tile_rows + every % tokens // tile_cols
    every_col = every // tokens % col_count * tile_cols + every % tile_cols
    every_angle = angles_of(jnp.asarray(every_row), jnp.asarray(every_col))
    every_cos, every_sin = jnp.cos(every_angle), jnp.sin(every_angle)
    job_images = (device * jobs + jnp.arange(jobs, dtype=jnp.int32)) % img_count
    ext_jobs = jnp.take(extent, job_images, axis=0)
    geo = (count, tile_rows, tile_cols, col_count, KEY_BLOCK // tokens)

    def gelu_tanh(values):
        return jax.nn.gelu(values, approximate=True)

    text_width = cross_keys.shape[1]
    text_count = -(-text.shape[1] // 128) * 128
    text_wide = jnp.pad(text, ((0, 0), (0, text_count - text.shape[1]), (0, 0)))
    is_key = device * text_width + jnp.arange(text_width, dtype=jnp.int32) < D

    def text_norm(values, scales, offsets):
        per_head = values.reshape(text_width // HD, HD, -1)
        centre = per_head - jnp.mean(per_head, axis=1, keepdims=True)
        spread = jnp.mean(centre * centre, axis=1, keepdims=True)
        unit = centre * lax.rsqrt(spread + NORM_EPS) * scales[:, None] + offsets[:, None]
        return jnp.where(is_key[:, None], unit.reshape(values.shape), values)

    text_part = dot(cross_keys, text_wide, (0,), (2,)).reshape(text_width, -1)
    text_part = text_part + cross_bias.astype(F32)[:, None]
    text_normed, text_pull = jax.vjp(text_norm, text_part, head_gains[3], head_offsets[3])
    moves = Moves()
    second_all = lax.all_gather(
        jnp.concatenate(
            [out_weight, cross_query, cross_out, beside(text_normed.astype(BF), 2)], axis=1
        ),
        GROUP,
        axis=0,
        tiled=True,
    )
    out_full, cross_q_full, cross_o_full = [second_all[:, i * D : (i + 1) * D] for i in range(3)]
    text_both = below(second_all[:, 3 * D :], 2).reshape(2, HEADS, HD, img_count * text_count)
    third_all = lax.all_gather(third, GROUP, axis=0, tiled=True)
    third_rows = third_all.reshape(count, fold_rows, -1)
    up_full = third_rows[:, :shard, : count * hid_part].reshape(D, count * hid_part)
    down_full = below(third_all[:, count * hid_part :], folds)
    shift_sums = small_all[:, small_len : small_len + img_count * D].astype(F32)
    shift_rows = jnp.sum(shift_sums, axis=0).reshape(img_count, D) + bias_shift

    lat_masked = (latents * inside[..., None]).astype(BF)
    cot_masked = (cotangent * inside[..., None]).astype(BF)
    rims = with_halo(
        jnp.concatenate([lat_masked, cot_masked], axis=-1), (("row", 1), ("col", 2)), 1
    )
    rims = rims.astype(F32)
    near = gather_near(rims[..., :patch_vals], tile_rows, tile_cols)
    near = near.reshape(img_count, tokens, near_vals).astype(BF)
    cot_near = gather_near(rims[..., patch_vals:], tile_rows, tile_cols)
    cot_near = cot_near.reshape(img_count, tokens, near_vals)
    embedded = matmul_back(near, embed_t) + bias_embed
    joined_full = jnp.concatenate(
        [embedded, skip.reshape(img_count, tokens, D).astype(F32)], axis=-1
    )
    skip_normed, skip_norm_pull = jax.vjp(layer_norm, joined_full, skip_gains, skip_offsets)
    skip_in = skip_normed.astype(BF)
    resid_in = matmul(skip_in, skip_full) + bias_skip
    self_norm, self_norm_pull = jax.vjp(layer_norm, resid_in, gain_rows[0], offset_rows[0])
    normed = (self_norm + shift_rows[:, None, :]).astype(BF)

    qkv_t = dot(qkv_full, normed, (0,), (2,)) + bias_qkv[:, None, None]
    qkv_t = qkv_t.astype(BF).reshape(3, HEADS, HD, img_count, tokens)
    qkv_jobs = all_to_all(
        jnp.transpose(qkv_t, (1, 3, 0, 2, 4)).reshape(count, jobs, 3, HD, tokens)
    )
    head_cols = jnp.stack([head_gains[0], head_offsets[0], head_gains[1], head_offsets[1]], axis=1)
    mixed_jobs, keep, total = attend(ext_jobs, qkv_jobs, every_cos, every_sin, head_cols, geo)
    mixed = all_to_all(mixed_jobs).reshape(HEADS, img_count, HD, tokens)
    attended_t = jnp.transpose(mixed, (1, 0, 2, 3)).reshape(img_count, D, tokens)
    resid_self = resid_in + dot(attended_t, out_full, (1,), (0,)) + bias_out

    cross_norm, cross_norm_pull = jax.vjp(layer_norm, resid_self, gain_rows[1], offset_rows[1])
    cross_in = cross_norm.astype(BF)
    all_tokens = img_count * tokens
    cross_rows = dot(cross_q_full, cross_in.reshape(all_tokens, D), (0,), (1,))
    cross_rows = (cross_rows + bias_cross_q[:, None]).reshape(HEADS, HD, all_tokens)
    cross_cols = jnp.stack([head_gains[2], head_offsets[2]], axis=1)
    cross_mixed, cross_total = cross_attend(
        text_len, cross_rows, text_both, own_cos, own_sin, cross_cols
    )
    cross_low = cross_mixed.reshape(D, all_tokens)
    cross_out_rows = dot(cross_low, cross_o_full, (0,), (0,)).reshape(img_count, tokens, D)
    resid_cross = resid_self + cross_out_rows + bias_cross_o

    mlp_norm, mlp_norm_pull = jax.vjp(layer_norm, resid_cross, gain_rows[2], offset_rows[2])
    mlp_in = images_gather(mlp_norm.astype(BF))
    hidden = matmul(mlp_in, up_full) + bias_up_part
    gelu_out, gelu_pull = jax.vjp(gelu_tanh, hidden)
    activated = gelu_out.astype(BF)
    resid_out = resid_cross + images_scatter(matmul(activated, down_full)) + bias_down
    resid_low = resid_out.astype(BF)
    emitted = matmul(resid_low, final_full) * token_inside
    emit_rim = with_halo(
        emitted.reshape(img_count, tile_rows, tile_cols, near_vals), (("row", 1), ("col", 2)), 1
    )
    out_latents = spread_near(emit_rim, tile_rows, tile_cols, patch_vals) * inside[..., None]

    lead = (0, 1)
    by_row = row_first()
    grad_emitted = (cot_near * token_inside).astype(BF)
    grad_final = weight_grad(resid_low, grad_emitted)
    grad_resid_out = matmul_back(grad_emitted, final_full)
    grad_down_low = grad_resid_out.astype(BF)
    bias_down_grad = column_sum(grad_down_low)
    grad_down_rows = images_gather(grad_down_low)
    every_lead = (0, 1, 2)
    activated, out_latents = lax.optimization_barrier((activated, out_latents))
    grad_down_rows = moves.begin(
        grad_down_rows,
        down=shard_sum(by_row, all_images, activated, grad_down_rows, every_lead, every_lead, 3),
    )
    grad_hidden = gelu_pull(matmul_back(grad_down_rows, down_full))[0].astype(BF)
    grad_hidden = moves.begin(
        grad_hidden,
        up=shard_sum(by_row, all_images, mlp_in, grad_hidden, every_lead, every_lead, 3),
    )
    bias_up_grad = column_sum(grad_hidden)
    grad_mlp_in = images_scatter(matmul_back(grad_hidden, up_full))
    grad_from_mlp, gain_mlp_grad, shift_mlp_grad = mlp_norm_pull(grad_mlp_in)
    grad_resid_cross = grad_resid_out + grad_from_mlp

    grad_cross_low = grad_resid_cross.astype(BF)
    grad_cross_flat = grad_cross_low.reshape(all_tokens, D)
    whole_grads = {"cross_o": dot(cross_low, grad_cross_flat, (1,), (0,))}
    bias_cross_o_grad = column_sum(grad_cross_low)
    grad_cross_mixed = dot(cross_o_full, grad_cross_flat, (1,), (1,)).astype(BF)
    grad_cross_rows, grad_text, cross_head_grads = cross_attend_back(
        text_len, cross_rows, text_both, grad_cross_mixed.reshape(HEADS, HD, all_tokens),
        cross_total, own_cos, own_sin, cross_cols,
    )
    cross_head_grads = jnp.sum(cross_head_grads, axis=0)
    grad_cross_rows = grad_cross_rows.reshape(D, all_tokens)
    whole_grads["cross_q"] = dot(cross_in.reshape(all_tokens, D), grad_cross_rows, (0,), (1,))
    bias_cross_q_grad = jnp.sum(grad_cross_rows.astype(F32), axis=1)
    grad_cross_in = dot(grad_cross_rows, cross_q_full, (0,), (1,))
    grad_from_cross, gain_cross_grad, shift_cross_grad = cross_norm_pull(
        grad_cross_in.reshape(img_count, tokens, D)
    )
    grad_resid_self = grad_resid_cross + grad_from_cross

    grad_out_rows = grad_resid_self.astype(BF)
    whole_grads["out"] = dot(attended_t, grad_out_rows, (0, 2), lead)
    bias_out_grad = column_sum(grad_out_rows)
    grad_attended = dot(out_full, grad_out_rows, (1,), (2,)).astype(BF)
    grad_attended = jnp.transpose(
        grad_attended.reshape(HEADS, HD, img_count, tokens), (0, 2, 1, 3)
    )
    grad_mixed_jobs = all_to_all(grad_attended.reshape(count, jobs, HD, tokens))
    grad_mixed_jobs = moves.step(grad_mixed_jobs, "down", "up")
    grad_jobs, head_grads = attend_back(
        ext_jobs, qkv_jobs, grad_mixed_jobs, keep, total, every_cos, every_sin, head_cols, geo
    )
    grad_qkv_t = moves.step(all_to_all(grad_jobs), "down", "up").reshape(
        HEADS, img_count, 3, HD, tokens
    )
    grad_qkv_t = moves.begin(
        grad_qkv_t, text=offload_sum(alone, grad_text.reshape(2 * D, img_count * text_count))
    )
    grad_qkv_t = jnp.transpose(grad_qkv_t, (2, 0, 3, 1, 4)).reshape(3 * D, img_count, tokens)
    head_grads = jnp.sum(head_grads, axis=0)

    for i, name in enumerate(("query", "key", "value")):
        whole_grads[name] = dot(normed, grad_qkv_t[i * D : (i + 1) * D], (0, 1), (1, 2))
    bias_qkv_grad = jnp.sum(grad_qkv_t.astype(F32), axis=(1, 2))
    grad_normed = dot(grad_qkv_t, qkv_full, (0,), (1,))
    grad_normed = moves.step(grad_normed, "down", "up")
    grad_shift_rows = jnp.sum(grad_normed, axis=1)
    bias_shift_grad = jnp.sum(grad_shift_rows, axis=0)
    grad_from_self, gain_self_grad, shift_self_grad = self_norm_pull(grad_normed)
    grad_resid_in = grad_resid_self + grad_from_self
    grad_merged = moves.step(grad_resid_in.astype(BF), "down", "up")
    whole_grads["skip"] = weight_grad(skip_in, grad_merged)
    bias_skip_grad = column_sum(grad_merged)
    grad_skip_normed = matmul_back(grad_merged, skip_full)
    grad_joined, skip_gain_grad, skip_shift_grad = skip_norm_pull(grad_skip_normed)
    grad_skip = grad_joined[..., D:].reshape(img_count, tile_rows, tile_cols, D)
    grad_embedded = grad_joined[..., :D].astype(BF)
    grad_embed_t = weight_grad(grad_embedded, near)
    bias_embed_grad = column_sum(grad_embedded)
    grad_near = matmul(grad_embedded, embed_t).reshape(
        img_count, tile_rows, tile_cols, near_vals
    )
    near_rim = with_halo(grad_near, (("row", 1), ("col", 2)), 1)
    grad_latents = spread_near(near_rim, tile_rows, tile_cols, patch_vals) * inside[..., None]

    moves.finish(*list(moves.running))
    shards = moves.done
    names = ("query", "key", "value", "skip", "out", "cross_q", "cross_o")
    packed = [whole_grads[name].astype(BF).reshape(count, -1, D) for name in names]
    packed_rows = sum(part.shape[1] for part in packed)
    fill = -packed_rows % (32 * groups)
    packed = jnp.pad(jnp.concatenate(packed, axis=1), ((0, 0), (0, fill), (0, 0)))
    summed = sum_everywhere(packed, (groups, row_count, col_count)).astype(F32)
    total_of, at = {}, 0
    for name in names:
        rows = whole_grads[name].shape[0] // count
        total_of[name] = summed[at : at + rows]
        at += rows
    grad_text_lin, head_gain_ck_grad, head_shift_ck_grad = text_pull(shards["text"])
    grad_text_low = grad_text_lin.astype(BF)
    grad_cross_keys = images_sum(
        dot(
            text_wide, grad_text_low.reshape(text_width, img_count, text_count), (0, 1), (1, 2)
        ),
        BF,
    )
    grad_cross_bias = images_sum(jnp.sum(grad_text_low.astype(F32), axis=1), F32)

    def by_device(vector):
        return vector.reshape(count, -1)

    def rows_by_device(rows):
        return jnp.transpose(rows.reshape(3, count, shard), (1, 0, 2)).reshape(count, -1)

    bias_up_all = jnp.where(
        (jnp.arange(groups) == group_index)[None, :, None],
        bias_up_grad.reshape(count, 1, hid_part),
        0.0,
    ).reshape(-1)
    small_grads = jnp.concatenate(
        [
            by_device(grad_embed_t),
            by_device(grad_final),
            rows_by_device(jnp.stack([gain_self_grad, gain_cross_grad, gain_mlp_grad])),
            rows_by_device(jnp.stack([shift_self_grad, shift_cross_grad, shift_mlp_grad])),
            by_device(skip_gain_grad),
            by_device(skip_shift_grad),
            by_device(
                jnp.concatenate(
                    [head_grads[:, 0], head_grads[:, 2], cross_head_grads[:, 0], head_gain_ck_grad]
                )
            ),
            by_device(
                jnp.concatenate(
                    [head_grads[:, 1], head_grads[:, 3], cross_head_grads[:, 1], head_shift_ck_grad]
                )
            ),
            by_device(
                jnp.concatenate([bias_embed_grad, bias_skip_grad, bias_shift_grad, bias_qkv_grad])
            ),
            by_device(
                jnp.concatenate(
                    [
                        bias_out_grad, bias_cross_q_grad, bias_cross_o_grad, bias_up_all,
                        bias_down_grad,
                    ]
                )
            ),
        ],
        axis=1,
    )
    shift_share = jnp.broadcast_to(grad_shift_rows.reshape(1, -1), (count, img_count * D))
    small_grads = jnp.concatenate([small_grads, shift_share], axis=1).astype(BF)
    small_grads = jnp.pad(small_grads, ((0, 0), (0, padded_len - small_grads.shape[1])))
    small_got = all_to_all(small_grads.reshape(count, -1, 128)).astype(F32)
    small_got = jnp.sum(small_got, axis=0).reshape(-1)
    small_sum = images_sum(small_got[:small_len], F32)
    total_parts = cuts(small_sum, (wide, wide) + small_widths)
    grad_shift = lax.dot_general(
        time_own.astype(F32),
        small_got[small_len : small_len + img_count * D].reshape(img_count, D),
        (((0,), (0,)), ((), ())),
        precision=lax.Precision.HIGHEST,
    )

    total_up = jnp.transpose(
        shards["up"].reshape(groups, shard, count, hid_part), (1, 2, 0, 3)
    ).reshape(shard, FF)
    total_down = shards["down"].reshape(hid_shard, D)
    return (
        out_latents,
        grad_latents,
        grad_skip,
        total_parts[0].reshape(shard, near_vals).T,
        total_of["skip"],
        images_sum(grad_shift, F32),
        jnp.concatenate([total_of[name] for name in ("query", "key", "value")], axis=1),
        total_of["out"],
        total_of["cross_q"],
        grad_cross_keys,
        total_of["cross_o"],
        total_up.astype(F32),
        total_down.astype(F32),
        total_parts[1].reshape(shard, near_vals),
        total_parts[2].reshape(3, shard),
        total_parts[3].reshape(3, shard),
        total_parts[4],
        total_parts[5],
        total_parts[6],
        total_parts[7],
        total_parts[8],
        total_parts[9],
        grad_cross_bias,
    )


def solution(mesh):
    tile = P("img", "row", "col", None)
    rows = P(GROUP, None)
    columns = P(None, GROUP)
    vector = P(GROUP)
    return jax.shard_map(
        body,
        mesh=mesh,
        in_specs=(
            tile, tile, P("img", None), P("img", None, None), P("img", None), P("img", None),
            columns, rows, rows, rows, rows, rows, columns, rows, rows, rows, rows,
            columns, columns, vector, vector, vector, vector, vector, vector, vector, tile,
        ),
        out_specs=(
            tile, tile, tile, columns, rows, rows, rows, rows, rows, columns, rows, rows, rows,
            rows, columns, columns, vector, vector, vector, vector, vector, vector, vector,
        ),
        check_vma=False,
    )
```

```python
import functools
import math
from typing import NamedTuple

import jax
import jax.numpy as jnp
import numpy as np
from jax import lax
from jax.experimental import pallas as pl
from jax.experimental.pallas import tpu as pltpu
from jax.sharding import PartitionSpec as P

D = 1408
HEADS = 16
HD = 88
FF = 6144
CLIP = 77
NORM_EPS = 1e-06
NEG_FILL = -1e30
STEPS = ((-1, -1), (-1, 0), (-1, 1), (0, -1), (0, 0), (0, 1), (1, -1), (1, 0), (1, 1))
GROUP = ("row", "col")
F32 = jnp.float32
BF = jnp.bfloat16
SCALE = 1.0 / math.sqrt(HD)
LOG2E = math.log2(math.e)
NT = (((1,), (1,)), ((), ()))
KEY_BLOCK = 256
QUERY_CHUNK = 1024


def with_halo(block, sides, width):
    for axis, dim in sides:
        count = lax.axis_size(axis)
        forward = [(i, i + 1) for i in range(count - 1)]
        backward = [(target, source) for source, target in forward]
        low = lax.ppermute(
            lax.slice_in_dim(block, block.shape[dim] - width, None, axis=dim), axis, forward
        )
        high = lax.ppermute(lax.slice_in_dim(block, 0, width, axis=dim), axis, backward)
        block = jnp.concatenate([low, block, high], axis=dim)
    return block


def dot(former, latter, former_dims, latter_dims):
    return lax.dot_general(
        former, latter, ((former_dims, latter_dims), ((), ())), preferred_element_type=F32
    )


def matmul(former, latter):
    return dot(former, latter, (former.ndim - 1,), (0,))


def matmul_back(former, latter):
    return dot(former, latter, (former.ndim - 1,), (1,))


def weight_grad(inputs, grads):
    lead = tuple(range(inputs.ndim - 1))
    return dot(inputs, grads, lead, lead)


def column_sum(grads):
    return jnp.sum(grads.astype(F32), axis=tuple(range(grads.ndim - 1)))


def layer_norm(values, scales, offsets):
    centre = values - jnp.mean(values, axis=-1, keepdims=True)
    spread = jnp.mean(centre * centre, axis=-1, keepdims=True)
    return centre * lax.rsqrt(spread + NORM_EPS) * scales + offsets


def angles_of(row_place, col_place):
    pair_index = np.arange(HD) // 2
    quarter = HD // 4
    within = np.where(pair_index < quarter, pair_index, pair_index - quarter).astype(np.float32)
    frequency = np.exp(np.float32(-math.log(10000.0)) * within / np.float32(quarter))
    by_row = jnp.asarray(pair_index < quarter)
    places = jnp.where(by_row[:, None], row_place[None, :], col_place[None, :])
    return places.astype(F32) * jnp.asarray(frequency.astype(np.float32))[:, None]


def gather_near(padded, tall, broad):
    return jnp.concatenate(
        [
            padded[..., 1 + step_row : 1 + step_row + tall, 1 + step_col : 1 + step_col + broad, :]
            for step_row, step_col in STEPS
        ],
        axis=-1,
    )


def spread_near(padded, tall, broad, channels):
    result = None
    for number, (step_row, step_col) in enumerate(STEPS):
        portion = padded[
            ...,
            1 - step_row : 1 - step_row + tall,
            1 - step_col : 1 - step_col + broad,
            number * channels : (number + 1) * channels,
        ]
        result = portion if result is None else result + portion
    return result


def cuts(vector, widths):
    ends = np.cumsum((0,) + widths)
    return [vector[..., ends[i] : ends[i + 1]] for i in range(len(widths))]


def swap_images(values, bit):
    count = lax.axis_size("img")
    return lax.ppermute(values, "img", [(i, i ^ bit) for i in range(count)])


def images_gather(values):
    blocks = values[None]
    while blocks.shape[0] < lax.axis_size("img"):
        blocks = jnp.concatenate([blocks, swap_images(blocks, blocks.shape[0])])
    return blocks


def images_scatter(parts):
    while parts.shape[0] > 1:
        half = parts.shape[0] // 2
        parts = parts[:half] + swap_images(parts[half:].astype(BF), half).astype(F32)
    return parts[0]


def images_sum(values, sent):
    bit = 1
    while bit < lax.axis_size("img"):
        values = values.astype(sent)
        values = values.astype(F32) + swap_images(values, bit).astype(F32)
        bit *= 2
    return values.astype(F32)


def exchange(values, axis, bit):
    if bit is None:
        return lax.psum_scatter(values, axis, scatter_dimension=0, tiled=True)
    size = lax.axis_size(axis)
    return lax.ppermute(values, axis, [(i, i ^ bit) for i in range(size)])


def halves(values, dim, bit):
    keep = lax.dynamic_index_in_dim(values, bit, dim, keepdims=False)
    return keep, lax.dynamic_index_in_dim(values, 1 - bit, dim, keepdims=False)


def core_features(values, dim, core):
    rows = lax.axis_size("row")
    block = values.shape[dim] // rows
    return jnp.concatenate(
        [
            lax.dynamic_slice_in_dim(values, (2 * i + core) * block, block, dim)
            for i in range(rows // 2)
        ],
        axis=dim,
    )


def row_first():
    rows, cols = lax.axis_size("row"), lax.axis_size("col")
    row_bits = [("row", 1 << i) for i in range(1, rows.bit_length() - 1)]
    return row_bits + [("col", 1 << i) for i in range(cols.bit_length() - 1)]


def shard_sum(order, after, inputs, grads, input_lead, grad_lead, feature):
    core = lax.axis_index("row") % 2
    give = dot(core_features(inputs, feature, 1 - core), grads, input_lead, grad_lead)
    (got,) = yield [give.astype(BF)], "row", 1
    keep = dot(core_features(inputs, feature, core), grads, input_lead, grad_lead)
    part = yield from scatter_sum(order, keep + got.astype(F32))
    part = yield from after(part)
    return part


def offload_sum(after, part):
    (got,) = yield [part.astype(BF)], GROUP, None
    part = yield from after(got.astype(F32))
    return part


def scatter_sum(order, part):
    dims = [d for d in reversed(row_first()) if d[0] == "row"]
    dims += [d for d in reversed(row_first()) if d[0] == "col"]
    width = part.shape[-1]
    part = part.reshape((2,) * len(dims) + (-1, width))
    for axis, bit in order:
        at = dims.index((axis, bit))
        keep, give = halves(part, at, lax.axis_index(axis) // bit % 2)
        del dims[at]
        (got,) = yield [give.astype(BF)], axis, bit
        part = keep + got.astype(F32)
    return part.reshape(-1, width)


def alone(part):
    return part
    yield


def all_images(part):
    bit, blocks = 1, part.astype(BF)[None]
    while bit < lax.axis_size("img"):
        (got,) = yield [blocks], "img", bit
        blocks = placed(blocks, got, lax.axis_index("img") // bit % 2, 0)
        blocks = blocks.reshape((-1,) + part.shape)
        bit *= 2
    return blocks


def placed(mine, other, bit, dim):
    first = lax.select(jnp.broadcast_to(bit == 0, mine.shape), mine, other)
    last = lax.select(jnp.broadcast_to(bit == 0, mine.shape), other, mine)
    return jnp.stack([first, last], axis=dim)


class Moves:
    def __init__(self):
        self.running = {}
        self.done = {}

    def begin(self, value, **makers):
        return self.launch(value, {name: (maker, next(maker)) for name, maker in makers.items()})

    def launch(self, value, wanted):
        if not wanted:
            return value
        gives = {name: request[0] for name, (_, request) in wanted.items()}
        value, gives = lax.optimization_barrier((value, gives))
        for name, (maker, (_, axis, bit)) in wanted.items():
            self.running[name] = (maker, [exchange(give, axis, bit) for give in gives[name]])
        return value

    def step(self, value, *names):
        names = [name for name in names if name in self.running]
        if not names:
            return value
        value, gots = lax.optimization_barrier(
            (value, {name: self.running[name][1] for name in names})
        )
        wanted = {}
        for name in names:
            maker = self.running.pop(name)[0]
            try:
                wanted[name] = (maker, maker.send(gots[name]))
            except StopIteration as stop:
                self.done[name] = stop.value
        return self.launch(value, wanted)

    def finish(self, *names):
        waiting = [name for name in names if name in self.running]
        while waiting:
            for name in waiting:
                maker, gots = self.running.pop(name)
                try:
                    gives, axis, bit = maker.send(gots)
                    self.running[name] = (maker, [exchange(give, axis, bit) for give in gives])
                except StopIteration as stop:
                    self.done[name] = stop.value
            waiting = [name for name in names if name in self.running]


def unit_rows(values):
    centre = values - jnp.mean(values, axis=0, keepdims=True)
    rstd = lax.rsqrt(jnp.mean(centre * centre, axis=0, keepdims=True) + NORM_EPS)
    return centre * rstd, rstd


def swap_pairs(values, back):
    rows = values.shape[0]
    even = lax.broadcasted_iota(jnp.int32, values.shape, 0) % 2 == 0
    up = pltpu.roll(values, rows - 1, 0)
    down = pltpu.roll(values, 1, 0)
    return jnp.where(even, up, -down) if back else jnp.where(even, -up, down)


def turn(values, cos, sin):
    return values * cos + swap_pairs(values, False) * sin


def turn_back(values, cos, sin):
    return values * cos + swap_pairs(values, True) * sin


def tiles(ref, part, count):
    return jnp.concatenate([ref[s, 0, part] for s in range(count)], axis=1)


def key_blocks(geo, ext_ref, job):
    count, tile_rows, tile_cols, col_tiles, block_tiles = geo
    rows = ext_ref[job, 0] // tile_rows
    groups = ext_ref[job, 1] // (block_tiles * tile_cols)

    def place(i):
        block = i // groups * (col_tiles // block_tiles) + i % groups
        return pl.multiple_of(block * KEY_BLOCK, KEY_BLOCK)

    return rows * groups, place


def attend_kernel(
    geo, ext_ref, qkv_ref, cos_ref, sin_ref, head_ref, out_ref, keep_ref, total_ref,
    q_s, kt_s, v_s, m_s, l_s,
):
    count = geo[0]
    cos, sin = cos_ref[...], sin_ref[...]
    unit, _ = unit_rows(tiles(qkv_ref, 0, count).astype(F32))
    q_s[...] = turn(unit * head_ref[:, 0:1] + head_ref[:, 1:2], cos, sin).astype(BF)
    unit, _ = unit_rows(tiles(qkv_ref, 1, count).astype(F32))
    kt_s[...] = turn(unit * head_ref[:, 2:3] + head_ref[:, 3:4], cos, sin).T.astype(BF)
    v_s[...] = tiles(qkv_ref, 2, count)
    block_count, place = key_blocks(geo, ext_ref, pl.program_id(0))
    width = q_s.shape[1]
    m_s[...] = jnp.full_like(m_s, NEG_FILL)
    l_s[...] = jnp.zeros_like(l_s)
    keep_ref[0] = jnp.zeros(keep_ref.shape[1:], F32)

    def key_step(i, carry):
        first = place(i)
        keys = kt_s[pl.ds(first, KEY_BLOCK), :]
        vals = v_s[:, pl.ds(first, KEY_BLOCK)]
        for part in range(width // QUERY_CHUNK):
            cut = slice(part * QUERY_CHUNK, (part + 1) * QUERY_CHUNK)
            scores = jnp.dot(keys, q_s[:, cut], preferred_element_type=F32)
            old = m_s[:, cut]
            new = jnp.maximum(old, jnp.max(scores, axis=0, keepdims=True))
            probs = jnp.exp2((scores - new) * (SCALE * LOG2E))
            factor = jnp.exp2((old - new) * (SCALE * LOG2E))
            m_s[:, cut] = new
            l_s[:, cut] = l_s[:, cut] * factor + jnp.sum(probs, axis=0, keepdims=True)
            keep_ref[0, :, cut] = keep_ref[0, :, cut] * factor + jnp.dot(
                vals, probs.astype(BF), preferred_element_type=F32
            )
        return carry

    lax.fori_loop(0, block_count, key_step, 0)
    total_ref[0] = m_s[...] * (SCALE * LOG2E) + jnp.log2(l_s[...])
    mixed = keep_ref[0] / l_s[...]
    keep_ref[0] = mixed
    low = mixed.astype(BF)
    tile = width // count
    for s in range(count):
        out_ref[s, 0] = low[:, s * tile : (s + 1) * tile]


def attend(ext_jobs, qkv, cos, sin, head, geo):
    count, jobs, _, _, tile = qkv.shape
    width = count * tile
    work = 4 * jobs * width * width * HD
    return pl.pallas_call(
        functools.partial(attend_kernel, geo),
        grid=(jobs,),
        in_specs=[
            pl.BlockSpec(memory_space=pltpu.SMEM),
            pl.BlockSpec((count, 1, 3, HD, tile), lambda j: (0, j, 0, 0, 0)),
            pl.BlockSpec((HD, width), lambda j: (0, 0)),
            pl.BlockSpec((HD, width), lambda j: (0, 0)),
            pl.BlockSpec((HD, 4), lambda j: (0, 0)),
        ],
        out_specs=[
            pl.BlockSpec((count, 1, HD, tile), lambda j: (0, j, 0, 0)),
            pl.BlockSpec((1, HD, width), lambda j: (j, 0, 0)),
            pl.BlockSpec((1, 1, width), lambda j: (j, 0, 0)),
        ],
        out_shape=[
            jax.ShapeDtypeStruct((count, jobs, HD, tile), BF),
            jax.ShapeDtypeStruct((jobs, HD, width), F32),
            jax.ShapeDtypeStruct((jobs, 1, width), F32),
        ],
        scratch_shapes=[
            pltpu.VMEM((HD, width), BF),
            pltpu.VMEM((width, HD), BF),
            pltpu.VMEM((HD, width), BF),
            pltpu.VMEM((1, width), F32),
            pltpu.VMEM((1, width), F32),
        ],
        compiler_params=pltpu.CompilerParams(vmem_limit_bytes=48 * 2**20),
        cost_estimate=pl.CostEstimate(
            flops=3 * work, bytes_accessed=6 * 2**20, transcendentals=jobs * width * width
        ),
    )(ext_jobs, qkv, cos, sin, head)


def attend_back_kernel(
    geo, ext_ref, qkv_ref, dout_ref, keep_ref, total_ref, cos_ref, sin_ref, head_ref,
    grad_ref, head_grad_ref, q_s, k_s, kt_s, vt_s, do_s, delta_s, dq_s, dk_s, dv_s,
):
    count = geo[0]
    cos, sin = cos_ref[...], sin_ref[...]
    unit, _ = unit_rows(tiles(qkv_ref, 0, count).astype(F32))
    q_s[...] = turn(unit * head_ref[:, 0:1] + head_ref[:, 1:2], cos, sin).astype(BF)
    unit, _ = unit_rows(tiles(qkv_ref, 1, count).astype(F32))
    keys = turn(unit * head_ref[:, 2:3] + head_ref[:, 3:4], cos, sin)
    k_s[...] = keys.astype(BF)
    kt_s[...] = keys.T.astype(BF)
    vt_s[...] = tiles(qkv_ref, 2, count).astype(F32).T.astype(BF)
    dout = jnp.concatenate([dout_ref[s, 0] for s in range(count)], axis=1)
    do_s[...] = dout
    delta_s[...] = jnp.sum(dout.astype(F32) * keep_ref[0], axis=0, keepdims=True)
    block_count, place = key_blocks(geo, ext_ref, pl.program_id(0))
    width = q_s.shape[1]
    dq_s[...] = jnp.zeros_like(dq_s)
    dk_s[...] = jnp.zeros_like(dk_s)
    dv_s[...] = jnp.zeros_like(dv_s)

    def key_step(i, carry):
        first = place(i)
        keys_t = kt_s[pl.ds(first, KEY_BLOCK), :]
        vals_t = vt_s[pl.ds(first, KEY_BLOCK), :]
        keys_n = k_s[:, pl.ds(first, KEY_BLOCK)]
        dk = jnp.zeros((HD, KEY_BLOCK), F32)
        dv = jnp.zeros((HD, KEY_BLOCK), F32)
        for part in range(width // QUERY_CHUNK):
            cut = slice(part * QUERY_CHUNK, (part + 1) * QUERY_CHUNK)
            queries = q_s[:, cut]
            douts = do_s[:, cut]
            scores = jnp.dot(keys_t, queries, preferred_element_type=F32)
            probs = jnp.exp2(scores * (SCALE * LOG2E) - total_ref[0, :, cut])
            dprob = jnp.dot(vals_t, douts, preferred_element_type=F32)
            dscore = (probs * (dprob - delta_s[:, cut])).astype(BF)
            dv = dv + lax.dot_general(douts, probs.astype(BF), NT, preferred_element_type=F32)
            dk = dk + lax.dot_general(queries, dscore, NT, preferred_element_type=F32)
            dq_s[:, cut] += jnp.dot(keys_n, dscore, preferred_element_type=F32)
        dk_s[:, pl.ds(first, KEY_BLOCK)] = dk
        dv_s[:, pl.ds(first, KEY_BLOCK)] = dv
        return carry

    lax.fori_loop(0, block_count, key_step, 0)
    tile = width // count

    def lift(part, turned, at):
        unit, rstd = unit_rows(tiles(qkv_ref, part, count).astype(F32))
        dy = turn_back(turned * SCALE, cos, sin)
        head_grad_ref[0, :, at : at + 1] = jnp.sum(dy * unit, axis=1, keepdims=True)
        head_grad_ref[0, :, at + 1 : at + 2] = jnp.sum(dy, axis=1, keepdims=True)
        dunit = dy * head_ref[:, at : at + 1]
        along = jnp.mean(dunit * unit, axis=0, keepdims=True)
        dx = (dunit - jnp.mean(dunit, axis=0, keepdims=True) - unit * along) * rstd
        low = dx.astype(BF)
        for s in range(count):
            grad_ref[s, 0, part] = low[:, s * tile : (s + 1) * tile]

    lift(0, dq_s[...], 0)
    lift(1, dk_s[...], 2)
    low = dv_s[...].astype(BF)
    for s in range(count):
        grad_ref[s, 0, 2] = low[:, s * tile : (s + 1) * tile]


def attend_back(ext_jobs, qkv, dout, keep, total, cos, sin, head, geo):
    count, jobs, _, _, tile = qkv.shape
    width = count * tile
    work = 10 * jobs * width * width * HD
    return pl.pallas_call(
        functools.partial(attend_back_kernel, geo),
        grid=(jobs,),
        in_specs=[
            pl.BlockSpec(memory_space=pltpu.SMEM),
            pl.BlockSpec((count, 1, 3, HD, tile), lambda j: (0, j, 0, 0, 0)),
            pl.BlockSpec((count, 1, HD, tile), lambda j: (0, j, 0, 0)),
            pl.BlockSpec((1, HD, width), lambda j: (j, 0, 0)),
            pl.BlockSpec((1, 1, width), lambda j: (j, 0, 0)),
            pl.BlockSpec((HD, width), lambda j: (0, 0)),
            pl.BlockSpec((HD, width), lambda j: (0, 0)),
            pl.BlockSpec((HD, 4), lambda j: (0, 0)),
        ],
        out_specs=[
            pl.BlockSpec((count, 1, 3, HD, tile), lambda j: (0, j, 0, 0, 0)),
            pl.BlockSpec((1, HD, 4), lambda j: (j, 0, 0)),
        ],
        out_shape=[
            jax.ShapeDtypeStruct((count, jobs, 3, HD, tile), BF),
            jax.ShapeDtypeStruct((jobs, HD, 4), F32),
        ],
        scratch_shapes=[
            pltpu.VMEM((HD, width), BF),
            pltpu.VMEM((HD, width), BF),
            pltpu.VMEM((width, HD), BF),
            pltpu.VMEM((width, HD), BF),
            pltpu.VMEM((HD, width), BF),
            pltpu.VMEM((1, width), F32),
            pltpu.VMEM((HD, width), F32),
            pltpu.VMEM((HD, width), F32),
            pltpu.VMEM((HD, width), F32),
        ],
        compiler_params=pltpu.CompilerParams(vmem_limit_bytes=56 * 2**20),
        cost_estimate=pl.CostEstimate(
            flops=3 * work, bytes_accessed=8 * 2**20, transcendentals=jobs * width * width
        ),
    )(ext_jobs, qkv, dout, keep, total, cos, sin, head)


TN = (((0,), (0,)), ((), ()))
CROSS_HEADS = 2


def text_scores(len_ref, keys, queries, image):
    scores = lax.dot_general(keys, queries, TN, preferred_element_type=F32) * (SCALE * LOG2E)
    place = lax.broadcasted_iota(jnp.int32, scores.shape, 0)
    live = (place < len_ref[image, 0]) | (
        (place >= CLIP) & (place < CLIP + len_ref[image, 1])
    )
    return jnp.where(live, scores, NEG_FILL)


def cross_kernel(images, len_ref, rows_ref, text_ref, cos_ref, sin_ref, head_ref, out_ref, total_ref):
    tile = rows_ref.shape[2] // images
    slots = text_ref.shape[3] // images
    for h in range(CROSS_HEADS):
        unit, _ = unit_rows(rows_ref[h])
        queries = turn(unit * head_ref[:, 0:1] + head_ref[:, 1:2], cos_ref[...], sin_ref[...])
        queries = queries.astype(BF)
        for i in range(images):
            own, slot = slice(i * tile, (i + 1) * tile), slice(i * slots, (i + 1) * slots)
            scores = text_scores(len_ref, text_ref[0, h, :, slot], queries[:, own], i)
            top = jnp.max(scores, axis=0, keepdims=True)
            probs = jnp.exp2(scores - top)
            weight = jnp.sum(probs, axis=0, keepdims=True)
            low = (probs / weight).astype(BF)
            mixed = jnp.dot(text_ref[1, h, :, slot], low, preferred_element_type=F32)
            out_ref[h, :, own] = mixed.astype(BF)
            total_ref[h, :, own] = top + jnp.log2(weight)


def cross_back_kernel(
    images, len_ref, rows_ref, text_ref, dout_ref, total_ref, cos_ref, sin_ref, head_ref,
    grad_ref, text_grad_ref, head_grad_ref,
):
    tile = rows_ref.shape[2] // images
    slots = text_ref.shape[3] // images
    cos, sin = cos_ref[...], sin_ref[...]
    gain_grad = jnp.zeros((HD, 1), F32)
    shift_grad = jnp.zeros((HD, 1), F32)
    for h in range(CROSS_HEADS):
        unit, rstd = unit_rows(rows_ref[h])
        queries = turn(unit * head_ref[:, 0:1] + head_ref[:, 1:2], cos, sin).astype(BF)
        turned = []
        for i in range(images):
            own, slot = slice(i * tile, (i + 1) * tile), slice(i * slots, (i + 1) * slots)
            keys = text_ref[0, h, :, slot]
            douts = dout_ref[h, :, own]
            scores = text_scores(len_ref, keys, queries[:, own], i)
            probs = jnp.exp2(scores - total_ref[h, :, own])
            dprob = lax.dot_general(
                text_ref[1, h, :, slot], douts, TN, preferred_element_type=F32
            )
            delta = jnp.sum(probs * dprob, axis=0, keepdims=True)
            dscore = (probs * (dprob - delta)).astype(BF)
            low = probs.astype(BF)
            dkeys = lax.dot_general(queries[:, own], dscore, NT, preferred_element_type=F32)
            text_grad_ref[0, h, :, slot] = (dkeys * SCALE).astype(BF)
            text_grad_ref[1, h, :, slot] = lax.dot_general(
                douts, low, NT, preferred_element_type=F32
            ).astype(BF)
            turned.append(jnp.dot(keys, dscore, preferred_element_type=F32))
        dy = turn_back(jnp.concatenate(turned, axis=1) * SCALE, cos, sin)
        gain_grad += jnp.sum(dy * unit, axis=1, keepdims=True)
        shift_grad += jnp.sum(dy, axis=1, keepdims=True)
        dunit = dy * head_ref[:, 0:1]
        along_unit = jnp.mean(dunit * unit, axis=0, keepdims=True)
        dx = (dunit - jnp.mean(dunit, axis=0, keepdims=True) - unit * along_unit) * rstd
        grad_ref[h] = dx.astype(BF)
    head_grad_ref[0, :, 0:1] = gain_grad
    head_grad_ref[0, :, 1:2] = shift_grad


def cross_specs(width, slots):
    return dict(
        smem=pl.BlockSpec(memory_space=pltpu.SMEM),
        rows=pl.BlockSpec((CROSS_HEADS, HD, width), lambda h: (h, 0, 0)),
        text=pl.BlockSpec((2, CROSS_HEADS, HD, slots), lambda h: (0, h, 0, 0)),
        table=pl.BlockSpec((HD, width), lambda h: (0, 0)),
        head=pl.BlockSpec((HD, 2), lambda h: (0, 0)),
        total=pl.BlockSpec((CROSS_HEADS, 1, width), lambda h: (h, 0, 0)),
        head_grad=pl.BlockSpec((1, HD, 2), lambda h: (h, 0, 0)),
    )


def cross_attend(lengths, rows, text, cos, sin, head):
    heads, _, width = rows.shape
    slots = text.shape[3]
    sp = cross_specs(width, slots)
    return pl.pallas_call(
        functools.partial(cross_kernel, lengths.shape[0]),
        grid=(heads // CROSS_HEADS,),
        in_specs=[sp["smem"], sp["rows"], sp["text"], sp["table"], sp["table"], sp["head"]],
        out_specs=[sp["rows"], sp["total"]],
        out_shape=[
            jax.ShapeDtypeStruct((heads, HD, width), BF),
            jax.ShapeDtypeStruct((heads, 1, width), F32),
        ],
        compiler_params=pltpu.CompilerParams(vmem_limit_bytes=32 * 2**20),
        cost_estimate=pl.CostEstimate(
            flops=2**32, bytes_accessed=10 * 2**20, transcendentals=heads * width * slots
        ),
    )(lengths, rows, text, cos, sin, head)


def cross_attend_back(lengths, rows, text, dout, total, cos, sin, head):
    heads, _, width = rows.shape
    slots = text.shape[3]
    sp = cross_specs(width, slots)
    return pl.pallas_call(
        functools.partial(cross_back_kernel, lengths.shape[0]),
        grid=(heads // CROSS_HEADS,),
        in_specs=[
            sp["smem"], sp["rows"], sp["text"], sp["rows"], sp["total"], sp["table"], sp["table"],
            sp["head"],
        ],
        out_specs=[sp["rows"], sp["text"], sp["head_grad"]],
        out_shape=[
            jax.ShapeDtypeStruct((heads, HD, width), BF),
            jax.ShapeDtypeStruct((2, heads, HD, slots), BF),
            jax.ShapeDtypeStruct((heads // CROSS_HEADS, HD, 2), F32),
        ],
        compiler_params=pltpu.CompilerParams(vmem_limit_bytes=32 * 2**20),
        cost_estimate=pl.CostEstimate(
            flops=2**33, bytes_accessed=16 * 2**20, transcendentals=heads * width * slots
        ),
    )(lengths, rows, text, dout, total, cos, sin, head)


MESH = pl.DeviceIdType.MESH
LAG = 3


class Kind(NamedTuple):
    width: int
    height: int
    chunks: int
    first_step: int
    over_images: bool


def sum_plan(sizes, kind):
    groups, row_count, cols = sizes
    count, height = row_count * cols // 2, kind.height
    image_bits = [("img", 1 << i) for i in range(groups.bit_length() - 1)]
    row_bits = [("row", 1 << i) for i in range(1, row_count.bit_length() - 1)]
    col_bits = [("col", 1 << i) for i in range(cols.bit_length() - 1)]
    plan = []
    for axis, bit in (image_bits if kind.over_images else []) + row_bits + col_bits:
        if axis == "img":
            height //= 2
        else:
            count //= 2
        plan.append((axis, bit, count, height))
    return plan


def sum_kernel(sizes, kinds, *refs):
    groups, row_count, cols = sizes
    number = len(kinds)
    grads_refs, out_refs, scratch = refs[:number], refs[number : 2 * number], refs[2 * number :]
    first_count = row_count * cols // 2
    places = {axis: lax.axis_index(axis) for axis in ("img", "row", "col")}
    plans = [sum_plan(sizes, kind) for kind in kinds]
    image_stages = groups.bit_length() - 1
    held, own, sems = [], [], []
    at = 0
    for plan in plans:
        held.append(scratch[at : at + len(plan) + 1])
        own.append(scratch[at + len(plan) + 1])
        sems.append(scratch[at + len(plan) + 2 : at + len(plan) + 8])
        at += len(plan) + 8
    core = places["row"] % 2

    def device_of(place):
        return tuple(place[name] for name in ("img", "row", "col"))

    def partner(axis, bit):
        place = dict(places)
        part = place[axis] // bit % 2
        place[axis] = place[axis] + bit - 2 * bit * part
        return device_of(place)

    def other_images():
        for i in range(1, groups):
            place = dict(places)
            place["img"] = lax.rem(places["img"] + i, groups)
            yield i, device_of(place)

    def bit_of(axis, bit):
        return places[axis] // bit % 2

    def chunk_rows(k, chunk):
        return pl.multiple_of(chunk * kinds[k].height, 16)

    def first_copies(k, chunk):
        rows = pl.ds(chunk_rows(k, chunk), kinds[k].height)
        for i in range(row_count // 2):
            shards = pl.ds((2 * i + 1 - core) * cols, cols)
            yield pltpu.make_async_remote_copy(
                src_ref=grads_refs[k].at[shards, rows],
                dst_ref=held[k][0].at[chunk, pl.ds(i * cols, cols)],
                send_sem=sems[k][0].at[0, chunk],
                recv_sem=sems[k][1].at[0, chunk],
                device_id=partner("row", 1),
                device_id_type=MESH,
            )

    def own_copies(k, chunk):
        rows = pl.ds(chunk_rows(k, chunk), kinds[k].height)
        for i in range(row_count // 2):
            shards = pl.ds((2 * i + core) * cols, cols)
            yield pltpu.make_async_copy(
                grads_refs[k].at[shards, rows],
                own[k].at[lax.rem(chunk, 2), pl.ds(i * cols, cols)],
                sems[k][4].at[lax.rem(chunk, 2)],
            )

    def split(k, stage):
        axis, bit, count, rows = plans[k][stage]
        part = bit_of(axis, bit)
        if axis == "img":
            give = pl.ds(pl.multiple_of((1 - part) * rows, 16), rows)
            keep = pl.ds(pl.multiple_of(part * rows, 16), rows)
            return [((pl.ds(0, count), give), pl.ds(0, count))], lambda i: (i, keep)
        every = pl.ds(0, rows)
        if axis == "row":
            give = pl.ds((1 - part) * count, count)
            return [((give, every), pl.ds(0, count))], lambda i: (part * count + i, every)
        return (
            [((pl.ds(2 * i + 1 - part, 1), every), pl.ds(i, 1)) for i in range(count)],
            lambda i: (2 * i + part, every),
        )

    def stage_copies(k, stage, chunk):
        axis, bit, _, _ = plans[k][stage]
        for (shards, lines), target in split(k, stage)[0]:
            yield pltpu.make_async_remote_copy(
                src_ref=held[k][stage].at[chunk, shards, lines],
                dst_ref=held[k][stage + 1].at[chunk, target],
                send_sem=sems[k][0].at[stage + 1, chunk],
                recv_sem=sems[k][1].at[stage + 1, chunk],
                device_id=partner(axis, bit),
                device_id_type=MESH,
            )

    def whole(k, stage, chunk):
        buffer = held[k][stage].at[chunk]
        return pltpu.make_async_remote_copy(
            src_ref=buffer,
            dst_ref=buffer,
            send_sem=sems[k][0].at[stage, chunk],
            recv_sem=sems[k][1].at[stage, chunk],
            device_id=partner("row", 1),
            device_id_type=MESH,
        )

    def home(k, chunk):
        rows = plans[k][-1][3]
        if not kinds[k].over_images:
            return out_refs[k].at[places["img"], pl.ds(chunk_rows(k, chunk), rows)]
        place = 0
        for i in range(image_stages):
            place = place + bit_of("img", 1 << i) * (1 << (image_stages - 1 - i))
        return out_refs[k].at[pl.ds(pl.multiple_of(chunk_rows(k, chunk) + place * rows, 16), rows)]

    def spread_copies(k, chunk):
        for i, other in other_images():
            yield pltpu.make_async_remote_copy(
                src_ref=held[k][-1].at[chunk, 0],
                dst_ref=home(k, chunk),
                send_sem=sems[k][2].at[i, chunk],
                recv_sem=sems[k][3].at[i, chunk],
                device_id=other,
                device_id_type=MESH,
            )

    def home_copy(k, chunk):
        return pltpu.make_async_copy(
            held[k][-1].at[chunk, 0], home(k, chunk), sems[k][5].at[chunk]
        )

    def start(copies):
        for copy in copies:
            copy.start()

    def begin(k, chunk):
        start(first_copies(k, chunk))
        start(own_copies(k, chunk))

    barrier = pltpu.get_barrier_semaphore()
    near = [partner("row", 1)] + [partner(a, b) for a, b, _, _ in plans[0] if a != "img"]
    near += [other for _, other in other_images()]
    for other in near:
        pl.semaphore_signal(barrier, inc=1, device_id=other, device_id_type=MESH)
    pl.semaphore_wait(barrier, len(near))

    for k in range(number):
        begin(k, 0)

    def advance(k, stage, chunk):
        if stage == 0:

            @pl.when(chunk + 1 < kinds[k].chunks)
            def _():
                begin(k, chunk + 1)

        buffer = held[k][stage]
        whole(k, stage, chunk).wait_recv()
        if stage == 0:
            count = first_count
            for copy in own_copies(k, chunk):
                copy.wait()

            def mine(i):
                return own[k][lax.rem(chunk, 2), i]
        else:
            count = plans[k][stage - 1][2]
            kept = split(k, stage - 1)[1]

            def mine(i):
                shard, lines = kept(i)
                return held[k][stage - 1][chunk, shard, lines]

        def add(i, carry):
            both = buffer[chunk, i].astype(F32) + mine(i).astype(F32)
            buffer[chunk, i] = both.astype(BF)
            return carry

        lax.fori_loop(0, count, add, 0)
        if stage < len(plans[k]):
            start(stage_copies(k, stage, chunk))
        else:
            start(spread_copies(k, chunk))
            home_copy(k, chunk).start()

    def time_step(t, carry):
        for stage in range(max(len(plan) for plan in plans), -1, -1):
            for k, kind in enumerate(kinds):
                if stage <= len(plans[k]):
                    chunk = t - LAG * stage - kind.first_step

                    @pl.when(jnp.logical_and(chunk >= 0, chunk < kind.chunks))
                    def _(k=k, stage=stage, chunk=chunk):
                        advance(k, stage, chunk)

        return carry

    last = max(k.first_step + k.chunks + LAG * len(plan) for k, plan in zip(kinds, plans))
    lax.fori_loop(0, last, time_step, 0)

    for k, kind in enumerate(kinds):

        def drain(chunk, carry, k=k):
            for stage in range(len(plans[k]) + 1):
                whole(k, stage, chunk).wait_send()
            for copy in spread_copies(k, chunk):
                copy.wait()
            home_copy(k, chunk).wait()
            return carry

        lax.fori_loop(0, kind.chunks, drain, 0)


def sum_everywhere(projections, down, up, sizes):
    groups, row_count, cols = sizes
    first_count = row_count * cols // 2
    kinds = [Kind(D, 16 * groups, projections.shape[1] // (16 * groups), 0, True)]
    kinds.append(Kind(up.shape[2], 16, up.shape[1] // 16, 0, False))
    kinds.append(Kind(D, 16, down.shape[1] // 16, kinds[1].chunks, False))
    scratch = []
    for kind in kinds:
        plan = sum_plan(sizes, kind)
        shapes = [(first_count, kind.height)] + [(c, h) for _, _, c, h in plan]
        scratch += [pltpu.VMEM((kind.chunks, c, h, kind.width), BF) for c, h in shapes]
        scratch.append(pltpu.VMEM((2, first_count, kind.height, kind.width), BF))
        stage_sems = pltpu.SemaphoreType.DMA((len(plan) + 1, kind.chunks))
        spread_sems = pltpu.SemaphoreType.DMA((groups, kind.chunks))
        scratch += [
            stage_sems, stage_sems, spread_sems, spread_sems,
            pltpu.SemaphoreType.DMA((2,)), pltpu.SemaphoreType.DMA((kind.chunks,)),
        ]
    space = pl.BlockSpec(memory_space=pl.ANY)
    return pl.pallas_call(
        functools.partial(sum_kernel, sizes, kinds),
        out_shape=[
            jax.ShapeDtypeStruct(projections.shape[1:], BF),
            jax.ShapeDtypeStruct((groups,) + up.shape[1:], BF),
            jax.ShapeDtypeStruct((groups,) + down.shape[1:], BF),
        ],
        in_specs=[space] * 3,
        out_specs=[space] * 3,
        scratch_shapes=scratch,
        compiler_params=pltpu.CompilerParams(
            collective_id=1, has_side_effects=True, vmem_limit_bytes=58 * 2**20
        ),
        cost_estimate=pl.CostEstimate(flops=2**28, bytes_accessed=2**28, transcendentals=0),
    )(projections, up, down)


def all_to_all(values):
    return lax.all_to_all(values, GROUP, split_axis=0, concat_axis=0, tiled=True)


def body(
    latents, skip, temb, text, text_len, extent, embed_weight, skip_weight, shift_weight,
    qkv_weight, out_weight, cross_query, cross_keys, cross_out, up_weight, down_weight,
    final_weight, norm_gain, norm_shift, skip_gain, skip_shift, head_gain, head_shift,
    front_biases, all_biases, cross_bias, cotangent,
):
    img_count, tile_rows, tile_cols, patch_vals = latents.shape
    tokens = tile_rows * tile_cols
    near_vals = 9 * patch_vals
    row_count = lax.axis_size("row")
    col_count = lax.axis_size("col")
    count = row_count * col_count
    groups = lax.axis_size("img")
    jobs = img_count * HEADS // count
    row_index = lax.axis_index("row")
    col_index = lax.axis_index("col")
    group_index = lax.axis_index("img")
    device = row_index * col_count + col_index
    shard = D // count
    hid_shard = FF // count
    hid_part = hid_shard // groups

    small_widths = (
        norm_gain.size, norm_shift.size, skip_gain.size, skip_shift.size,
        head_gain.size, head_shift.size, front_biases.size, all_biases.size,
    )
    small = jnp.concatenate(
        [
            embed_weight.T.reshape(-1), final_weight.reshape(-1), norm_gain.reshape(-1),
            norm_shift.reshape(-1), skip_gain, skip_shift, head_gain, head_shift,
            front_biases, all_biases,
        ]
    )
    small_len = small.size
    padded_len = -(-(small_len + img_count * D) // 2048) * 2048
    time_act = jax.nn.silu(temb.astype(F32)).astype(BF)
    time_own = lax.dynamic_slice_in_dim(time_act, device * shard, shard, 1)
    shift_share = matmul(time_own, shift_weight).astype(BF).reshape(-1)
    small = jnp.pad(jnp.concatenate([small, shift_share]), (0, padded_len - small_len - shift_share.size))
    small_all = all_to_all(jnp.broadcast_to(small.reshape(1, -1, 128), (count, padded_len // 128, 128)))
    small_all = small_all.reshape(count, padded_len)
    def beside(values, parts):
        return jnp.concatenate(jnp.split(values, parts, axis=0), axis=1)

    def below(values, parts):
        width = values.shape[1] // parts
        blocks = [values[:, i * width : (i + 1) * width] for i in range(parts)]
        return jnp.stack([b.reshape(count, -1, width) for b in blocks], axis=1).reshape(-1, width)

    first_all = lax.all_gather(
        jnp.concatenate([beside(skip_weight, 2), qkv_weight], axis=1), GROUP, axis=0, tiled=True
    )
    skip_full = below(first_all[:, : 2 * D], 2)
    qkv_full = first_all[:, 2 * D :]
    folds = hid_part // shard
    fold_rows = hid_part // folds
    up_part = lax.dynamic_index_in_dim(
        up_weight.reshape(shard, count, groups, hid_part), group_index, 2, keepdims=False
    ).reshape(shard, count * hid_part)
    down_part = lax.dynamic_index_in_dim(
        down_weight.reshape(groups, hid_part, D), group_index, 0, keepdims=False
    )
    third = jnp.concatenate(
        [jnp.pad(up_part, ((0, fold_rows - shard), (0, 0))), beside(down_part, folds)], axis=1
    )

    wide = shard * near_vals
    embed_t = small_all[:, :wide].reshape(D, near_vals)
    final_full = small_all[:, wide : 2 * wide].reshape(D, near_vals)
    vectors = cuts(small_all[:, 2 * wide : small_len].astype(F32), small_widths)
    gain_rows = jnp.transpose(vectors[0].reshape(count, 3, shard), (1, 0, 2)).reshape(3, D)
    offset_rows = jnp.transpose(vectors[1].reshape(count, 3, shard), (1, 0, 2)).reshape(3, D)
    skip_gains, skip_offsets = vectors[2].reshape(-1), vectors[3].reshape(-1)
    head_gains, head_offsets = vectors[4].reshape(4, HD), vectors[5].reshape(4, HD)
    bias_embed, bias_skip, bias_shift, bias_qkv = cuts(vectors[6].reshape(-1), (D, D, D, 3 * D))
    bias_out, bias_cross_q, bias_cross_o, bias_up, bias_down = cuts(
        vectors[7].reshape(-1), (D, D, D, FF, D)
    )
    bias_up_part = lax.dynamic_index_in_dim(
        bias_up.reshape(count, groups, hid_part), group_index, 1, keepdims=False
    ).reshape(-1)

    local_rows = row_index * tile_rows + jnp.arange(tile_rows, dtype=jnp.int32)
    local_cols = col_index * tile_cols + jnp.arange(tile_cols, dtype=jnp.int32)
    inside = (
        (local_rows[None, :, None] < extent[:, 0, None, None])
        & (local_cols[None, None, :] < extent[:, 1, None, None])
    ).astype(F32)
    token_inside = inside.reshape(img_count, tokens, 1)
    own_angle = angles_of(
        jnp.tile(jnp.repeat(local_rows, tile_cols), img_count),
        jnp.tile(jnp.tile(local_cols, tile_rows), img_count),
    )
    own_cos, own_sin = jnp.cos(own_angle), jnp.sin(own_angle)
    every = np.arange(count * tokens)
    every_row = every // tokens // col_count * tile_rows + every % tokens // tile_cols
    every_col = every // tokens % col_count * tile_cols + every % tile_cols
    every_angle = angles_of(jnp.asarray(every_row), jnp.asarray(every_col))
    every_cos, every_sin = jnp.cos(every_angle), jnp.sin(every_angle)
    job_images = (device * jobs + jnp.arange(jobs, dtype=jnp.int32)) % img_count
    ext_jobs = jnp.take(extent, job_images, axis=0)
    geo = (count, tile_rows, tile_cols, col_count, KEY_BLOCK // tokens)

    def gelu_tanh(values):
        return jax.nn.gelu(values, approximate=True)

    text_width = cross_keys.shape[1]
    text_count = -(-text.shape[1] // 128) * 128
    text_wide = jnp.pad(text, ((0, 0), (0, text_count - text.shape[1]), (0, 0)))
    is_key = device * text_width + jnp.arange(text_width, dtype=jnp.int32) < D

    def text_norm(values, scales, offsets):
        per_head = values.reshape(text_width // HD, HD, -1)
        centre = per_head - jnp.mean(per_head, axis=1, keepdims=True)
        spread = jnp.mean(centre * centre, axis=1, keepdims=True)
        unit = centre * lax.rsqrt(spread + NORM_EPS) * scales[:, None] + offsets[:, None]
        return jnp.where(is_key[:, None], unit.reshape(values.shape), values)

    text_part = dot(cross_keys, text_wide, (0,), (2,)).reshape(text_width, -1)
    text_part = text_part + cross_bias.astype(F32)[:, None]
    text_normed, text_pull = jax.vjp(text_norm, text_part, head_gains[3], head_offsets[3])
    moves = Moves()
    second_all = lax.all_gather(
        jnp.concatenate(
            [out_weight, cross_query, cross_out, beside(text_normed.astype(BF), 2)], axis=1
        ),
        GROUP,
        axis=0,
        tiled=True,
    )
    out_full, cross_q_full, cross_o_full = [second_all[:, i * D : (i + 1) * D] for i in range(3)]
    text_both = below(second_all[:, 3 * D :], 2).reshape(2, HEADS, HD, img_count * text_count)
    third_all = lax.all_gather(third, GROUP, axis=0, tiled=True)
    third_rows = third_all.reshape(count, fold_rows, -1)
    up_full = third_rows[:, :shard, : count * hid_part].reshape(D, count * hid_part)
    down_full = below(third_all[:, count * hid_part :], folds)
    shift_sums = small_all[:, small_len : small_len + img_count * D].astype(F32)
    shift_rows = jnp.sum(shift_sums, axis=0).reshape(img_count, D) + bias_shift

    lat_masked = (latents * inside[..., None]).astype(BF)
    cot_masked = (cotangent * inside[..., None]).astype(BF)
    rims = with_halo(
        jnp.concatenate([lat_masked, cot_masked], axis=-1), (("row", 1), ("col", 2)), 1
    )
    rims = rims.astype(F32)
    near = gather_near(rims[..., :patch_vals], tile_rows, tile_cols)
    near = near.reshape(img_count, tokens, near_vals).astype(BF)
    cot_near = gather_near(rims[..., patch_vals:], tile_rows, tile_cols)
    cot_near = cot_near.reshape(img_count, tokens, near_vals)
    embedded = matmul_back(near, embed_t) + bias_embed
    joined_full = jnp.concatenate(
        [embedded, skip.reshape(img_count, tokens, D).astype(F32)], axis=-1
    )
    skip_normed, skip_norm_pull = jax.vjp(layer_norm, joined_full, skip_gains, skip_offsets)
    skip_in = skip_normed.astype(BF)
    resid_in = matmul(skip_in, skip_full) + bias_skip
    self_norm, self_norm_pull = jax.vjp(layer_norm, resid_in, gain_rows[0], offset_rows[0])
    normed = (self_norm + shift_rows[:, None, :]).astype(BF)

    qkv_t = dot(qkv_full, normed, (0,), (2,)) + bias_qkv[:, None, None]
    qkv_t = qkv_t.astype(BF).reshape(3, HEADS, HD, img_count, tokens)
    qkv_jobs = all_to_all(
        jnp.transpose(qkv_t, (1, 3, 0, 2, 4)).reshape(count, jobs, 3, HD, tokens)
    )
    head_cols = jnp.stack([head_gains[0], head_offsets[0], head_gains[1], head_offsets[1]], axis=1)
    mixed_jobs, keep, total = attend(ext_jobs, qkv_jobs, every_cos, every_sin, head_cols, geo)
    mixed = all_to_all(mixed_jobs).reshape(HEADS, img_count, HD, tokens)
    attended_t = jnp.transpose(mixed, (1, 0, 2, 3)).reshape(img_count, D, tokens)
    resid_self = resid_in + dot(attended_t, out_full, (1,), (0,)) + bias_out

    cross_norm, cross_norm_pull = jax.vjp(layer_norm, resid_self, gain_rows[1], offset_rows[1])
    cross_in = cross_norm.astype(BF)
    all_tokens = img_count * tokens
    cross_rows = dot(cross_q_full, cross_in.reshape(all_tokens, D), (0,), (1,))
    cross_rows = (cross_rows + bias_cross_q[:, None]).reshape(HEADS, HD, all_tokens)
    cross_cols = jnp.stack([head_gains[2], head_offsets[2]], axis=1)
    cross_mixed, cross_total = cross_attend(
        text_len, cross_rows, text_both, own_cos, own_sin, cross_cols
    )
    cross_low = cross_mixed.reshape(D, all_tokens)
    cross_out_rows = dot(cross_low, cross_o_full, (0,), (0,)).reshape(img_count, tokens, D)
    resid_cross = resid_self + cross_out_rows + bias_cross_o

    mlp_norm, mlp_norm_pull = jax.vjp(layer_norm, resid_cross, gain_rows[2], offset_rows[2])
    mlp_in = images_gather(mlp_norm.astype(BF))
    hidden = matmul(mlp_in, up_full) + bias_up_part
    gelu_out, gelu_pull = jax.vjp(gelu_tanh, hidden)
    activated = gelu_out.astype(BF)
    resid_out = resid_cross + images_scatter(matmul(activated, down_full)) + bias_down
    resid_low = resid_out.astype(BF)
    emitted = matmul(resid_low, final_full) * token_inside
    emit_rim = with_halo(
        emitted.reshape(img_count, tile_rows, tile_cols, near_vals), (("row", 1), ("col", 2)), 1
    )
    out_latents = spread_near(emit_rim, tile_rows, tile_cols, patch_vals) * inside[..., None]

    lead = (0, 1)
    by_row = row_first()
    grad_emitted = (cot_near * token_inside).astype(BF)
    grad_final = weight_grad(resid_low, grad_emitted)
    grad_resid_out = matmul_back(grad_emitted, final_full)
    grad_down_low = grad_resid_out.astype(BF)
    bias_down_grad = column_sum(grad_down_low)
    grad_down_rows = images_gather(grad_down_low)
    every_lead = (0, 1, 2)
    whole_down = dot(activated, grad_down_rows, every_lead, every_lead)
    grad_hidden = gelu_pull(matmul_back(grad_down_rows, down_full))[0].astype(BF)
    whole_up = dot(mlp_in, grad_hidden, every_lead, every_lead)
    bias_up_grad = column_sum(grad_hidden)
    grad_mlp_in = images_scatter(matmul_back(grad_hidden, up_full))
    grad_from_mlp, gain_mlp_grad, shift_mlp_grad = mlp_norm_pull(grad_mlp_in)
    grad_resid_cross = grad_resid_out + grad_from_mlp

    grad_cross_low = grad_resid_cross.astype(BF)
    grad_cross_flat = grad_cross_low.reshape(all_tokens, D)
    whole_grads = {"cross_o": dot(cross_low, grad_cross_flat, (1,), (0,))}
    bias_cross_o_grad = column_sum(grad_cross_low)
    grad_cross_mixed = dot(cross_o_full, grad_cross_flat, (1,), (1,)).astype(BF)
    grad_cross_rows, grad_text, cross_head_grads = cross_attend_back(
        text_len, cross_rows, text_both, grad_cross_mixed.reshape(HEADS, HD, all_tokens),
        cross_total, own_cos, own_sin, cross_cols,
    )
    cross_head_grads = jnp.sum(cross_head_grads, axis=0)
    grad_cross_rows = grad_cross_rows.reshape(D, all_tokens)
    whole_grads["cross_q"] = dot(cross_in.reshape(all_tokens, D), grad_cross_rows, (0,), (1,))
    bias_cross_q_grad = jnp.sum(grad_cross_rows.astype(F32), axis=1)
    grad_cross_in = dot(grad_cross_rows, cross_q_full, (0,), (1,))
    grad_from_cross, gain_cross_grad, shift_cross_grad = cross_norm_pull(
        grad_cross_in.reshape(img_count, tokens, D)
    )
    grad_resid_self = grad_resid_cross + grad_from_cross

    grad_out_rows = grad_resid_self.astype(BF)
    whole_grads["out"] = dot(attended_t, grad_out_rows, (0, 2), lead)
    bias_out_grad = column_sum(grad_out_rows)
    grad_attended = dot(out_full, grad_out_rows, (1,), (2,)).astype(BF)
    grad_attended = jnp.transpose(
        grad_attended.reshape(HEADS, HD, img_count, tokens), (0, 2, 1, 3)
    )
    grad_mixed_jobs = all_to_all(grad_attended.reshape(count, jobs, HD, tokens))
    grad_jobs, head_grads = attend_back(
        ext_jobs, qkv_jobs, grad_mixed_jobs, keep, total, every_cos, every_sin, head_cols, geo
    )
    grad_qkv_t = all_to_all(grad_jobs).reshape(HEADS, img_count, 3, HD, tokens)
    grad_qkv_t = moves.begin(
        grad_qkv_t, text=offload_sum(alone, grad_text.reshape(2 * D, img_count * text_count))
    )
    grad_qkv_t = jnp.transpose(grad_qkv_t, (2, 0, 3, 1, 4)).reshape(3 * D, img_count, tokens)
    head_grads = jnp.sum(head_grads, axis=0)

    for i, name in enumerate(("query", "key", "value")):
        whole_grads[name] = dot(normed, grad_qkv_t[i * D : (i + 1) * D], (0, 1), (1, 2))
    bias_qkv_grad = jnp.sum(grad_qkv_t.astype(F32), axis=(1, 2))
    grad_normed = dot(grad_qkv_t, qkv_full, (0,), (1,))
    grad_shift_rows = jnp.sum(grad_normed, axis=1)
    bias_shift_grad = jnp.sum(grad_shift_rows, axis=0)
    grad_from_self, gain_self_grad, shift_self_grad = self_norm_pull(grad_normed)
    grad_resid_in = grad_resid_self + grad_from_self
    grad_merged = grad_resid_in.astype(BF)
    whole_grads["skip"] = weight_grad(skip_in, grad_merged)
    bias_skip_grad = column_sum(grad_merged)
    grad_skip_normed = matmul_back(grad_merged, skip_full)
    grad_joined, skip_gain_grad, skip_shift_grad = skip_norm_pull(grad_skip_normed)
    grad_skip = grad_joined[..., D:].reshape(img_count, tile_rows, tile_cols, D)
    grad_embedded = grad_joined[..., :D].astype(BF)
    grad_embed_t = weight_grad(grad_embedded, near)
    bias_embed_grad = column_sum(grad_embedded)
    grad_near = matmul(grad_embedded, embed_t).reshape(
        img_count, tile_rows, tile_cols, near_vals
    )
    near_rim = with_halo(grad_near, (("row", 1), ("col", 2)), 1)
    grad_latents = spread_near(near_rim, tile_rows, tile_cols, patch_vals) * inside[..., None]

    moves.finish(*list(moves.running))
    shards = moves.done
    names = ("query", "key", "value", "skip", "out", "cross_q", "cross_o")
    packed = [whole_grads[name].astype(BF).reshape(count, -1, D) for name in names]
    packed_rows = sum(part.shape[1] for part in packed)
    fill = -packed_rows % (16 * groups)
    packed = jnp.pad(jnp.concatenate(packed, axis=1), ((0, 0), (0, fill), (0, 0)))
    up_rows = jnp.pad(
        whole_up.astype(BF).reshape(count, shard, -1), ((0, 0), (0, -shard % 16), (0, 0))
    )
    down_rows = whole_down.astype(BF).reshape(count, hid_part, D)
    summed, up_sums, down_sums = sum_everywhere(
        packed, down_rows, up_rows, (groups, row_count, col_count)
    )
    summed = summed.astype(F32)
    total_of, at = {}, 0
    for name in names:
        rows = whole_grads[name].shape[0] // count
        total_of[name] = summed[at : at + rows]
        at += rows
    grad_text_lin, head_gain_ck_grad, head_shift_ck_grad = text_pull(shards["text"])
    grad_text_low = grad_text_lin.astype(BF)
    grad_cross_keys = images_sum(
        dot(
            text_wide, grad_text_low.reshape(text_width, img_count, text_count), (0, 1), (1, 2)
        ),
        BF,
    )
    grad_cross_bias = images_sum(jnp.sum(grad_text_low.astype(F32), axis=1), F32)

    def by_device(vector):
        return vector.reshape(count, -1)

    def rows_by_device(rows):
        return jnp.transpose(rows.reshape(3, count, shard), (1, 0, 2)).reshape(count, -1)

    bias_up_all = jnp.where(
        (jnp.arange(groups) == group_index)[None, :, None],
        bias_up_grad.reshape(count, 1, hid_part),
        0.0,
    ).reshape(-1)
    small_grads = jnp.concatenate(
        [
            by_device(grad_embed_t),
            by_device(grad_final),
            rows_by_device(jnp.stack([gain_self_grad, gain_cross_grad, gain_mlp_grad])),
            rows_by_device(jnp.stack([shift_self_grad, shift_cross_grad, shift_mlp_grad])),
            by_device(skip_gain_grad),
            by_device(skip_shift_grad),
            by_device(
                jnp.concatenate(
                    [head_grads[:, 0], head_grads[:, 2], cross_head_grads[:, 0], head_gain_ck_grad]
                )
            ),
            by_device(
                jnp.concatenate(
                    [head_grads[:, 1], head_grads[:, 3], cross_head_grads[:, 1], head_shift_ck_grad]
                )
            ),
            by_device(
                jnp.concatenate([bias_embed_grad, bias_skip_grad, bias_shift_grad, bias_qkv_grad])
            ),
            by_device(
                jnp.concatenate(
                    [
                        bias_out_grad, bias_cross_q_grad, bias_cross_o_grad, bias_up_all,
                        bias_down_grad,
                    ]
                )
            ),
        ],
        axis=1,
    )
    shift_share = jnp.broadcast_to(grad_shift_rows.reshape(1, -1), (count, img_count * D))
    small_grads = jnp.concatenate([small_grads, shift_share], axis=1).astype(BF)
    small_grads = jnp.pad(small_grads, ((0, 0), (0, padded_len - small_grads.shape[1])))
    small_got = all_to_all(small_grads.reshape(count, -1, 128)).astype(F32)
    small_got = jnp.sum(small_got, axis=0).reshape(-1)
    small_sum = images_sum(small_got[:small_len], F32)
    total_parts = cuts(small_sum, (wide, wide) + small_widths)
    grad_shift = lax.dot_general(
        time_own.astype(F32),
        small_got[small_len : small_len + img_count * D].reshape(img_count, D),
        (((0,), (0,)), ((), ())),
        precision=lax.Precision.HIGHEST,
    )

    total_up = jnp.transpose(
        up_sums[:, :shard].reshape(groups, shard, count, hid_part), (1, 2, 0, 3)
    ).reshape(shard, FF)
    total_down = down_sums.reshape(hid_shard, D)
    return (
        out_latents,
        grad_latents,
        grad_skip,
        total_parts[0].reshape(shard, near_vals).T,
        total_of["skip"],
        images_sum(grad_shift, F32),
        jnp.concatenate([total_of[name] for name in ("query", "key", "value")], axis=1),
        total_of["out"],
        total_of["cross_q"],
        grad_cross_keys,
        total_of["cross_o"],
        total_up.astype(F32),
        total_down.astype(F32),
        total_parts[1].reshape(shard, near_vals),
        total_parts[2].reshape(3, shard),
        total_parts[3].reshape(3, shard),
        total_parts[4],
        total_parts[5],
        total_parts[6],
        total_parts[7],
        total_parts[8],
        total_parts[9],
        grad_cross_bias,
    )


def solution(mesh):
    tile = P("img", "row", "col", None)
    rows = P(GROUP, None)
    columns = P(None, GROUP)
    vector = P(GROUP)
    return jax.shard_map(
        body,
        mesh=mesh,
        in_specs=(
            tile, tile, P("img", None), P("img", None, None), P("img", None), P("img", None),
            columns, rows, rows, rows, rows, rows, columns, rows, rows, rows, rows,
            columns, columns, vector, vector, vector, vector, vector, vector, vector, tile,
        ),
        out_specs=(
            tile, tile, tile, columns, rows, rows, rows, rows, rows, columns, rows, rows, rows,
            rows, columns, columns, vector, vector, vector, vector, vector, vector, vector,
        ),
        check_vma=False,
    )
```

```python
import functools
import math
from typing import NamedTuple

import jax
import jax.numpy as jnp
import numpy as np
from jax import lax
from jax.experimental import pallas as pl
from jax.experimental.pallas import tpu as pltpu
from jax.sharding import PartitionSpec as P

D = 1408
HEADS = 16
HD = 88
FF = 6144
CLIP = 77
NORM_EPS = 1e-06
NEG_FILL = -1e30
STEPS = ((-1, -1), (-1, 0), (-1, 1), (0, -1), (0, 0), (0, 1), (1, -1), (1, 0), (1, 1))
GROUP = ("row", "col")
F32 = jnp.float32
BF = jnp.bfloat16
SCALE = 1.0 / math.sqrt(HD)
LOG2E = math.log2(math.e)
NT = (((1,), (1,)), ((), ()))
KEY_BLOCK = 256
QUERY_CHUNK = 1024


def with_halo(block, sides, width):
    for axis, dim in sides:
        count = lax.axis_size(axis)
        forward = [(i, i + 1) for i in range(count - 1)]
        backward = [(target, source) for source, target in forward]
        low = lax.ppermute(
            lax.slice_in_dim(block, block.shape[dim] - width, None, axis=dim), axis, forward
        )
        high = lax.ppermute(lax.slice_in_dim(block, 0, width, axis=dim), axis, backward)
        block = jnp.concatenate([low, block, high], axis=dim)
    return block


def dot(former, latter, former_dims, latter_dims):
    return lax.dot_general(
        former, latter, ((former_dims, latter_dims), ((), ())), preferred_element_type=F32
    )


def matmul(former, latter):
    return dot(former, latter, (former.ndim - 1,), (0,))


def matmul_back(former, latter):
    return dot(former, latter, (former.ndim - 1,), (1,))


def weight_grad(inputs, grads):
    lead = tuple(range(inputs.ndim - 1))
    return dot(inputs, grads, lead, lead)


def column_sum(grads):
    return jnp.sum(grads.astype(F32), axis=tuple(range(grads.ndim - 1)))


def layer_norm(values, scales, offsets):
    centre = values - jnp.mean(values, axis=-1, keepdims=True)
    spread = jnp.mean(centre * centre, axis=-1, keepdims=True)
    return centre * lax.rsqrt(spread + NORM_EPS) * scales + offsets


def angles_of(row_place, col_place):
    pair_index = np.arange(HD) // 2
    quarter = HD // 4
    within = np.where(pair_index < quarter, pair_index, pair_index - quarter).astype(np.float32)
    frequency = np.exp(np.float32(-math.log(10000.0)) * within / np.float32(quarter))
    by_row = jnp.asarray(pair_index < quarter)
    places = jnp.where(by_row[:, None], row_place[None, :], col_place[None, :])
    return places.astype(F32) * jnp.asarray(frequency.astype(np.float32))[:, None]


def gather_near(padded, tall, broad):
    return jnp.concatenate(
        [
            padded[..., 1 + step_row : 1 + step_row + tall, 1 + step_col : 1 + step_col + broad, :]
            for step_row, step_col in STEPS
        ],
        axis=-1,
    )


def spread_near(padded, tall, broad, channels):
    result = None
    for number, (step_row, step_col) in enumerate(STEPS):
        portion = padded[
            ...,
            1 - step_row : 1 - step_row + tall,
            1 - step_col : 1 - step_col + broad,
            number * channels : (number + 1) * channels,
        ]
        result = portion if result is None else result + portion
    return result


def cuts(vector, widths):
    ends = np.cumsum((0,) + widths)
    return [vector[..., ends[i] : ends[i + 1]] for i in range(len(widths))]


def swap_images(values, bit):
    count = lax.axis_size("img")
    return lax.ppermute(values, "img", [(i, i ^ bit) for i in range(count)])


def images_gather(values):
    blocks = values[None]
    while blocks.shape[0] < lax.axis_size("img"):
        blocks = jnp.concatenate([blocks, swap_images(blocks, blocks.shape[0])])
    return blocks


def images_scatter(parts):
    while parts.shape[0] > 1:
        half = parts.shape[0] // 2
        parts = parts[:half] + swap_images(parts[half:].astype(BF), half).astype(F32)
    return parts[0]


def images_sum(values, sent):
    bit = 1
    while bit < lax.axis_size("img"):
        values = values.astype(sent)
        values = values.astype(F32) + swap_images(values, bit).astype(F32)
        bit *= 2
    return values.astype(F32)


def exchange(values, axis, bit):
    if bit is None:
        return lax.psum_scatter(values, axis, scatter_dimension=0, tiled=True)
    size = lax.axis_size(axis)
    return lax.ppermute(values, axis, [(i, i ^ bit) for i in range(size)])


def halves(values, dim, bit):
    keep = lax.dynamic_index_in_dim(values, bit, dim, keepdims=False)
    return keep, lax.dynamic_index_in_dim(values, 1 - bit, dim, keepdims=False)


def core_features(values, dim, core):
    rows = lax.axis_size("row")
    block = values.shape[dim] // rows
    return jnp.concatenate(
        [
            lax.dynamic_slice_in_dim(values, (2 * i + core) * block, block, dim)
            for i in range(rows // 2)
        ],
        axis=dim,
    )


def row_first():
    rows, cols = lax.axis_size("row"), lax.axis_size("col")
    row_bits = [("row", 1 << i) for i in range(1, rows.bit_length() - 1)]
    return row_bits + [("col", 1 << i) for i in range(cols.bit_length() - 1)]


def shard_sum(order, after, inputs, grads, input_lead, grad_lead, feature):
    core = lax.axis_index("row") % 2
    give = dot(core_features(inputs, feature, 1 - core), grads, input_lead, grad_lead)
    (got,) = yield [give.astype(BF)], "row", 1
    keep = dot(core_features(inputs, feature, core), grads, input_lead, grad_lead)
    part = yield from scatter_sum(order, keep + got.astype(F32))
    part = yield from after(part)
    return part


def offload_sum(after, part):
    (got,) = yield [part.astype(BF)], GROUP, None
    part = yield from after(got.astype(F32))
    return part


def scatter_sum(order, part):
    dims = [d for d in reversed(row_first()) if d[0] == "row"]
    dims += [d for d in reversed(row_first()) if d[0] == "col"]
    width = part.shape[-1]
    part = part.reshape((2,) * len(dims) + (-1, width))
    for axis, bit in order:
        at = dims.index((axis, bit))
        keep, give = halves(part, at, lax.axis_index(axis) // bit % 2)
        del dims[at]
        (got,) = yield [give.astype(BF)], axis, bit
        part = keep + got.astype(F32)
    return part.reshape(-1, width)


def alone(part):
    return part
    yield


def all_images(part):
    bit, blocks = 1, part.astype(BF)[None]
    while bit < lax.axis_size("img"):
        (got,) = yield [blocks], "img", bit
        blocks = placed(blocks, got, lax.axis_index("img") // bit % 2, 0)
        blocks = blocks.reshape((-1,) + part.shape)
        bit *= 2
    return blocks


def placed(mine, other, bit, dim):
    first = lax.select(jnp.broadcast_to(bit == 0, mine.shape), mine, other)
    last = lax.select(jnp.broadcast_to(bit == 0, mine.shape), other, mine)
    return jnp.stack([first, last], axis=dim)


class Moves:
    def __init__(self):
        self.running = {}
        self.done = {}

    def begin(self, value, **makers):
        return self.launch(value, {name: (maker, next(maker)) for name, maker in makers.items()})

    def launch(self, value, wanted):
        if not wanted:
            return value
        gives = {name: request[0] for name, (_, request) in wanted.items()}
        value, gives = lax.optimization_barrier((value, gives))
        for name, (maker, (_, axis, bit)) in wanted.items():
            self.running[name] = (maker, [exchange(give, axis, bit) for give in gives[name]])
        return value

    def step(self, value, *names):
        names = [name for name in names if name in self.running]
        if not names:
            return value
        value, gots = lax.optimization_barrier(
            (value, {name: self.running[name][1] for name in names})
        )
        wanted = {}
        for name in names:
            maker = self.running.pop(name)[0]
            try:
                wanted[name] = (maker, maker.send(gots[name]))
            except StopIteration as stop:
                self.done[name] = stop.value
        return self.launch(value, wanted)

    def finish(self, *names):
        waiting = [name for name in names if name in self.running]
        while waiting:
            for name in waiting:
                maker, gots = self.running.pop(name)
                try:
                    gives, axis, bit = maker.send(gots)
                    self.running[name] = (maker, [exchange(give, axis, bit) for give in gives])
                except StopIteration as stop:
                    self.done[name] = stop.value
            waiting = [name for name in names if name in self.running]


def unit_rows(values):
    centre = values - jnp.mean(values, axis=0, keepdims=True)
    rstd = lax.rsqrt(jnp.mean(centre * centre, axis=0, keepdims=True) + NORM_EPS)
    return centre * rstd, rstd


def swap_pairs(values, back):
    rows = values.shape[0]
    even = lax.broadcasted_iota(jnp.int32, values.shape, 0) % 2 == 0
    up = pltpu.roll(values, rows - 1, 0)
    down = pltpu.roll(values, 1, 0)
    return jnp.where(even, up, -down) if back else jnp.where(even, -up, down)


def turn(values, cos, sin):
    return values * cos + swap_pairs(values, False) * sin


def turn_back(values, cos, sin):
    return values * cos + swap_pairs(values, True) * sin


def tiles(ref, part, count):
    return jnp.concatenate([ref[s, 0, part] for s in range(count)], axis=1)


def key_blocks(geo, ext_ref, job):
    count, tile_rows, tile_cols, col_tiles, block_tiles = geo
    rows = ext_ref[job, 0] // tile_rows
    groups = ext_ref[job, 1] // (block_tiles * tile_cols)

    def place(i):
        block = i // groups * (col_tiles // block_tiles) + i % groups
        return pl.multiple_of(block * KEY_BLOCK, KEY_BLOCK)

    return rows * groups, place


def attend_kernel(
    geo, ext_ref, qkv_ref, cos_ref, sin_ref, head_ref, out_ref, keep_ref, total_ref,
    q_s, kt_s, v_s, m_s, l_s,
):
    count = geo[0]
    cos, sin = cos_ref[...], sin_ref[...]
    unit, _ = unit_rows(tiles(qkv_ref, 0, count).astype(F32))
    q_s[...] = turn(unit * head_ref[:, 0:1] + head_ref[:, 1:2], cos, sin).astype(BF)
    unit, _ = unit_rows(tiles(qkv_ref, 1, count).astype(F32))
    kt_s[...] = turn(unit * head_ref[:, 2:3] + head_ref[:, 3:4], cos, sin).T.astype(BF)
    v_s[...] = tiles(qkv_ref, 2, count)
    block_count, place = key_blocks(geo, ext_ref, pl.program_id(0))
    width = q_s.shape[1]
    m_s[...] = jnp.full_like(m_s, NEG_FILL)
    l_s[...] = jnp.zeros_like(l_s)
    keep_ref[0] = jnp.zeros(keep_ref.shape[1:], F32)

    def key_step(i, carry):
        first = place(i)
        keys = kt_s[pl.ds(first, KEY_BLOCK), :]
        vals = v_s[:, pl.ds(first, KEY_BLOCK)]
        for part in range(width // QUERY_CHUNK):
            cut = slice(part * QUERY_CHUNK, (part + 1) * QUERY_CHUNK)
            scores = jnp.dot(keys, q_s[:, cut], preferred_element_type=F32)
            old = m_s[:, cut]
            new = jnp.maximum(old, jnp.max(scores, axis=0, keepdims=True))
            probs = jnp.exp2((scores - new) * (SCALE * LOG2E))
            factor = jnp.exp2((old - new) * (SCALE * LOG2E))
            m_s[:, cut] = new
            l_s[:, cut] = l_s[:, cut] * factor + jnp.sum(probs, axis=0, keepdims=True)
            keep_ref[0, :, cut] = keep_ref[0, :, cut] * factor + jnp.dot(
                vals, probs.astype(BF), preferred_element_type=F32
            )
        return carry

    lax.fori_loop(0, block_count, key_step, 0)
    total_ref[0] = m_s[...] * (SCALE * LOG2E) + jnp.log2(l_s[...])
    mixed = keep_ref[0] / l_s[...]
    keep_ref[0] = mixed
    low = mixed.astype(BF)
    tile = width // count
    for s in range(count):
        out_ref[s, 0] = low[:, s * tile : (s + 1) * tile]


def attend(ext_jobs, qkv, cos, sin, head, geo):
    count, jobs, _, _, tile = qkv.shape
    width = count * tile
    work = 4 * jobs * width * width * HD
    return pl.pallas_call(
        functools.partial(attend_kernel, geo),
        grid=(jobs,),
        in_specs=[
            pl.BlockSpec(memory_space=pltpu.SMEM),
            pl.BlockSpec((count, 1, 3, HD, tile), lambda j: (0, j, 0, 0, 0)),
            pl.BlockSpec((HD, width), lambda j: (0, 0)),
            pl.BlockSpec((HD, width), lambda j: (0, 0)),
            pl.BlockSpec((HD, 4), lambda j: (0, 0)),
        ],
        out_specs=[
            pl.BlockSpec((count, 1, HD, tile), lambda j: (0, j, 0, 0)),
            pl.BlockSpec((1, HD, width), lambda j: (j, 0, 0)),
            pl.BlockSpec((1, 1, width), lambda j: (j, 0, 0)),
        ],
        out_shape=[
            jax.ShapeDtypeStruct((count, jobs, HD, tile), BF),
            jax.ShapeDtypeStruct((jobs, HD, width), F32),
            jax.ShapeDtypeStruct((jobs, 1, width), F32),
        ],
        scratch_shapes=[
            pltpu.VMEM((HD, width), BF),
            pltpu.VMEM((width, HD), BF),
            pltpu.VMEM((HD, width), BF),
            pltpu.VMEM((1, width), F32),
            pltpu.VMEM((1, width), F32),
        ],
        compiler_params=pltpu.CompilerParams(vmem_limit_bytes=48 * 2**20),
        cost_estimate=pl.CostEstimate(
            flops=3 * work, bytes_accessed=6 * 2**20, transcendentals=jobs * width * width
        ),
    )(ext_jobs, qkv, cos, sin, head)


def attend_back_kernel(
    geo, ext_ref, qkv_ref, dout_ref, keep_ref, total_ref, cos_ref, sin_ref, head_ref,
    grad_ref, head_grad_ref, q_s, k_s, kt_s, vt_s, do_s, delta_s, dq_s, dk_s, dv_s,
):
    count = geo[0]
    cos, sin = cos_ref[...], sin_ref[...]
    unit, _ = unit_rows(tiles(qkv_ref, 0, count).astype(F32))
    q_s[...] = turn(unit * head_ref[:, 0:1] + head_ref[:, 1:2], cos, sin).astype(BF)
    unit, _ = unit_rows(tiles(qkv_ref, 1, count).astype(F32))
    keys = turn(unit * head_ref[:, 2:3] + head_ref[:, 3:4], cos, sin)
    k_s[...] = keys.astype(BF)
    kt_s[...] = keys.T.astype(BF)
    vt_s[...] = tiles(qkv_ref, 2, count).astype(F32).T.astype(BF)
    dout = jnp.concatenate([dout_ref[s, 0] for s in range(count)], axis=1)
    do_s[...] = dout
    delta_s[...] = jnp.sum(dout.astype(F32) * keep_ref[0], axis=0, keepdims=True)
    block_count, place = key_blocks(geo, ext_ref, pl.program_id(0))
    width = q_s.shape[1]
    dq_s[...] = jnp.zeros_like(dq_s)
    dk_s[...] = jnp.zeros_like(dk_s)
    dv_s[...] = jnp.zeros_like(dv_s)

    def key_step(i, carry):
        first = place(i)
        keys_t = kt_s[pl.ds(first, KEY_BLOCK), :]
        vals_t = vt_s[pl.ds(first, KEY_BLOCK), :]
        keys_n = k_s[:, pl.ds(first, KEY_BLOCK)]
        dk = jnp.zeros((HD, KEY_BLOCK), F32)
        dv = jnp.zeros((HD, KEY_BLOCK), F32)
        for part in range(width // QUERY_CHUNK):
            cut = slice(part * QUERY_CHUNK, (part + 1) * QUERY_CHUNK)
            queries = q_s[:, cut]
            douts = do_s[:, cut]
            scores = jnp.dot(keys_t, queries, preferred_element_type=F32)
            probs = jnp.exp2(scores * (SCALE * LOG2E) - total_ref[0, :, cut])
            dprob = jnp.dot(vals_t, douts, preferred_element_type=F32)
            dscore = (probs * (dprob - delta_s[:, cut])).astype(BF)
            dv = dv + lax.dot_general(douts, probs.astype(BF), NT, preferred_element_type=F32)
            dk = dk + lax.dot_general(queries, dscore, NT, preferred_element_type=F32)
            dq_s[:, cut] += jnp.dot(keys_n, dscore, preferred_element_type=F32)
        dk_s[:, pl.ds(first, KEY_BLOCK)] = dk
        dv_s[:, pl.ds(first, KEY_BLOCK)] = dv
        return carry

    lax.fori_loop(0, block_count, key_step, 0)
    tile = width // count

    def lift(part, turned, at):
        unit, rstd = unit_rows(tiles(qkv_ref, part, count).astype(F32))
        dy = turn_back(turned * SCALE, cos, sin)
        head_grad_ref[0, :, at : at + 1] = jnp.sum(dy * unit, axis=1, keepdims=True)
        head_grad_ref[0, :, at + 1 : at + 2] = jnp.sum(dy, axis=1, keepdims=True)
        dunit = dy * head_ref[:, at : at + 1]
        along = jnp.mean(dunit * unit, axis=0, keepdims=True)
        dx = (dunit - jnp.mean(dunit, axis=0, keepdims=True) - unit * along) * rstd
        low = dx.astype(BF)
        for s in range(count):
            grad_ref[s, 0, part] = low[:, s * tile : (s + 1) * tile]

    lift(0, dq_s[...], 0)
    lift(1, dk_s[...], 2)
    low = dv_s[...].astype(BF)
    for s in range(count):
        grad_ref[s, 0, 2] = low[:, s * tile : (s + 1) * tile]


def attend_back(ext_jobs, qkv, dout, keep, total, cos, sin, head, geo):
    count, jobs, _, _, tile = qkv.shape
    width = count * tile
    work = 10 * jobs * width * width * HD
    return pl.pallas_call(
        functools.partial(attend_back_kernel, geo),
        grid=(jobs,),
        in_specs=[
            pl.BlockSpec(memory_space=pltpu.SMEM),
            pl.BlockSpec((count, 1, 3, HD, tile), lambda j: (0, j, 0, 0, 0)),
            pl.BlockSpec((count, 1, HD, tile), lambda j: (0, j, 0, 0)),
            pl.BlockSpec((1, HD, width), lambda j: (j, 0, 0)),
            pl.BlockSpec((1, 1, width), lambda j: (j, 0, 0)),
            pl.BlockSpec((HD, width), lambda j: (0, 0)),
            pl.BlockSpec((HD, width), lambda j: (0, 0)),
            pl.BlockSpec((HD, 4), lambda j: (0, 0)),
        ],
        out_specs=[
            pl.BlockSpec((count, 1, 3, HD, tile), lambda j: (0, j, 0, 0, 0)),
            pl.BlockSpec((1, HD, 4), lambda j: (j, 0, 0)),
        ],
        out_shape=[
            jax.ShapeDtypeStruct((count, jobs, 3, HD, tile), BF),
            jax.ShapeDtypeStruct((jobs, HD, 4), F32),
        ],
        scratch_shapes=[
            pltpu.VMEM((HD, width), BF),
            pltpu.VMEM((HD, width), BF),
            pltpu.VMEM((width, HD), BF),
            pltpu.VMEM((width, HD), BF),
            pltpu.VMEM((HD, width), BF),
            pltpu.VMEM((1, width), F32),
            pltpu.VMEM((HD, width), F32),
            pltpu.VMEM((HD, width), F32),
            pltpu.VMEM((HD, width), F32),
        ],
        compiler_params=pltpu.CompilerParams(vmem_limit_bytes=56 * 2**20),
        cost_estimate=pl.CostEstimate(
            flops=3 * work, bytes_accessed=8 * 2**20, transcendentals=jobs * width * width
        ),
    )(ext_jobs, qkv, dout, keep, total, cos, sin, head)


TN = (((0,), (0,)), ((), ()))
CROSS_HEADS = 2


def text_scores(len_ref, keys, queries, image):
    scores = lax.dot_general(keys, queries, TN, preferred_element_type=F32) * (SCALE * LOG2E)
    place = lax.broadcasted_iota(jnp.int32, scores.shape, 0)
    live = (place < len_ref[image, 0]) | (
        (place >= CLIP) & (place < CLIP + len_ref[image, 1])
    )
    return jnp.where(live, scores, NEG_FILL)


def cross_kernel(images, len_ref, rows_ref, text_ref, cos_ref, sin_ref, head_ref, out_ref, total_ref):
    tile = rows_ref.shape[2] // images
    slots = text_ref.shape[3] // images
    for h in range(CROSS_HEADS):
        unit, _ = unit_rows(rows_ref[h])
        queries = turn(unit * head_ref[:, 0:1] + head_ref[:, 1:2], cos_ref[...], sin_ref[...])
        queries = queries.astype(BF)
        for i in range(images):
            own, slot = slice(i * tile, (i + 1) * tile), slice(i * slots, (i + 1) * slots)
            scores = text_scores(len_ref, text_ref[0, h, :, slot], queries[:, own], i)
            top = jnp.max(scores, axis=0, keepdims=True)
            probs = jnp.exp2(scores - top)
            weight = jnp.sum(probs, axis=0, keepdims=True)
            low = (probs / weight).astype(BF)
            mixed = jnp.dot(text_ref[1, h, :, slot], low, preferred_element_type=F32)
            out_ref[h, :, own] = mixed.astype(BF)
            total_ref[h, :, own] = top + jnp.log2(weight)


def cross_back_kernel(
    images, len_ref, rows_ref, text_ref, dout_ref, total_ref, cos_ref, sin_ref, head_ref,
    grad_ref, text_grad_ref, head_grad_ref,
):
    tile = rows_ref.shape[2] // images
    slots = text_ref.shape[3] // images
    cos, sin = cos_ref[...], sin_ref[...]
    gain_grad = jnp.zeros((HD, 1), F32)
    shift_grad = jnp.zeros((HD, 1), F32)
    for h in range(CROSS_HEADS):
        unit, rstd = unit_rows(rows_ref[h])
        queries = turn(unit * head_ref[:, 0:1] + head_ref[:, 1:2], cos, sin).astype(BF)
        turned = []
        for i in range(images):
            own, slot = slice(i * tile, (i + 1) * tile), slice(i * slots, (i + 1) * slots)
            keys = text_ref[0, h, :, slot]
            douts = dout_ref[h, :, own]
            scores = text_scores(len_ref, keys, queries[:, own], i)
            probs = jnp.exp2(scores - total_ref[h, :, own])
            dprob = lax.dot_general(
                text_ref[1, h, :, slot], douts, TN, preferred_element_type=F32
            )
            delta = jnp.sum(probs * dprob, axis=0, keepdims=True)
            dscore = (probs * (dprob - delta)).astype(BF)
            low = probs.astype(BF)
            dkeys = lax.dot_general(queries[:, own], dscore, NT, preferred_element_type=F32)
            text_grad_ref[0, h, :, slot] = (dkeys * SCALE).astype(BF)
            text_grad_ref[1, h, :, slot] = lax.dot_general(
                douts, low, NT, preferred_element_type=F32
            ).astype(BF)
            turned.append(jnp.dot(keys, dscore, preferred_element_type=F32))
        dy = turn_back(jnp.concatenate(turned, axis=1) * SCALE, cos, sin)
        gain_grad += jnp.sum(dy * unit, axis=1, keepdims=True)
        shift_grad += jnp.sum(dy, axis=1, keepdims=True)
        dunit = dy * head_ref[:, 0:1]
        along_unit = jnp.mean(dunit * unit, axis=0, keepdims=True)
        dx = (dunit - jnp.mean(dunit, axis=0, keepdims=True) - unit * along_unit) * rstd
        grad_ref[h] = dx.astype(BF)
    head_grad_ref[0, :, 0:1] = gain_grad
    head_grad_ref[0, :, 1:2] = shift_grad


def cross_specs(width, slots):
    return dict(
        smem=pl.BlockSpec(memory_space=pltpu.SMEM),
        rows=pl.BlockSpec((CROSS_HEADS, HD, width), lambda h: (h, 0, 0)),
        text=pl.BlockSpec((2, CROSS_HEADS, HD, slots), lambda h: (0, h, 0, 0)),
        table=pl.BlockSpec((HD, width), lambda h: (0, 0)),
        head=pl.BlockSpec((HD, 2), lambda h: (0, 0)),
        total=pl.BlockSpec((CROSS_HEADS, 1, width), lambda h: (h, 0, 0)),
        head_grad=pl.BlockSpec((1, HD, 2), lambda h: (h, 0, 0)),
    )


def cross_attend(lengths, rows, text, cos, sin, head):
    heads, _, width = rows.shape
    slots = text.shape[3]
    sp = cross_specs(width, slots)
    return pl.pallas_call(
        functools.partial(cross_kernel, lengths.shape[0]),
        grid=(heads // CROSS_HEADS,),
        in_specs=[sp["smem"], sp["rows"], sp["text"], sp["table"], sp["table"], sp["head"]],
        out_specs=[sp["rows"], sp["total"]],
        out_shape=[
            jax.ShapeDtypeStruct((heads, HD, width), BF),
            jax.ShapeDtypeStruct((heads, 1, width), F32),
        ],
        compiler_params=pltpu.CompilerParams(vmem_limit_bytes=32 * 2**20),
        cost_estimate=pl.CostEstimate(
            flops=2**32, bytes_accessed=10 * 2**20, transcendentals=heads * width * slots
        ),
    )(lengths, rows, text, cos, sin, head)


def cross_attend_back(lengths, rows, text, dout, total, cos, sin, head):
    heads, _, width = rows.shape
    slots = text.shape[3]
    sp = cross_specs(width, slots)
    return pl.pallas_call(
        functools.partial(cross_back_kernel, lengths.shape[0]),
        grid=(heads // CROSS_HEADS,),
        in_specs=[
            sp["smem"], sp["rows"], sp["text"], sp["rows"], sp["total"], sp["table"], sp["table"],
            sp["head"],
        ],
        out_specs=[sp["rows"], sp["text"], sp["head_grad"]],
        out_shape=[
            jax.ShapeDtypeStruct((heads, HD, width), BF),
            jax.ShapeDtypeStruct((2, heads, HD, slots), BF),
            jax.ShapeDtypeStruct((heads // CROSS_HEADS, HD, 2), F32),
        ],
        compiler_params=pltpu.CompilerParams(vmem_limit_bytes=32 * 2**20),
        cost_estimate=pl.CostEstimate(
            flops=2**33, bytes_accessed=16 * 2**20, transcendentals=heads * width * slots
        ),
    )(lengths, rows, text, dout, total, cos, sin, head)


MESH = pl.DeviceIdType.MESH
LAG = 3
ROW_SHARE = 5


class Kind(NamedTuple):
    operand: int
    first_row: int
    width: int
    height: int
    chunks: int
    stride: int
    order: tuple


def sum_plan(sizes, kind):
    groups, row_count, cols = sizes
    count, height = row_count * cols // 2, kind.height
    firsts = {"img": (0, groups), "row": (1, row_count), "col": (0, cols)}
    plan = []
    for axis, i in [
        (axis, i)
        for axis in kind.order
        for i in range(firsts[axis][0], firsts[axis][1].bit_length() - 1)
    ]:
        bit = 1 << i
        if axis == "img":
            height //= 2
        else:
            count //= 2
        plan.append((axis, bit, count, height))
    return plan


def sum_kernel(sizes, kinds, *refs):
    groups, row_count, cols = sizes
    number = 1 + max(kind.operand for kind in kinds)
    grads_refs, out_refs, scratch = refs[:number], refs[number : 2 * number], refs[2 * number :]
    first_count = row_count * cols // 2
    places = {axis: lax.axis_index(axis) for axis in ("img", "row", "col")}
    plans = [sum_plan(sizes, kind) for kind in kinds]
    image_stages = groups.bit_length() - 1
    held, own, sems = [], [], []
    at = 0
    for plan in plans:
        held.append(scratch[at : at + len(plan) + 1])
        own.append(scratch[at + len(plan) + 1])
        sems.append(scratch[at + len(plan) + 2 : at + len(plan) + 8])
        at += len(plan) + 8
    core = places["row"] % 2

    def device_of(place):
        return tuple(place[name] for name in ("img", "row", "col"))

    def partner(axis, bit):
        place = dict(places)
        part = place[axis] // bit % 2
        place[axis] = place[axis] + bit - 2 * bit * part
        return device_of(place)

    def other_images():
        for i in range(1, groups):
            place = dict(places)
            place["img"] = lax.rem(places["img"] + i, groups)
            yield i, device_of(place)

    def bit_of(axis, bit):
        return places[axis] // bit % 2

    def chunk_rows(k, chunk):
        return pl.multiple_of(kinds[k].first_row + chunk * kinds[k].height, 16)

    def first_copies(k, chunk):
        rows = pl.ds(chunk_rows(k, chunk), kinds[k].height)
        for i in range(row_count // 2):
            shards = pl.ds((2 * i + 1 - core) * cols, cols)
            yield pltpu.make_async_remote_copy(
                src_ref=grads_refs[kinds[k].operand].at[shards, rows],
                dst_ref=held[k][0].at[chunk, pl.ds(i * cols, cols)],
                send_sem=sems[k][0].at[0, chunk],
                recv_sem=sems[k][1].at[0, chunk],
                device_id=partner("row", 1),
                device_id_type=MESH,
            )

    def own_copies(k, chunk):
        rows = pl.ds(chunk_rows(k, chunk), kinds[k].height)
        for i in range(row_count // 2):
            shards = pl.ds((2 * i + core) * cols, cols)
            yield pltpu.make_async_copy(
                grads_refs[kinds[k].operand].at[shards, rows],
                own[k].at[lax.rem(chunk, 2), pl.ds(i * cols, cols)],
                sems[k][4].at[lax.rem(chunk, 2)],
            )

    def split(k, stage):
        axis, bit, count, rows = plans[k][stage]
        part = bit_of(axis, bit)
        if axis == "img":
            give = pl.ds(pl.multiple_of((1 - part) * rows, 16), rows)
            keep = pl.ds(pl.multiple_of(part * rows, 16), rows)
            return [((pl.ds(0, count), give), pl.ds(0, count))], lambda i: (i, keep)
        every = pl.ds(0, rows)
        if axis == "row":
            give = pl.ds((1 - part) * count, count)
            return [((give, every), pl.ds(0, count))], lambda i: (part * count + i, every)
        return (
            [((pl.ds(2 * i + 1 - part, 1), every), pl.ds(i, 1)) for i in range(count)],
            lambda i: (2 * i + part, every),
        )

    def stage_copies(k, stage, chunk):
        axis, bit, _, _ = plans[k][stage]
        for (shards, lines), target in split(k, stage)[0]:
            yield pltpu.make_async_remote_copy(
                src_ref=held[k][stage].at[chunk, shards, lines],
                dst_ref=held[k][stage + 1].at[chunk, target],
                send_sem=sems[k][0].at[stage + 1, chunk],
                recv_sem=sems[k][1].at[stage + 1, chunk],
                device_id=partner(axis, bit),
                device_id_type=MESH,
            )

    def whole(k, stage, chunk):
        buffer = held[k][stage].at[chunk]
        return pltpu.make_async_remote_copy(
            src_ref=buffer,
            dst_ref=buffer,
            send_sem=sems[k][0].at[stage, chunk],
            recv_sem=sems[k][1].at[stage, chunk],
            device_id=partner("row", 1),
            device_id_type=MESH,
        )

    def home(k, chunk):
        rows = plans[k][-1][3]
        out_ref = out_refs[kinds[k].operand]
        if "img" not in kinds[k].order:
            return out_ref.at[places["img"], pl.ds(chunk_rows(k, chunk), rows)]
        place = 0
        for i in range(image_stages):
            place = place + bit_of("img", 1 << i) * (1 << (image_stages - 1 - i))
        return out_ref.at[pl.ds(pl.multiple_of(chunk_rows(k, chunk) + place * rows, 16), rows)]

    def spread_copies(k, chunk):
        for i, other in other_images():
            yield pltpu.make_async_remote_copy(
                src_ref=held[k][-1].at[chunk, 0],
                dst_ref=home(k, chunk),
                send_sem=sems[k][2].at[i, chunk],
                recv_sem=sems[k][3].at[i, chunk],
                device_id=other,
                device_id_type=MESH,
            )

    def home_copy(k, chunk):
        return pltpu.make_async_copy(
            held[k][-1].at[chunk, 0], home(k, chunk), sems[k][5].at[chunk]
        )

    def start(copies):
        for copy in copies:
            copy.start()

    def begin(k, chunk):
        start(first_copies(k, chunk))
        start(own_copies(k, chunk))

    barrier = pltpu.get_barrier_semaphore()
    near = [partner("row", 1)] + [partner(a, b) for a, b, _, _ in plans[0] if a != "img"]
    near += [other for _, other in other_images()]
    for other in near:
        pl.semaphore_signal(barrier, inc=1, device_id=other, device_id_type=MESH)
    pl.semaphore_wait(barrier, len(near))

    for k in range(len(kinds)):
        begin(k, 0)

    def advance(k, stage, chunk):
        if stage == 0:

            @pl.when(chunk + 1 < kinds[k].chunks)
            def _():
                begin(k, chunk + 1)

        buffer = held[k][stage]
        whole(k, stage, chunk).wait_recv()
        if stage == 0:
            count = first_count
            for copy in own_copies(k, chunk):
                copy.wait()

            def mine(i):
                return own[k][lax.rem(chunk, 2), i]
        else:
            count = plans[k][stage - 1][2]
            kept = split(k, stage - 1)[1]

            def mine(i):
                shard, lines = kept(i)
                return held[k][stage - 1][chunk, shard, lines]

        def add(i, carry):
            both = buffer[chunk, i].astype(F32) + mine(i).astype(F32)
            buffer[chunk, i] = both.astype(BF)
            return carry

        lax.fori_loop(0, count, add, 0)
        if stage < len(plans[k]):
            start(stage_copies(k, stage, chunk))
        else:
            start(spread_copies(k, chunk))
            home_copy(k, chunk).start()

    def time_step(t, carry):
        for stage in range(max(len(plan) for plan in plans), -1, -1):
            for k, kind in enumerate(kinds):
                if stage <= len(plans[k]):
                    since = t - LAG * stage
                    chunk = since // kind.stride
                    due = jnp.logical_and(since >= 0, since % kind.stride == 0)

                    @pl.when(jnp.logical_and(due, chunk < kind.chunks))
                    def _(k=k, stage=stage, chunk=chunk):
                        advance(k, stage, chunk)

        return carry

    last = max(k.stride * k.chunks + LAG * len(plan) for k, plan in zip(kinds, plans))
    lax.fori_loop(0, last, time_step, 0)

    for k, kind in enumerate(kinds):

        def drain(chunk, carry, k=k):
            for stage in range(len(plans[k]) + 1):
                whole(k, stage, chunk).wait_send()
            for copy in spread_copies(k, chunk):
                copy.wait()
            home_copy(k, chunk).wait()
            return carry

        lax.fori_loop(0, kind.chunks, drain, 0)


def sum_everywhere(projections, down, up, sizes):
    groups, row_count, cols = sizes
    first_count = row_count * cols // 2
    height = 16 * groups
    chunks = projections.shape[1] // height
    late = max(1, chunks * ROW_SHARE // 22)
    early = chunks - late
    kinds = [
        Kind(0, 0, D, height, early, 1, ("img", "row", "col")),
        Kind(0, early * height, D, height, late, 3, ("row", "img", "col")),
        Kind(1, 0, up.shape[2], 16, up.shape[1] // 16, 3, ("row", "col")),
        Kind(2, 0, D, 16, down.shape[1] // 16, 1, ("col", "row")),
    ]
    scratch = []
    for kind in kinds:
        plan = sum_plan(sizes, kind)
        shapes = [(first_count, kind.height)] + [(c, h) for _, _, c, h in plan]
        scratch += [pltpu.VMEM((kind.chunks, c, h, kind.width), BF) for c, h in shapes]
        scratch.append(pltpu.VMEM((2, first_count, kind.height, kind.width), BF))
        stage_sems = pltpu.SemaphoreType.DMA((len(plan) + 1, kind.chunks))
        spread_sems = pltpu.SemaphoreType.DMA((groups, kind.chunks))
        scratch += [
            stage_sems, stage_sems, spread_sems, spread_sems,
            pltpu.SemaphoreType.DMA((2,)), pltpu.SemaphoreType.DMA((kind.chunks,)),
        ]
    space = pl.BlockSpec(memory_space=pl.ANY)
    return pl.pallas_call(
        functools.partial(sum_kernel, sizes, kinds),
        out_shape=[
            jax.ShapeDtypeStruct(projections.shape[1:], BF),
            jax.ShapeDtypeStruct((groups,) + up.shape[1:], BF),
            jax.ShapeDtypeStruct((groups,) + down.shape[1:], BF),
        ],
        in_specs=[space] * 3,
        out_specs=[space] * 3,
        scratch_shapes=scratch,
        compiler_params=pltpu.CompilerParams(
            collective_id=1, has_side_effects=True, vmem_limit_bytes=58 * 2**20
        ),
        cost_estimate=pl.CostEstimate(flops=2**28, bytes_accessed=2**28, transcendentals=0),
    )(projections, up, down)


def all_to_all(values):
    return lax.all_to_all(values, GROUP, split_axis=0, concat_axis=0, tiled=True)


def body(
    latents, skip, temb, text, text_len, extent, embed_weight, skip_weight, shift_weight,
    qkv_weight, out_weight, cross_query, cross_keys, cross_out, up_weight, down_weight,
    final_weight, norm_gain, norm_shift, skip_gain, skip_shift, head_gain, head_shift,
    front_biases, all_biases, cross_bias, cotangent,
):
    img_count, tile_rows, tile_cols, patch_vals = latents.shape
    tokens = tile_rows * tile_cols
    near_vals = 9 * patch_vals
    row_count = lax.axis_size("row")
    col_count = lax.axis_size("col")
    count = row_count * col_count
    groups = lax.axis_size("img")
    jobs = img_count * HEADS // count
    row_index = lax.axis_index("row")
    col_index = lax.axis_index("col")
    group_index = lax.axis_index("img")
    device = row_index * col_count + col_index
    shard = D // count
    hid_shard = FF // count
    hid_part = hid_shard // groups

    small_widths = (
        norm_gain.size, norm_shift.size, skip_gain.size, skip_shift.size,
        head_gain.size, head_shift.size, front_biases.size, all_biases.size,
    )
    small = jnp.concatenate(
        [
            embed_weight.T.reshape(-1), final_weight.reshape(-1), norm_gain.reshape(-1),
            norm_shift.reshape(-1), skip_gain, skip_shift, head_gain, head_shift,
            front_biases, all_biases,
        ]
    )
    small_len = small.size
    padded_len = -(-(small_len + img_count * D) // 2048) * 2048
    time_act = jax.nn.silu(temb.astype(F32)).astype(BF)
    time_own = lax.dynamic_slice_in_dim(time_act, device * shard, shard, 1)
    shift_share = matmul(time_own, shift_weight).astype(BF).reshape(-1)
    small = jnp.pad(jnp.concatenate([small, shift_share]), (0, padded_len - small_len - shift_share.size))
    small_all = all_to_all(jnp.broadcast_to(small.reshape(1, -1, 128), (count, padded_len // 128, 128)))
    small_all = small_all.reshape(count, padded_len)
    def beside(values, parts):
        return jnp.concatenate(jnp.split(values, parts, axis=0), axis=1)

    def below(values, parts):
        width = values.shape[1] // parts
        blocks = [values[:, i * width : (i + 1) * width] for i in range(parts)]
        return jnp.stack([b.reshape(count, -1, width) for b in blocks], axis=1).reshape(-1, width)

    first_all = lax.all_gather(
        jnp.concatenate([beside(skip_weight, 2), qkv_weight], axis=1), GROUP, axis=0, tiled=True
    )
    skip_full = below(first_all[:, : 2 * D], 2)
    qkv_full = first_all[:, 2 * D :]
    folds = hid_part // shard
    fold_rows = hid_part // folds
    up_part = lax.dynamic_index_in_dim(
        up_weight.reshape(shard, count, groups, hid_part), group_index, 2, keepdims=False
    ).reshape(shard, count * hid_part)
    down_part = lax.dynamic_index_in_dim(
        down_weight.reshape(groups, hid_part, D), group_index, 0, keepdims=False
    )
    third = jnp.concatenate(
        [jnp.pad(up_part, ((0, fold_rows - shard), (0, 0))), beside(down_part, folds)], axis=1
    )

    wide = shard * near_vals
    embed_t = small_all[:, :wide].reshape(D, near_vals)
    final_full = small_all[:, wide : 2 * wide].reshape(D, near_vals)
    vectors = cuts(small_all[:, 2 * wide : small_len].astype(F32), small_widths)
    gain_rows = jnp.transpose(vectors[0].reshape(count, 3, shard), (1, 0, 2)).reshape(3, D)
    offset_rows = jnp.transpose(vectors[1].reshape(count, 3, shard), (1, 0, 2)).reshape(3, D)
    skip_gains, skip_offsets = vectors[2].reshape(-1), vectors[3].reshape(-1)
    head_gains, head_offsets = vectors[4].reshape(4, HD), vectors[5].reshape(4, HD)
    bias_embed, bias_skip, bias_shift, bias_qkv = cuts(vectors[6].reshape(-1), (D, D, D, 3 * D))
    bias_out, bias_cross_q, bias_cross_o, bias_up, bias_down = cuts(
        vectors[7].reshape(-1), (D, D, D, FF, D)
    )
    bias_up_part = lax.dynamic_index_in_dim(
        bias_up.reshape(count, groups, hid_part), group_index, 1, keepdims=False
    ).reshape(-1)

    local_rows = row_index * tile_rows + jnp.arange(tile_rows, dtype=jnp.int32)
    local_cols = col_index * tile_cols + jnp.arange(tile_cols, dtype=jnp.int32)
    inside = (
        (local_rows[None, :, None] < extent[:, 0, None, None])
        & (local_cols[None, None, :] < extent[:, 1, None, None])
    ).astype(F32)
    token_inside = inside.reshape(img_count, tokens, 1)
    own_angle = angles_of(
        jnp.tile(jnp.repeat(local_rows, tile_cols), img_count),
        jnp.tile(jnp.tile(local_cols, tile_rows), img_count),
    )
    own_cos, own_sin = jnp.cos(own_angle), jnp.sin(own_angle)
    every = np.arange(count * tokens)
    every_row = every // tokens // col_count * tile_rows + every % tokens // tile_cols
    every_col = every // tokens % col_count * tile_cols + every % tile_cols
    every_angle = angles_of(jnp.asarray(every_row), jnp.asarray(every_col))
    every_cos, every_sin = jnp.cos(every_angle), jnp.sin(every_angle)
    job_images = (device * jobs + jnp.arange(jobs, dtype=jnp.int32)) % img_count
    ext_jobs = jnp.take(extent, job_images, axis=0)
    geo = (count, tile_rows, tile_cols, col_count, KEY_BLOCK // tokens)

    def gelu_tanh(values):
        return jax.nn.gelu(values, approximate=True)

    text_width = cross_keys.shape[1]
    text_count = -(-text.shape[1] // 128) * 128
    text_wide = jnp.pad(text, ((0, 0), (0, text_count - text.shape[1]), (0, 0)))
    is_key = device * text_width + jnp.arange(text_width, dtype=jnp.int32) < D

    def text_norm(values, scales, offsets):
        per_head = values.reshape(text_width // HD, HD, -1)
        centre = per_head - jnp.mean(per_head, axis=1, keepdims=True)
        spread = jnp.mean(centre * centre, axis=1, keepdims=True)
        unit = centre * lax.rsqrt(spread + NORM_EPS) * scales[:, None] + offsets[:, None]
        return jnp.where(is_key[:, None], unit.reshape(values.shape), values)

    text_part = dot(cross_keys, text_wide, (0,), (2,)).reshape(text_width, -1)
    text_part = text_part + cross_bias.astype(F32)[:, None]
    text_normed, text_pull = jax.vjp(text_norm, text_part, head_gains[3], head_offsets[3])
    moves = Moves()
    second_all = lax.all_gather(
        jnp.concatenate(
            [out_weight, cross_query, cross_out, beside(text_normed.astype(BF), 2)], axis=1
        ),
        GROUP,
        axis=0,
        tiled=True,
    )
    out_full, cross_q_full, cross_o_full = [second_all[:, i * D : (i + 1) * D] for i in range(3)]
    text_both = below(second_all[:, 3 * D :], 2).reshape(2, HEADS, HD, img_count * text_count)
    third_all = lax.all_gather(third, GROUP, axis=0, tiled=True)
    third_rows = third_all.reshape(count, fold_rows, -1)
    up_full = third_rows[:, :shard, : count * hid_part].reshape(D, count * hid_part)
    down_full = below(third_all[:, count * hid_part :], folds)
    shift_sums = small_all[:, small_len : small_len + img_count * D].astype(F32)
    shift_rows = jnp.sum(shift_sums, axis=0).reshape(img_count, D) + bias_shift

    lat_masked = (latents * inside[..., None]).astype(BF)
    cot_masked = (cotangent * inside[..., None]).astype(BF)
    rims = with_halo(
        jnp.concatenate([lat_masked, cot_masked], axis=-1), (("row", 1), ("col", 2)), 1
    )
    rims = rims.astype(F32)
    near = gather_near(rims[..., :patch_vals], tile_rows, tile_cols)
    near = near.reshape(img_count, tokens, near_vals).astype(BF)
    cot_near = gather_near(rims[..., patch_vals:], tile_rows, tile_cols)
    cot_near = cot_near.reshape(img_count, tokens, near_vals)
    embedded = matmul_back(near, embed_t) + bias_embed
    joined_full = jnp.concatenate(
        [embedded, skip.reshape(img_count, tokens, D).astype(F32)], axis=-1
    )
    skip_normed, skip_norm_pull = jax.vjp(layer_norm, joined_full, skip_gains, skip_offsets)
    skip_in = skip_normed.astype(BF)
    resid_in = matmul(skip_in, skip_full) + bias_skip
    self_norm, self_norm_pull = jax.vjp(layer_norm, resid_in, gain_rows[0], offset_rows[0])
    normed = (self_norm + shift_rows[:, None, :]).astype(BF)

    qkv_t = dot(qkv_full, normed, (0,), (2,)) + bias_qkv[:, None, None]
    qkv_t = qkv_t.astype(BF).reshape(3, HEADS, HD, img_count, tokens)
    qkv_jobs = all_to_all(
        jnp.transpose(qkv_t, (1, 3, 0, 2, 4)).reshape(count, jobs, 3, HD, tokens)
    )
    head_cols = jnp.stack([head_gains[0], head_offsets[0], head_gains[1], head_offsets[1]], axis=1)
    mixed_jobs, keep, total = attend(ext_jobs, qkv_jobs, every_cos, every_sin, head_cols, geo)
    mixed = all_to_all(mixed_jobs).reshape(HEADS, img_count, HD, tokens)
    attended_t = jnp.transpose(mixed, (1, 0, 2, 3)).reshape(img_count, D, tokens)
    resid_self = resid_in + dot(attended_t, out_full, (1,), (0,)) + bias_out

    cross_norm, cross_norm_pull = jax.vjp(layer_norm, resid_self, gain_rows[1], offset_rows[1])
    cross_in = cross_norm.astype(BF)
    all_tokens = img_count * tokens
    cross_rows = dot(cross_q_full, cross_in.reshape(all_tokens, D), (0,), (1,))
    cross_rows = (cross_rows + bias_cross_q[:, None]).reshape(HEADS, HD, all_tokens)
    cross_cols = jnp.stack([head_gains[2], head_offsets[2]], axis=1)
    cross_mixed, cross_total = cross_attend(
        text_len, cross_rows, text_both, own_cos, own_sin, cross_cols
    )
    cross_low = cross_mixed.reshape(D, all_tokens)
    cross_out_rows = dot(cross_low, cross_o_full, (0,), (0,)).reshape(img_count, tokens, D)
    resid_cross = resid_self + cross_out_rows + bias_cross_o

    mlp_norm, mlp_norm_pull = jax.vjp(layer_norm, resid_cross, gain_rows[2], offset_rows[2])
    mlp_in = images_gather(mlp_norm.astype(BF))
    hidden = matmul(mlp_in, up_full) + bias_up_part
    gelu_out, gelu_pull = jax.vjp(gelu_tanh, hidden)
    activated = gelu_out.astype(BF)
    resid_out = resid_cross + images_scatter(matmul(activated, down_full)) + bias_down
    resid_low = resid_out.astype(BF)
    emitted = matmul(resid_low, final_full) * token_inside
    emit_rim = with_halo(
        emitted.reshape(img_count, tile_rows, tile_cols, near_vals), (("row", 1), ("col", 2)), 1
    )
    out_latents = spread_near(emit_rim, tile_rows, tile_cols, patch_vals) * inside[..., None]

    lead = (0, 1)
    by_row = row_first()
    grad_emitted = (cot_near * token_inside).astype(BF)
    grad_final = weight_grad(resid_low, grad_emitted)
    grad_resid_out = matmul_back(grad_emitted, final_full)
    grad_down_low = grad_resid_out.astype(BF)
    bias_down_grad = column_sum(grad_down_low)
    grad_down_rows = images_gather(grad_down_low)
    every_lead = (0, 1, 2)
    whole_down = dot(activated, grad_down_rows, every_lead, every_lead)
    grad_hidden = gelu_pull(matmul_back(grad_down_rows, down_full))[0].astype(BF)
    whole_up = dot(mlp_in, grad_hidden, every_lead, every_lead)
    bias_up_grad = column_sum(grad_hidden)
    grad_mlp_in = images_scatter(matmul_back(grad_hidden, up_full))
    grad_from_mlp, gain_mlp_grad, shift_mlp_grad = mlp_norm_pull(grad_mlp_in)
    grad_resid_cross = grad_resid_out + grad_from_mlp

    grad_cross_low = grad_resid_cross.astype(BF)
    grad_cross_flat = grad_cross_low.reshape(all_tokens, D)
    whole_grads = {"cross_o": dot(cross_low, grad_cross_flat, (1,), (0,))}
    bias_cross_o_grad = column_sum(grad_cross_low)
    grad_cross_mixed = dot(cross_o_full, grad_cross_flat, (1,), (1,)).astype(BF)
    grad_cross_rows, grad_text, cross_head_grads = cross_attend_back(
        text_len, cross_rows, text_both, grad_cross_mixed.reshape(HEADS, HD, all_tokens),
        cross_total, own_cos, own_sin, cross_cols,
    )
    cross_head_grads = jnp.sum(cross_head_grads, axis=0)
    grad_cross_rows = grad_cross_rows.reshape(D, all_tokens)
    grad_cross_rows = moves.begin(
        grad_cross_rows,
        text=offload_sum(alone, grad_text.reshape(2 * D, img_count * text_count)),
    )
    whole_grads["cross_q"] = dot(cross_in.reshape(all_tokens, D), grad_cross_rows, (0,), (1,))
    bias_cross_q_grad = jnp.sum(grad_cross_rows.astype(F32), axis=1)
    grad_cross_in = dot(grad_cross_rows, cross_q_full, (0,), (1,))
    grad_from_cross, gain_cross_grad, shift_cross_grad = cross_norm_pull(
        grad_cross_in.reshape(img_count, tokens, D)
    )
    grad_resid_self = grad_resid_cross + grad_from_cross

    grad_out_rows = grad_resid_self.astype(BF)
    whole_grads["out"] = dot(attended_t, grad_out_rows, (0, 2), lead)
    bias_out_grad = column_sum(grad_out_rows)
    grad_attended = dot(out_full, grad_out_rows, (1,), (2,)).astype(BF)
    grad_attended = jnp.transpose(
        grad_attended.reshape(HEADS, HD, img_count, tokens), (0, 2, 1, 3)
    )
    grad_mixed_jobs = all_to_all(grad_attended.reshape(count, jobs, HD, tokens))
    grad_jobs, head_grads = attend_back(
        ext_jobs, qkv_jobs, grad_mixed_jobs, keep, total, every_cos, every_sin, head_cols, geo
    )
    grad_qkv_t = all_to_all(grad_jobs).reshape(HEADS, img_count, 3, HD, tokens)
    grad_qkv_t = jnp.transpose(grad_qkv_t, (2, 0, 3, 1, 4)).reshape(3 * D, img_count, tokens)
    head_grads = jnp.sum(head_grads, axis=0)

    for i, name in enumerate(("query", "key", "value")):
        whole_grads[name] = dot(normed, grad_qkv_t[i * D : (i + 1) * D], (0, 1), (1, 2))
    bias_qkv_grad = jnp.sum(grad_qkv_t.astype(F32), axis=(1, 2))
    grad_normed = dot(grad_qkv_t, qkv_full, (0,), (1,))
    grad_shift_rows = jnp.sum(grad_normed, axis=1)
    bias_shift_grad = jnp.sum(grad_shift_rows, axis=0)
    grad_from_self, gain_self_grad, shift_self_grad = self_norm_pull(grad_normed)
    grad_resid_in = grad_resid_self + grad_from_self
    grad_merged = grad_resid_in.astype(BF)
    whole_grads["skip"] = weight_grad(skip_in, grad_merged)
    bias_skip_grad = column_sum(grad_merged)
    grad_skip_normed = matmul_back(grad_merged, skip_full)
    grad_joined, skip_gain_grad, skip_shift_grad = skip_norm_pull(grad_skip_normed)
    grad_skip = grad_joined[..., D:].reshape(img_count, tile_rows, tile_cols, D)
    grad_embedded = grad_joined[..., :D].astype(BF)
    grad_embed_t = weight_grad(grad_embedded, near)
    bias_embed_grad = column_sum(grad_embedded)
    grad_near = matmul(grad_embedded, embed_t).reshape(
        img_count, tile_rows, tile_cols, near_vals
    )
    near_rim = with_halo(grad_near, (("row", 1), ("col", 2)), 1)
    grad_latents = spread_near(near_rim, tile_rows, tile_cols, patch_vals) * inside[..., None]

    moves.finish(*list(moves.running))
    shards = moves.done
    names = ("query", "key", "value", "skip", "out", "cross_q", "cross_o")
    packed = [whole_grads[name].astype(BF).reshape(count, -1, D) for name in names]
    packed_rows = sum(part.shape[1] for part in packed)
    fill = -packed_rows % (16 * groups)
    packed = jnp.pad(jnp.concatenate(packed, axis=1), ((0, 0), (0, fill), (0, 0)))
    up_rows = jnp.pad(
        whole_up.astype(BF).reshape(count, shard, -1), ((0, 0), (0, -shard % 16), (0, 0))
    )
    down_rows = whole_down.astype(BF).reshape(count, hid_part, D)
    summed, up_sums, down_sums = sum_everywhere(
        packed, down_rows, up_rows, (groups, row_count, col_count)
    )
    summed = summed.astype(F32)
    total_of, at = {}, 0
    for name in names:
        rows = whole_grads[name].shape[0] // count
        total_of[name] = summed[at : at + rows]
        at += rows
    grad_text_lin, head_gain_ck_grad, head_shift_ck_grad = text_pull(shards["text"])
    grad_text_low = grad_text_lin.astype(BF)
    grad_cross_keys = images_sum(
        dot(
            text_wide, grad_text_low.reshape(text_width, img_count, text_count), (0, 1), (1, 2)
        ),
        BF,
    )
    grad_cross_bias = images_sum(jnp.sum(grad_text_low.astype(F32), axis=1), F32)

    def by_device(vector):
        return vector.reshape(count, -1)

    def rows_by_device(rows):
        return jnp.transpose(rows.reshape(3, count, shard), (1, 0, 2)).reshape(count, -1)

    bias_up_all = jnp.where(
        (jnp.arange(groups) == group_index)[None, :, None],
        bias_up_grad.reshape(count, 1, hid_part),
        0.0,
    ).reshape(-1)
    small_grads = jnp.concatenate(
        [
            by_device(grad_embed_t),
            by_device(grad_final),
            rows_by_device(jnp.stack([gain_self_grad, gain_cross_grad, gain_mlp_grad])),
            rows_by_device(jnp.stack([shift_self_grad, shift_cross_grad, shift_mlp_grad])),
            by_device(skip_gain_grad),
            by_device(skip_shift_grad),
            by_device(
                jnp.concatenate(
                    [head_grads[:, 0], head_grads[:, 2], cross_head_grads[:, 0], head_gain_ck_grad]
                )
            ),
            by_device(
                jnp.concatenate(
                    [head_grads[:, 1], head_grads[:, 3], cross_head_grads[:, 1], head_shift_ck_grad]
                )
            ),
            by_device(
                jnp.concatenate([bias_embed_grad, bias_skip_grad, bias_shift_grad, bias_qkv_grad])
            ),
            by_device(
                jnp.concatenate(
                    [
                        bias_out_grad, bias_cross_q_grad, bias_cross_o_grad, bias_up_all,
                        bias_down_grad,
                    ]
                )
            ),
        ],
        axis=1,
    )
    shift_share = jnp.broadcast_to(grad_shift_rows.reshape(1, -1), (count, img_count * D))
    small_grads = jnp.concatenate([small_grads, shift_share], axis=1).astype(BF)
    small_grads = jnp.pad(small_grads, ((0, 0), (0, padded_len - small_grads.shape[1])))
    small_got = all_to_all(small_grads.reshape(count, -1, 128)).astype(F32)
    small_got = jnp.sum(small_got, axis=0).reshape(-1)
    small_sum = images_sum(small_got[:small_len], F32)
    total_parts = cuts(small_sum, (wide, wide) + small_widths)
    grad_shift = lax.dot_general(
        time_own.astype(F32),
        small_got[small_len : small_len + img_count * D].reshape(img_count, D),
        (((0,), (0,)), ((), ())),
        precision=lax.Precision.HIGHEST,
    )

    total_up = jnp.transpose(
        up_sums[:, :shard].reshape(groups, shard, count, hid_part), (1, 2, 0, 3)
    ).reshape(shard, FF)
    total_down = down_sums.reshape(hid_shard, D)
    return (
        out_latents,
        grad_latents,
        grad_skip,
        total_parts[0].reshape(shard, near_vals).T,
        total_of["skip"],
        images_sum(grad_shift, F32),
        jnp.concatenate([total_of[name] for name in ("query", "key", "value")], axis=1),
        total_of["out"],
        total_of["cross_q"],
        grad_cross_keys,
        total_of["cross_o"],
        total_up.astype(F32),
        total_down.astype(F32),
        total_parts[1].reshape(shard, near_vals),
        total_parts[2].reshape(3, shard),
        total_parts[3].reshape(3, shard),
        total_parts[4],
        total_parts[5],
        total_parts[6],
        total_parts[7],
        total_parts[8],
        total_parts[9],
        grad_cross_bias,
    )


def solution(mesh):
    tile = P("img", "row", "col", None)
    rows = P(GROUP, None)
    columns = P(None, GROUP)
    vector = P(GROUP)
    return jax.shard_map(
        body,
        mesh=mesh,
        in_specs=(
            tile, tile, P("img", None), P("img", None, None), P("img", None), P("img", None),
            columns, rows, rows, rows, rows, rows, columns, rows, rows, rows, rows,
            columns, columns, vector, vector, vector, vector, vector, vector, vector, tile,
        ),
        out_specs=(
            tile, tile, tile, columns, rows, rows, rows, rows, rows, columns, rows, rows, rows,
            rows, columns, columns, vector, vector, vector, vector, vector, vector, vector,
        ),
        check_vma=False,
    )
```

```python
import functools
import math
from typing import NamedTuple

import jax
import jax.numpy as jnp
import numpy as np
from jax import lax
from jax.experimental import pallas as pl
from jax.experimental.pallas import tpu as pltpu
from jax.sharding import PartitionSpec as P

D = 1408
HEADS = 16
HD = 88
FF = 6144
CLIP = 77
NORM_EPS = 1e-06
NEG_FILL = -1e30
STEPS = ((-1, -1), (-1, 0), (-1, 1), (0, -1), (0, 0), (0, 1), (1, -1), (1, 0), (1, 1))
GROUP = ("row", "col")
F32 = jnp.float32
BF = jnp.bfloat16
SCALE = 1.0 / math.sqrt(HD)
LOG2E = math.log2(math.e)
NT = (((1,), (1,)), ((), ()))
KEY_BLOCK = 256
QUERY_CHUNK = 1024


def with_halo(block, sides, width):
    for axis, dim in sides:
        count = lax.axis_size(axis)
        forward = [(i, i + 1) for i in range(count - 1)]
        backward = [(target, source) for source, target in forward]
        low = lax.ppermute(
            lax.slice_in_dim(block, block.shape[dim] - width, None, axis=dim), axis, forward
        )
        high = lax.ppermute(lax.slice_in_dim(block, 0, width, axis=dim), axis, backward)
        block = jnp.concatenate([low, block, high], axis=dim)
    return block


def dot(former, latter, former_dims, latter_dims):
    return lax.dot_general(
        former, latter, ((former_dims, latter_dims), ((), ())), preferred_element_type=F32
    )


def matmul(former, latter):
    return dot(former, latter, (former.ndim - 1,), (0,))


def matmul_back(former, latter):
    return dot(former, latter, (former.ndim - 1,), (1,))


def weight_grad(inputs, grads):
    lead = tuple(range(inputs.ndim - 1))
    return dot(inputs, grads, lead, lead)


def column_sum(grads):
    return jnp.sum(grads.astype(F32), axis=tuple(range(grads.ndim - 1)))


def layer_norm(values, scales, offsets):
    centre = values - jnp.mean(values, axis=-1, keepdims=True)
    spread = jnp.mean(centre * centre, axis=-1, keepdims=True)
    return centre * lax.rsqrt(spread + NORM_EPS) * scales + offsets


def angles_of(row_place, col_place):
    pair_index = np.arange(HD) // 2
    quarter = HD // 4
    within = np.where(pair_index < quarter, pair_index, pair_index - quarter).astype(np.float32)
    frequency = np.exp(np.float32(-math.log(10000.0)) * within / np.float32(quarter))
    by_row = jnp.asarray(pair_index < quarter)
    places = jnp.where(by_row[:, None], row_place[None, :], col_place[None, :])
    return places.astype(F32) * jnp.asarray(frequency.astype(np.float32))[:, None]


def gather_near(padded, tall, broad):
    return jnp.concatenate(
        [
            padded[..., 1 + step_row : 1 + step_row + tall, 1 + step_col : 1 + step_col + broad, :]
            for step_row, step_col in STEPS
        ],
        axis=-1,
    )


def spread_near(padded, tall, broad, channels):
    result = None
    for number, (step_row, step_col) in enumerate(STEPS):
        portion = padded[
            ...,
            1 - step_row : 1 - step_row + tall,
            1 - step_col : 1 - step_col + broad,
            number * channels : (number + 1) * channels,
        ]
        result = portion if result is None else result + portion
    return result


def cuts(vector, widths):
    ends = np.cumsum((0,) + widths)
    return [vector[..., ends[i] : ends[i + 1]] for i in range(len(widths))]


def swap_images(values, bit):
    count = lax.axis_size("img")
    return lax.ppermute(values, "img", [(i, i ^ bit) for i in range(count)])


def images_gather(values):
    blocks = values[None]
    while blocks.shape[0] < lax.axis_size("img"):
        blocks = jnp.concatenate([blocks, swap_images(blocks, blocks.shape[0])])
    return blocks


def images_scatter(parts):
    while parts.shape[0] > 1:
        half = parts.shape[0] // 2
        parts = parts[:half] + swap_images(parts[half:].astype(BF), half).astype(F32)
    return parts[0]


def images_sum(values, sent):
    bit = 1
    while bit < lax.axis_size("img"):
        values = values.astype(sent)
        values = values.astype(F32) + swap_images(values, bit).astype(F32)
        bit *= 2
    return values.astype(F32)


def exchange(values, axis, bit):
    if bit is None:
        return lax.psum_scatter(values, axis, scatter_dimension=0, tiled=True)
    size = lax.axis_size(axis)
    return lax.ppermute(values, axis, [(i, i ^ bit) for i in range(size)])


def halves(values, dim, bit):
    keep = lax.dynamic_index_in_dim(values, bit, dim, keepdims=False)
    return keep, lax.dynamic_index_in_dim(values, 1 - bit, dim, keepdims=False)


def core_features(values, dim, core):
    rows = lax.axis_size("row")
    block = values.shape[dim] // rows
    return jnp.concatenate(
        [
            lax.dynamic_slice_in_dim(values, (2 * i + core) * block, block, dim)
            for i in range(rows // 2)
        ],
        axis=dim,
    )


def row_first():
    rows, cols = lax.axis_size("row"), lax.axis_size("col")
    row_bits = [("row", 1 << i) for i in range(1, rows.bit_length() - 1)]
    return row_bits + [("col", 1 << i) for i in range(cols.bit_length() - 1)]


def shard_sum(order, after, inputs, grads, input_lead, grad_lead, feature):
    core = lax.axis_index("row") % 2
    give = dot(core_features(inputs, feature, 1 - core), grads, input_lead, grad_lead)
    (got,) = yield [give.astype(BF)], "row", 1
    keep = dot(core_features(inputs, feature, core), grads, input_lead, grad_lead)
    part = yield from scatter_sum(order, keep + got.astype(F32))
    part = yield from after(part)
    return part


def offload_sum(after, part):
    (got,) = yield [part.astype(BF)], GROUP, None
    part = yield from after(got.astype(F32))
    return part


def scatter_sum(order, part):
    dims = [d for d in reversed(row_first()) if d[0] == "row"]
    dims += [d for d in reversed(row_first()) if d[0] == "col"]
    width = part.shape[-1]
    part = part.reshape((2,) * len(dims) + (-1, width))
    for axis, bit in order:
        at = dims.index((axis, bit))
        keep, give = halves(part, at, lax.axis_index(axis) // bit % 2)
        del dims[at]
        (got,) = yield [give.astype(BF)], axis, bit
        part = keep + got.astype(F32)
    return part.reshape(-1, width)


def alone(part):
    return part
    yield


def all_images(part):
    bit, blocks = 1, part.astype(BF)[None]
    while bit < lax.axis_size("img"):
        (got,) = yield [blocks], "img", bit
        blocks = placed(blocks, got, lax.axis_index("img") // bit % 2, 0)
        blocks = blocks.reshape((-1,) + part.shape)
        bit *= 2
    return blocks


def placed(mine, other, bit, dim):
    first = lax.select(jnp.broadcast_to(bit == 0, mine.shape), mine, other)
    last = lax.select(jnp.broadcast_to(bit == 0, mine.shape), other, mine)
    return jnp.stack([first, last], axis=dim)


class Moves:
    def __init__(self):
        self.running = {}
        self.done = {}

    def begin(self, value, **makers):
        return self.launch(value, {name: (maker, next(maker)) for name, maker in makers.items()})

    def launch(self, value, wanted):
        if not wanted:
            return value
        gives = {name: request[0] for name, (_, request) in wanted.items()}
        value, gives = lax.optimization_barrier((value, gives))
        for name, (maker, (_, axis, bit)) in wanted.items():
            self.running[name] = (maker, [exchange(give, axis, bit) for give in gives[name]])
        return value

    def step(self, value, *names):
        names = [name for name in names if name in self.running]
        if not names:
            return value
        value, gots = lax.optimization_barrier(
            (value, {name: self.running[name][1] for name in names})
        )
        wanted = {}
        for name in names:
            maker = self.running.pop(name)[0]
            try:
                wanted[name] = (maker, maker.send(gots[name]))
            except StopIteration as stop:
                self.done[name] = stop.value
        return self.launch(value, wanted)

    def finish(self, *names):
        waiting = [name for name in names if name in self.running]
        while waiting:
            for name in waiting:
                maker, gots = self.running.pop(name)
                try:
                    gives, axis, bit = maker.send(gots)
                    self.running[name] = (maker, [exchange(give, axis, bit) for give in gives])
                except StopIteration as stop:
                    self.done[name] = stop.value
            waiting = [name for name in names if name in self.running]


def unit_rows(values):
    centre = values - jnp.mean(values, axis=0, keepdims=True)
    rstd = lax.rsqrt(jnp.mean(centre * centre, axis=0, keepdims=True) + NORM_EPS)
    return centre * rstd, rstd


def swap_pairs(values, back):
    rows = values.shape[0]
    even = lax.broadcasted_iota(jnp.int32, values.shape, 0) % 2 == 0
    up = pltpu.roll(values, rows - 1, 0)
    down = pltpu.roll(values, 1, 0)
    return jnp.where(even, up, -down) if back else jnp.where(even, -up, down)


def turn(values, cos, sin):
    return values * cos + swap_pairs(values, False) * sin


def turn_back(values, cos, sin):
    return values * cos + swap_pairs(values, True) * sin


def tiles(ref, part, count):
    return jnp.concatenate([ref[s, 0, part] for s in range(count)], axis=1)


def key_blocks(geo, ext_ref, job):
    count, tile_rows, tile_cols, col_tiles, block_tiles = geo
    rows = ext_ref[job, 0] // tile_rows
    groups = ext_ref[job, 1] // (block_tiles * tile_cols)

    def place(i):
        block = i // groups * (col_tiles // block_tiles) + i % groups
        return pl.multiple_of(block * KEY_BLOCK, KEY_BLOCK)

    return rows * groups, place


def attend_kernel(
    geo, ext_ref, qkv_ref, cos_ref, sin_ref, head_ref, out_ref, keep_ref, total_ref,
    q_s, kt_s, v_s, m_s, l_s,
):
    count = geo[0]
    cos, sin = cos_ref[...], sin_ref[...]
    unit, _ = unit_rows(tiles(qkv_ref, 0, count).astype(F32))
    q_s[...] = turn(unit * head_ref[:, 0:1] + head_ref[:, 1:2], cos, sin).astype(BF)
    unit, _ = unit_rows(tiles(qkv_ref, 1, count).astype(F32))
    kt_s[...] = turn(unit * head_ref[:, 2:3] + head_ref[:, 3:4], cos, sin).T.astype(BF)
    v_s[...] = tiles(qkv_ref, 2, count)
    block_count, place = key_blocks(geo, ext_ref, pl.program_id(0))
    width = q_s.shape[1]
    m_s[...] = jnp.full_like(m_s, NEG_FILL)
    l_s[...] = jnp.zeros_like(l_s)
    keep_ref[0] = jnp.zeros(keep_ref.shape[1:], F32)

    def key_step(i, carry):
        first = place(i)
        keys = kt_s[pl.ds(first, KEY_BLOCK), :]
        vals = v_s[:, pl.ds(first, KEY_BLOCK)]
        for part in range(width // QUERY_CHUNK):
            cut = slice(part * QUERY_CHUNK, (part + 1) * QUERY_CHUNK)
            scores = jnp.dot(keys, q_s[:, cut], preferred_element_type=F32)
            old = m_s[:, cut]
            new = jnp.maximum(old, jnp.max(scores, axis=0, keepdims=True))
            probs = jnp.exp2((scores - new) * (SCALE * LOG2E))
            factor = jnp.exp2((old - new) * (SCALE * LOG2E))
            m_s[:, cut] = new
            l_s[:, cut] = l_s[:, cut] * factor + jnp.sum(probs, axis=0, keepdims=True)
            keep_ref[0, :, cut] = keep_ref[0, :, cut] * factor + jnp.dot(
                vals, probs.astype(BF), preferred_element_type=F32
            )
        return carry

    lax.fori_loop(0, block_count, key_step, 0)
    total_ref[0] = m_s[...] * (SCALE * LOG2E) + jnp.log2(l_s[...])
    mixed = keep_ref[0] / l_s[...]
    keep_ref[0] = mixed
    low = mixed.astype(BF)
    tile = width // count
    for s in range(count):
        out_ref[s, 0] = low[:, s * tile : (s + 1) * tile]


def attend(ext_jobs, qkv, cos, sin, head, geo):
    count, jobs, _, _, tile = qkv.shape
    width = count * tile
    work = 4 * jobs * width * width * HD
    return pl.pallas_call(
        functools.partial(attend_kernel, geo),
        grid=(jobs,),
        in_specs=[
            pl.BlockSpec(memory_space=pltpu.SMEM),
            pl.BlockSpec((count, 1, 3, HD, tile), lambda j: (0, j, 0, 0, 0)),
            pl.BlockSpec((HD, width), lambda j: (0, 0)),
            pl.BlockSpec((HD, width), lambda j: (0, 0)),
            pl.BlockSpec((HD, 4), lambda j: (0, 0)),
        ],
        out_specs=[
            pl.BlockSpec((count, 1, HD, tile), lambda j: (0, j, 0, 0)),
            pl.BlockSpec((1, HD, width), lambda j: (j, 0, 0)),
            pl.BlockSpec((1, 1, width), lambda j: (j, 0, 0)),
        ],
        out_shape=[
            jax.ShapeDtypeStruct((count, jobs, HD, tile), BF),
            jax.ShapeDtypeStruct((jobs, HD, width), F32),
            jax.ShapeDtypeStruct((jobs, 1, width), F32),
        ],
        scratch_shapes=[
            pltpu.VMEM((HD, width), BF),
            pltpu.VMEM((width, HD), BF),
            pltpu.VMEM((HD, width), BF),
            pltpu.VMEM((1, width), F32),
            pltpu.VMEM((1, width), F32),
        ],
        compiler_params=pltpu.CompilerParams(vmem_limit_bytes=48 * 2**20),
        cost_estimate=pl.CostEstimate(
            flops=3 * work, bytes_accessed=6 * 2**20, transcendentals=jobs * width * width
        ),
    )(ext_jobs, qkv, cos, sin, head)


def attend_back_kernel(
    geo, ext_ref, qkv_ref, dout_ref, keep_ref, total_ref, cos_ref, sin_ref, head_ref,
    grad_ref, head_grad_ref, q_s, k_s, kt_s, vt_s, do_s, delta_s, dq_s, dk_s, dv_s,
):
    count = geo[0]
    cos, sin = cos_ref[...], sin_ref[...]
    unit, _ = unit_rows(tiles(qkv_ref, 0, count).astype(F32))
    q_s[...] = turn(unit * head_ref[:, 0:1] + head_ref[:, 1:2], cos, sin).astype(BF)
    unit, _ = unit_rows(tiles(qkv_ref, 1, count).astype(F32))
    keys = turn(unit * head_ref[:, 2:3] + head_ref[:, 3:4], cos, sin)
    k_s[...] = keys.astype(BF)
    kt_s[...] = keys.T.astype(BF)
    vt_s[...] = tiles(qkv_ref, 2, count).astype(F32).T.astype(BF)
    dout = jnp.concatenate([dout_ref[s, 0] for s in range(count)], axis=1)
    do_s[...] = dout
    delta_s[...] = jnp.sum(dout.astype(F32) * keep_ref[0], axis=0, keepdims=True)
    block_count, place = key_blocks(geo, ext_ref, pl.program_id(0))
    width = q_s.shape[1]
    dq_s[...] = jnp.zeros_like(dq_s)
    dk_s[...] = jnp.zeros_like(dk_s)
    dv_s[...] = jnp.zeros_like(dv_s)

    def key_step(i, carry):
        first = place(i)
        keys_t = kt_s[pl.ds(first, KEY_BLOCK), :]
        vals_t = vt_s[pl.ds(first, KEY_BLOCK), :]
        keys_n = k_s[:, pl.ds(first, KEY_BLOCK)]
        dk = jnp.zeros((HD, KEY_BLOCK), F32)
        dv = jnp.zeros((HD, KEY_BLOCK), F32)
        for part in range(width // QUERY_CHUNK):
            cut = slice(part * QUERY_CHUNK, (part + 1) * QUERY_CHUNK)
            queries = q_s[:, cut]
            douts = do_s[:, cut]
            scores = jnp.dot(keys_t, queries, preferred_element_type=F32)
            probs = jnp.exp2(scores * (SCALE * LOG2E) - total_ref[0, :, cut])
            dprob = jnp.dot(vals_t, douts, preferred_element_type=F32)
            dscore = (probs * (dprob - delta_s[:, cut])).astype(BF)
            dv = dv + lax.dot_general(douts, probs.astype(BF), NT, preferred_element_type=F32)
            dk = dk + lax.dot_general(queries, dscore, NT, preferred_element_type=F32)
            dq_s[:, cut] += jnp.dot(keys_n, dscore, preferred_element_type=F32)
        dk_s[:, pl.ds(first, KEY_BLOCK)] = dk
        dv_s[:, pl.ds(first, KEY_BLOCK)] = dv
        return carry

    lax.fori_loop(0, block_count, key_step, 0)
    tile = width // count

    def lift(part, turned, at):
        unit, rstd = unit_rows(tiles(qkv_ref, part, count).astype(F32))
        dy = turn_back(turned * SCALE, cos, sin)
        head_grad_ref[0, :, at : at + 1] = jnp.sum(dy * unit, axis=1, keepdims=True)
        head_grad_ref[0, :, at + 1 : at + 2] = jnp.sum(dy, axis=1, keepdims=True)
        dunit = dy * head_ref[:, at : at + 1]
        along = jnp.mean(dunit * unit, axis=0, keepdims=True)
        dx = (dunit - jnp.mean(dunit, axis=0, keepdims=True) - unit * along) * rstd
        low = dx.astype(BF)
        for s in range(count):
            grad_ref[s, 0, part] = low[:, s * tile : (s + 1) * tile]

    lift(0, dq_s[...], 0)
    lift(1, dk_s[...], 2)
    low = dv_s[...].astype(BF)
    for s in range(count):
        grad_ref[s, 0, 2] = low[:, s * tile : (s + 1) * tile]


def attend_back(ext_jobs, qkv, dout, keep, total, cos, sin, head, geo):
    count, jobs, _, _, tile = qkv.shape
    width = count * tile
    work = 10 * jobs * width * width * HD
    return pl.pallas_call(
        functools.partial(attend_back_kernel, geo),
        grid=(jobs,),
        in_specs=[
            pl.BlockSpec(memory_space=pltpu.SMEM),
            pl.BlockSpec((count, 1, 3, HD, tile), lambda j: (0, j, 0, 0, 0)),
            pl.BlockSpec((count, 1, HD, tile), lambda j: (0, j, 0, 0)),
            pl.BlockSpec((1, HD, width), lambda j: (j, 0, 0)),
            pl.BlockSpec((1, 1, width), lambda j: (j, 0, 0)),
            pl.BlockSpec((HD, width), lambda j: (0, 0)),
            pl.BlockSpec((HD, width), lambda j: (0, 0)),
            pl.BlockSpec((HD, 4), lambda j: (0, 0)),
        ],
        out_specs=[
            pl.BlockSpec((count, 1, 3, HD, tile), lambda j: (0, j, 0, 0, 0)),
            pl.BlockSpec((1, HD, 4), lambda j: (j, 0, 0)),
        ],
        out_shape=[
            jax.ShapeDtypeStruct((count, jobs, 3, HD, tile), BF),
            jax.ShapeDtypeStruct((jobs, HD, 4), F32),
        ],
        scratch_shapes=[
            pltpu.VMEM((HD, width), BF),
            pltpu.VMEM((HD, width), BF),
            pltpu.VMEM((width, HD), BF),
            pltpu.VMEM((width, HD), BF),
            pltpu.VMEM((HD, width), BF),
            pltpu.VMEM((1, width), F32),
            pltpu.VMEM((HD, width), F32),
            pltpu.VMEM((HD, width), F32),
            pltpu.VMEM((HD, width), F32),
        ],
        compiler_params=pltpu.CompilerParams(vmem_limit_bytes=56 * 2**20),
        cost_estimate=pl.CostEstimate(
            flops=3 * work, bytes_accessed=8 * 2**20, transcendentals=jobs * width * width
        ),
    )(ext_jobs, qkv, dout, keep, total, cos, sin, head)


TN = (((0,), (0,)), ((), ()))
CROSS_HEADS = 2


def text_scores(len_ref, keys, queries, image):
    scores = lax.dot_general(keys, queries, TN, preferred_element_type=F32) * (SCALE * LOG2E)
    place = lax.broadcasted_iota(jnp.int32, scores.shape, 0)
    live = (place < len_ref[image, 0]) | (
        (place >= CLIP) & (place < CLIP + len_ref[image, 1])
    )
    return jnp.where(live, scores, NEG_FILL)


def cross_kernel(images, len_ref, rows_ref, text_ref, cos_ref, sin_ref, head_ref, out_ref, total_ref):
    tile = rows_ref.shape[2] // images
    slots = text_ref.shape[3] // images
    for h in range(CROSS_HEADS):
        unit, _ = unit_rows(rows_ref[h])
        queries = turn(unit * head_ref[:, 0:1] + head_ref[:, 1:2], cos_ref[...], sin_ref[...])
        queries = queries.astype(BF)
        for i in range(images):
            own, slot = slice(i * tile, (i + 1) * tile), slice(i * slots, (i + 1) * slots)
            scores = text_scores(len_ref, text_ref[0, h, :, slot], queries[:, own], i)
            top = jnp.max(scores, axis=0, keepdims=True)
            probs = jnp.exp2(scores - top)
            weight = jnp.sum(probs, axis=0, keepdims=True)
            low = (probs / weight).astype(BF)
            mixed = jnp.dot(text_ref[1, h, :, slot], low, preferred_element_type=F32)
            out_ref[h, :, own] = mixed.astype(BF)
            total_ref[h, :, own] = top + jnp.log2(weight)


def cross_back_kernel(
    images, len_ref, rows_ref, text_ref, dout_ref, total_ref, cos_ref, sin_ref, head_ref,
    grad_ref, text_grad_ref, head_grad_ref,
):
    tile = rows_ref.shape[2] // images
    slots = text_ref.shape[3] // images
    cos, sin = cos_ref[...], sin_ref[...]
    gain_grad = jnp.zeros((HD, 1), F32)
    shift_grad = jnp.zeros((HD, 1), F32)
    for h in range(CROSS_HEADS):
        unit, rstd = unit_rows(rows_ref[h])
        queries = turn(unit * head_ref[:, 0:1] + head_ref[:, 1:2], cos, sin).astype(BF)
        turned = []
        for i in range(images):
            own, slot = slice(i * tile, (i + 1) * tile), slice(i * slots, (i + 1) * slots)
            keys = text_ref[0, h, :, slot]
            douts = dout_ref[h, :, own]
            scores = text_scores(len_ref, keys, queries[:, own], i)
            probs = jnp.exp2(scores - total_ref[h, :, own])
            dprob = lax.dot_general(
                text_ref[1, h, :, slot], douts, TN, preferred_element_type=F32
            )
            delta = jnp.sum(probs * dprob, axis=0, keepdims=True)
            dscore = (probs * (dprob - delta)).astype(BF)
            low = probs.astype(BF)
            dkeys = lax.dot_general(queries[:, own], dscore, NT, preferred_element_type=F32)
            text_grad_ref[0, h, :, slot] = (dkeys * SCALE).astype(BF)
            text_grad_ref[1, h, :, slot] = lax.dot_general(
                douts, low, NT, preferred_element_type=F32
            ).astype(BF)
            turned.append(jnp.dot(keys, dscore, preferred_element_type=F32))
        dy = turn_back(jnp.concatenate(turned, axis=1) * SCALE, cos, sin)
        gain_grad += jnp.sum(dy * unit, axis=1, keepdims=True)
        shift_grad += jnp.sum(dy, axis=1, keepdims=True)
        dunit = dy * head_ref[:, 0:1]
        along_unit = jnp.mean(dunit * unit, axis=0, keepdims=True)
        dx = (dunit - jnp.mean(dunit, axis=0, keepdims=True) - unit * along_unit) * rstd
        grad_ref[h] = dx.astype(BF)
    head_grad_ref[0, :, 0:1] = gain_grad
    head_grad_ref[0, :, 1:2] = shift_grad


def cross_specs(width, slots):
    return dict(
        smem=pl.BlockSpec(memory_space=pltpu.SMEM),
        rows=pl.BlockSpec((CROSS_HEADS, HD, width), lambda h: (h, 0, 0)),
        text=pl.BlockSpec((2, CROSS_HEADS, HD, slots), lambda h: (0, h, 0, 0)),
        table=pl.BlockSpec((HD, width), lambda h: (0, 0)),
        head=pl.BlockSpec((HD, 2), lambda h: (0, 0)),
        total=pl.BlockSpec((CROSS_HEADS, 1, width), lambda h: (h, 0, 0)),
        head_grad=pl.BlockSpec((1, HD, 2), lambda h: (h, 0, 0)),
    )


def cross_attend(lengths, rows, text, cos, sin, head):
    heads, _, width = rows.shape
    slots = text.shape[3]
    sp = cross_specs(width, slots)
    return pl.pallas_call(
        functools.partial(cross_kernel, lengths.shape[0]),
        grid=(heads // CROSS_HEADS,),
        in_specs=[sp["smem"], sp["rows"], sp["text"], sp["table"], sp["table"], sp["head"]],
        out_specs=[sp["rows"], sp["total"]],
        out_shape=[
            jax.ShapeDtypeStruct((heads, HD, width), BF),
            jax.ShapeDtypeStruct((heads, 1, width), F32),
        ],
        compiler_params=pltpu.CompilerParams(vmem_limit_bytes=32 * 2**20),
        cost_estimate=pl.CostEstimate(
            flops=2**32, bytes_accessed=10 * 2**20, transcendentals=heads * width * slots
        ),
    )(lengths, rows, text, cos, sin, head)


def cross_attend_back(lengths, rows, text, dout, total, cos, sin, head):
    heads, _, width = rows.shape
    slots = text.shape[3]
    sp = cross_specs(width, slots)
    return pl.pallas_call(
        functools.partial(cross_back_kernel, lengths.shape[0]),
        grid=(heads // CROSS_HEADS,),
        in_specs=[
            sp["smem"], sp["rows"], sp["text"], sp["rows"], sp["total"], sp["table"], sp["table"],
            sp["head"],
        ],
        out_specs=[sp["rows"], sp["text"], sp["head_grad"]],
        out_shape=[
            jax.ShapeDtypeStruct((heads, HD, width), BF),
            jax.ShapeDtypeStruct((2, heads, HD, slots), BF),
            jax.ShapeDtypeStruct((heads // CROSS_HEADS, HD, 2), F32),
        ],
        compiler_params=pltpu.CompilerParams(vmem_limit_bytes=32 * 2**20),
        cost_estimate=pl.CostEstimate(
            flops=2**33, bytes_accessed=16 * 2**20, transcendentals=heads * width * slots
        ),
    )(lengths, rows, text, dout, total, cos, sin, head)


MESH = pl.DeviceIdType.MESH
LAG = 3
ROW_SHARE = 5


class Kind(NamedTuple):
    operand: int
    first_row: int
    width: int
    height: int
    chunks: int
    stride: int
    order: tuple


def sum_plan(sizes, kind):
    groups, row_count, cols = sizes
    count, height = row_count * cols // 2, kind.height
    firsts = {"img": (0, groups), "row": (1, row_count), "col": (0, cols)}
    plan = []
    for axis, i in [
        (axis, i)
        for axis in kind.order
        for i in range(firsts[axis][0], firsts[axis][1].bit_length() - 1)
    ]:
        bit = 1 << i
        if axis == "img":
            height //= 2
        else:
            count //= 2
        plan.append((axis, bit, count, height))
    return plan


def sum_kernel(sizes, kinds, *refs):
    groups, row_count, cols = sizes
    number = 1 + max(kind.operand for kind in kinds)
    grads_refs, out_refs, scratch = refs[:number], refs[number : 2 * number], refs[2 * number :]
    first_count = row_count * cols // 2
    places = {axis: lax.axis_index(axis) for axis in ("img", "row", "col")}
    plans = [sum_plan(sizes, kind) for kind in kinds]
    image_stages = groups.bit_length() - 1
    held, own, sems = [], [], []
    at = 0
    for plan in plans:
        held.append(scratch[at : at + len(plan) + 1])
        own.append(scratch[at + len(plan) + 1])
        sems.append(scratch[at + len(plan) + 2 : at + len(plan) + 8])
        at += len(plan) + 8
    core = places["row"] % 2

    def device_of(place):
        return tuple(place[name] for name in ("img", "row", "col"))

    def partner(axis, bit):
        place = dict(places)
        part = place[axis] // bit % 2
        place[axis] = place[axis] + bit - 2 * bit * part
        return device_of(place)

    def other_images():
        for i in range(1, groups):
            place = dict(places)
            place["img"] = lax.rem(places["img"] + i, groups)
            yield i, device_of(place)

    def bit_of(axis, bit):
        return places[axis] // bit % 2

    def chunk_rows(k, chunk):
        return pl.multiple_of(kinds[k].first_row + chunk * kinds[k].height, 16)

    def first_copies(k, chunk):
        rows = pl.ds(chunk_rows(k, chunk), kinds[k].height)
        for i in range(row_count // 2):
            shards = pl.ds((2 * i + 1 - core) * cols, cols)
            yield pltpu.make_async_remote_copy(
                src_ref=grads_refs[kinds[k].operand].at[shards, rows],
                dst_ref=held[k][0].at[chunk, pl.ds(i * cols, cols)],
                send_sem=sems[k][0].at[0, chunk],
                recv_sem=sems[k][1].at[0, chunk],
                device_id=partner("row", 1),
                device_id_type=MESH,
            )

    def own_copies(k, chunk):
        rows = pl.ds(chunk_rows(k, chunk), kinds[k].height)
        for i in range(row_count // 2):
            shards = pl.ds((2 * i + core) * cols, cols)
            yield pltpu.make_async_copy(
                grads_refs[kinds[k].operand].at[shards, rows],
                own[k].at[lax.rem(chunk, 2), pl.ds(i * cols, cols)],
                sems[k][4].at[lax.rem(chunk, 2)],
            )

    def split(k, stage):
        axis, bit, count, rows = plans[k][stage]
        part = bit_of(axis, bit)
        if axis == "img":
            give = pl.ds(pl.multiple_of((1 - part) * rows, 16), rows)
            keep = pl.ds(pl.multiple_of(part * rows, 16), rows)
            return [((pl.ds(0, count), give), pl.ds(0, count))], lambda i: (i, keep)
        every = pl.ds(0, rows)
        if axis == "row":
            give = pl.ds((1 - part) * count, count)
            return [((give, every), pl.ds(0, count))], lambda i: (part * count + i, every)
        return (
            [((pl.ds(2 * i + 1 - part, 1), every), pl.ds(i, 1)) for i in range(count)],
            lambda i: (2 * i + part, every),
        )

    def stage_copies(k, stage, chunk):
        axis, bit, _, _ = plans[k][stage]
        for (shards, lines), target in split(k, stage)[0]:
            yield pltpu.make_async_remote_copy(
                src_ref=held[k][stage].at[chunk, shards, lines],
                dst_ref=held[k][stage + 1].at[chunk, target],
                send_sem=sems[k][0].at[stage + 1, chunk],
                recv_sem=sems[k][1].at[stage + 1, chunk],
                device_id=partner(axis, bit),
                device_id_type=MESH,
            )

    def whole(k, stage, chunk):
        buffer = held[k][stage].at[chunk]
        return pltpu.make_async_remote_copy(
            src_ref=buffer,
            dst_ref=buffer,
            send_sem=sems[k][0].at[stage, chunk],
            recv_sem=sems[k][1].at[stage, chunk],
            device_id=partner("row", 1),
            device_id_type=MESH,
        )

    def home(k, chunk):
        rows = plans[k][-1][3]
        out_ref = out_refs[kinds[k].operand]
        if "img" not in kinds[k].order:
            return out_ref.at[places["img"], pl.ds(chunk_rows(k, chunk), rows)]
        place = 0
        for i in range(image_stages):
            place = place + bit_of("img", 1 << i) * (1 << (image_stages - 1 - i))
        return out_ref.at[pl.ds(pl.multiple_of(chunk_rows(k, chunk) + place * rows, 16), rows)]

    def spread_copies(k, chunk):
        for i, other in other_images():
            yield pltpu.make_async_remote_copy(
                src_ref=held[k][-1].at[chunk, 0],
                dst_ref=home(k, chunk),
                send_sem=sems[k][2].at[i, chunk],
                recv_sem=sems[k][3].at[i, chunk],
                device_id=other,
                device_id_type=MESH,
            )

    def home_copy(k, chunk):
        return pltpu.make_async_copy(
            held[k][-1].at[chunk, 0], home(k, chunk), sems[k][5].at[chunk]
        )

    def start(copies):
        for copy in copies:
            copy.start()

    def begin(k, chunk):
        start(first_copies(k, chunk))
        start(own_copies(k, chunk))

    barrier = pltpu.get_barrier_semaphore()
    near = [partner("row", 1)] + [partner(a, b) for a, b, _, _ in plans[0] if a != "img"]
    near += [other for _, other in other_images()]
    for other in near:
        pl.semaphore_signal(barrier, inc=1, device_id=other, device_id_type=MESH)
    pl.semaphore_wait(barrier, len(near))

    for k in range(len(kinds)):
        begin(k, 0)

    def advance(k, stage, chunk):
        if stage == 0:

            @pl.when(chunk + 1 < kinds[k].chunks)
            def _():
                begin(k, chunk + 1)

        buffer = held[k][stage]
        whole(k, stage, chunk).wait_recv()
        if stage == 0:
            count = first_count
            for copy in own_copies(k, chunk):
                copy.wait()

            def mine(i):
                return own[k][lax.rem(chunk, 2), i]
        else:
            count = plans[k][stage - 1][2]
            kept = split(k, stage - 1)[1]

            def mine(i):
                shard, lines = kept(i)
                return held[k][stage - 1][chunk, shard, lines]

        def add(i, carry):
            both = buffer[chunk, i].astype(F32) + mine(i).astype(F32)
            buffer[chunk, i] = both.astype(BF)
            return carry

        lax.fori_loop(0, count, add, 0)
        if stage < len(plans[k]):
            start(stage_copies(k, stage, chunk))
        else:
            start(spread_copies(k, chunk))
            home_copy(k, chunk).start()

    def time_step(t, carry):
        for stage in range(max(len(plan) for plan in plans), -1, -1):
            for k, kind in enumerate(kinds):
                if stage <= len(plans[k]):
                    since = t - LAG * stage
                    chunk = since // kind.stride
                    due = jnp.logical_and(since >= 0, since % kind.stride == 0)

                    @pl.when(jnp.logical_and(due, chunk < kind.chunks))
                    def _(k=k, stage=stage, chunk=chunk):
                        advance(k, stage, chunk)

        return carry

    last = max(k.stride * k.chunks + LAG * len(plan) for k, plan in zip(kinds, plans))
    lax.fori_loop(0, last, time_step, 0)

    for k, kind in enumerate(kinds):

        def drain(chunk, carry, k=k):
            for stage in range(len(plans[k]) + 1):
                whole(k, stage, chunk).wait_send()
            for copy in spread_copies(k, chunk):
                copy.wait()
            home_copy(k, chunk).wait()
            return carry

        lax.fori_loop(0, kind.chunks, drain, 0)


def sum_everywhere(projections, down, up, sizes):
    groups, row_count, cols = sizes
    first_count = row_count * cols // 2
    height = 16 * groups
    chunks = projections.shape[1] // height
    late = max(1, chunks * ROW_SHARE // 22)
    early = chunks - late
    kinds = [
        Kind(0, 0, D, height, early, 1, ("img", "row", "col")),
        Kind(0, early * height, D, height, late, 3, ("row", "img", "col")),
        Kind(1, 0, up.shape[2], 16, up.shape[1] // 16, 3, ("row", "col")),
        Kind(2, 0, D, 16, down.shape[1] // 16, 1, ("col", "row")),
    ]
    scratch = []
    for kind in kinds:
        plan = sum_plan(sizes, kind)
        shapes = [(first_count, kind.height)] + [(c, h) for _, _, c, h in plan]
        scratch += [pltpu.VMEM((kind.chunks, c, h, kind.width), BF) for c, h in shapes]
        scratch.append(pltpu.VMEM((2, first_count, kind.height, kind.width), BF))
        stage_sems = pltpu.SemaphoreType.DMA((len(plan) + 1, kind.chunks))
        spread_sems = pltpu.SemaphoreType.DMA((groups, kind.chunks))
        scratch += [
            stage_sems, stage_sems, spread_sems, spread_sems,
            pltpu.SemaphoreType.DMA((2,)), pltpu.SemaphoreType.DMA((kind.chunks,)),
        ]
    space = pl.BlockSpec(memory_space=pl.ANY)
    return pl.pallas_call(
        functools.partial(sum_kernel, sizes, kinds),
        out_shape=[
            jax.ShapeDtypeStruct(projections.shape[1:], BF),
            jax.ShapeDtypeStruct((groups,) + up.shape[1:], BF),
            jax.ShapeDtypeStruct((groups,) + down.shape[1:], BF),
        ],
        in_specs=[space] * 3,
        out_specs=[space] * 3,
        scratch_shapes=scratch,
        compiler_params=pltpu.CompilerParams(
            collective_id=1, has_side_effects=True, vmem_limit_bytes=58 * 2**20
        ),
        cost_estimate=pl.CostEstimate(flops=2**28, bytes_accessed=2**28, transcendentals=0),
    )(projections, up, down)


def all_to_all(values):
    return lax.all_to_all(values, GROUP, split_axis=0, concat_axis=0, tiled=True)


def body(
    latents, skip, temb, text, text_len, extent, embed_weight, skip_weight, shift_weight,
    qkv_weight, out_weight, cross_query, cross_keys, cross_out, up_weight, down_weight,
    final_weight, norm_gain, norm_shift, skip_gain, skip_shift, head_gain, head_shift,
    front_biases, all_biases, cross_bias, cotangent,
):
    img_count, tile_rows, tile_cols, patch_vals = latents.shape
    tokens = tile_rows * tile_cols
    near_vals = 9 * patch_vals
    row_count = lax.axis_size("row")
    col_count = lax.axis_size("col")
    count = row_count * col_count
    groups = lax.axis_size("img")
    jobs = img_count * HEADS // count
    row_index = lax.axis_index("row")
    col_index = lax.axis_index("col")
    group_index = lax.axis_index("img")
    device = row_index * col_count + col_index
    shard = D // count
    hid_shard = FF // count
    hid_part = hid_shard // groups

    small_widths = (
        norm_gain.size, norm_shift.size, skip_gain.size, skip_shift.size,
        head_gain.size, head_shift.size, front_biases.size, all_biases.size,
    )
    small = jnp.concatenate(
        [
            embed_weight.T.reshape(-1), final_weight.reshape(-1), norm_gain.reshape(-1),
            norm_shift.reshape(-1), skip_gain, skip_shift, head_gain, head_shift,
            front_biases, all_biases,
        ]
    )
    small_len = small.size
    padded_len = -(-(small_len + img_count * D) // 2048) * 2048
    time_act = jax.nn.silu(temb.astype(F32)).astype(BF)
    time_own = lax.dynamic_slice_in_dim(time_act, device * shard, shard, 1)
    shift_share = matmul(time_own, shift_weight).astype(BF).reshape(-1)
    small = jnp.pad(jnp.concatenate([small, shift_share]), (0, padded_len - small_len - shift_share.size))
    small_all = all_to_all(jnp.broadcast_to(small.reshape(1, -1, 128), (count, padded_len // 128, 128)))
    small_all = small_all.reshape(count, padded_len)
    def beside(values, parts):
        return jnp.concatenate(jnp.split(values, parts, axis=0), axis=1)

    def below(values, parts):
        width = values.shape[1] // parts
        blocks = [values[:, i * width : (i + 1) * width] for i in range(parts)]
        return jnp.stack([b.reshape(count, -1, width) for b in blocks], axis=1).reshape(-1, width)

    first_all = lax.all_gather(
        jnp.concatenate([beside(skip_weight, 2), qkv_weight], axis=1), GROUP, axis=0, tiled=True
    )
    skip_full = below(first_all[:, : 2 * D], 2)
    qkv_full = first_all[:, 2 * D :]
    folds = hid_part // shard
    fold_rows = hid_part // folds
    up_part = lax.dynamic_index_in_dim(
        up_weight.reshape(shard, count, groups, hid_part), group_index, 2, keepdims=False
    ).reshape(shard, count * hid_part)
    down_part = lax.dynamic_index_in_dim(
        down_weight.reshape(groups, hid_part, D), group_index, 0, keepdims=False
    )
    third = jnp.concatenate(
        [jnp.pad(up_part, ((0, fold_rows - shard), (0, 0))), beside(down_part, folds)], axis=1
    )

    wide = shard * near_vals
    embed_t = small_all[:, :wide].reshape(D, near_vals)
    final_full = small_all[:, wide : 2 * wide].reshape(D, near_vals)
    vectors = cuts(small_all[:, 2 * wide : small_len].astype(F32), small_widths)
    gain_rows = jnp.transpose(vectors[0].reshape(count, 3, shard), (1, 0, 2)).reshape(3, D)
    offset_rows = jnp.transpose(vectors[1].reshape(count, 3, shard), (1, 0, 2)).reshape(3, D)
    skip_gains, skip_offsets = vectors[2].reshape(-1), vectors[3].reshape(-1)
    head_gains, head_offsets = vectors[4].reshape(4, HD), vectors[5].reshape(4, HD)
    bias_embed, bias_skip, bias_shift, bias_qkv = cuts(vectors[6].reshape(-1), (D, D, D, 3 * D))
    bias_out, bias_cross_q, bias_cross_o, bias_up, bias_down = cuts(
        vectors[7].reshape(-1), (D, D, D, FF, D)
    )
    bias_up_part = lax.dynamic_index_in_dim(
        bias_up.reshape(count, groups, hid_part), group_index, 1, keepdims=False
    ).reshape(-1)

    local_rows = row_index * tile_rows + jnp.arange(tile_rows, dtype=jnp.int32)
    local_cols = col_index * tile_cols + jnp.arange(tile_cols, dtype=jnp.int32)
    inside = (
        (local_rows[None, :, None] < extent[:, 0, None, None])
        & (local_cols[None, None, :] < extent[:, 1, None, None])
    ).astype(F32)
    token_inside = inside.reshape(img_count, tokens, 1)
    own_angle = angles_of(
        jnp.tile(jnp.repeat(local_rows, tile_cols), img_count),
        jnp.tile(jnp.tile(local_cols, tile_rows), img_count),
    )
    own_cos, own_sin = jnp.cos(own_angle), jnp.sin(own_angle)
    every = np.arange(count * tokens)
    every_row = every // tokens // col_count * tile_rows + every % tokens // tile_cols
    every_col = every // tokens % col_count * tile_cols + every % tile_cols
    every_angle = angles_of(jnp.asarray(every_row), jnp.asarray(every_col))
    every_cos, every_sin = jnp.cos(every_angle), jnp.sin(every_angle)
    job_images = (device * jobs + jnp.arange(jobs, dtype=jnp.int32)) % img_count
    ext_jobs = jnp.take(extent, job_images, axis=0)
    geo = (count, tile_rows, tile_cols, col_count, KEY_BLOCK // tokens)

    def gelu_tanh(values):
        return jax.nn.gelu(values, approximate=True)

    text_width = cross_keys.shape[1]
    text_count = -(-text.shape[1] // 128) * 128
    text_wide = jnp.pad(text, ((0, 0), (0, text_count - text.shape[1]), (0, 0)))
    is_key = device * text_width + jnp.arange(text_width, dtype=jnp.int32) < D

    def text_norm(values, scales, offsets):
        per_head = values.reshape(text_width // HD, HD, -1)
        centre = per_head - jnp.mean(per_head, axis=1, keepdims=True)
        spread = jnp.mean(centre * centre, axis=1, keepdims=True)
        unit = centre * lax.rsqrt(spread + NORM_EPS) * scales[:, None] + offsets[:, None]
        return jnp.where(is_key[:, None], unit.reshape(values.shape), values)

    text_part = dot(cross_keys, text_wide, (0,), (2,)).reshape(text_width, -1)
    text_part = text_part + cross_bias.astype(F32)[:, None]
    text_normed, text_pull = jax.vjp(text_norm, text_part, head_gains[3], head_offsets[3])
    moves = Moves()
    even_group = group_index % 2 == 0
    second_all = lax.all_gather(
        jnp.concatenate(
            [
                out_weight,
                lax.select(jnp.broadcast_to(even_group, cross_out.shape), cross_query, cross_out),
                beside(text_normed.astype(BF), 2),
            ],
            axis=1,
        ),
        GROUP,
        axis=0,
        tiled=True,
    )
    out_full, cross_mine = second_all[:, :D], second_all[:, D : 2 * D]
    cross_other = exchange(cross_mine, "img", 1)
    choose = jnp.broadcast_to(even_group, cross_mine.shape)
    cross_q_full = lax.select(choose, cross_mine, cross_other)
    cross_o_full = lax.select(choose, cross_other, cross_mine)
    text_both = below(second_all[:, 2 * D :], 2).reshape(2, HEADS, HD, img_count * text_count)
    third_all = lax.all_gather(third, GROUP, axis=0, tiled=True)
    third_rows = third_all.reshape(count, fold_rows, -1)
    up_full = third_rows[:, :shard, : count * hid_part].reshape(D, count * hid_part)
    down_full = below(third_all[:, count * hid_part :], folds)
    shift_sums = small_all[:, small_len : small_len + img_count * D].astype(F32)
    shift_rows = jnp.sum(shift_sums, axis=0).reshape(img_count, D) + bias_shift

    lat_masked = (latents * inside[..., None]).astype(BF)
    cot_masked = (cotangent * inside[..., None]).astype(BF)
    rims = with_halo(
        jnp.concatenate([lat_masked, cot_masked], axis=-1), (("row", 1), ("col", 2)), 1
    )
    rims = rims.astype(F32)
    near = gather_near(rims[..., :patch_vals], tile_rows, tile_cols)
    near = near.reshape(img_count, tokens, near_vals).astype(BF)
    cot_near = gather_near(rims[..., patch_vals:], tile_rows, tile_cols)
    cot_near = cot_near.reshape(img_count, tokens, near_vals)
    embedded = matmul_back(near, embed_t) + bias_embed
    joined_full = jnp.concatenate(
        [embedded, skip.reshape(img_count, tokens, D).astype(F32)], axis=-1
    )
    skip_normed, skip_norm_pull = jax.vjp(layer_norm, joined_full, skip_gains, skip_offsets)
    skip_in = skip_normed.astype(BF)
    resid_in = matmul(skip_in, skip_full) + bias_skip
    self_norm, self_norm_pull = jax.vjp(layer_norm, resid_in, gain_rows[0], offset_rows[0])
    normed = (self_norm + shift_rows[:, None, :]).astype(BF)

    qkv_t = dot(qkv_full, normed, (0,), (2,)) + bias_qkv[:, None, None]
    qkv_t = qkv_t.astype(BF).reshape(3, HEADS, HD, img_count, tokens)
    qkv_jobs = all_to_all(
        jnp.transpose(qkv_t, (1, 3, 0, 2, 4)).reshape(count, jobs, 3, HD, tokens)
    )
    head_cols = jnp.stack([head_gains[0], head_offsets[0], head_gains[1], head_offsets[1]], axis=1)
    mixed_jobs, keep, total = attend(ext_jobs, qkv_jobs, every_cos, every_sin, head_cols, geo)
    mixed = all_to_all(mixed_jobs).reshape(HEADS, img_count, HD, tokens)
    attended_t = jnp.transpose(mixed, (1, 0, 2, 3)).reshape(img_count, D, tokens)
    resid_self = resid_in + dot(attended_t, out_full, (1,), (0,)) + bias_out

    cross_norm, cross_norm_pull = jax.vjp(layer_norm, resid_self, gain_rows[1], offset_rows[1])
    cross_in = cross_norm.astype(BF)
    all_tokens = img_count * tokens
    cross_rows = dot(cross_q_full, cross_in.reshape(all_tokens, D), (0,), (1,))
    cross_rows = (cross_rows + bias_cross_q[:, None]).reshape(HEADS, HD, all_tokens)
    cross_cols = jnp.stack([head_gains[2], head_offsets[2]], axis=1)
    cross_mixed, cross_total = cross_attend(
        text_len, cross_rows, text_both, own_cos, own_sin, cross_cols
    )
    cross_low = cross_mixed.reshape(D, all_tokens)
    cross_out_rows = dot(cross_low, cross_o_full, (0,), (0,)).reshape(img_count, tokens, D)
    resid_cross = resid_self + cross_out_rows + bias_cross_o

    mlp_norm, mlp_norm_pull = jax.vjp(layer_norm, resid_cross, gain_rows[2], offset_rows[2])
    mlp_in = images_gather(mlp_norm.astype(BF))
    hidden = matmul(mlp_in, up_full) + bias_up_part
    gelu_out, gelu_pull = jax.vjp(gelu_tanh, hidden)
    activated = gelu_out.astype(BF)
    resid_out = resid_cross + images_scatter(matmul(activated, down_full)) + bias_down
    resid_low = resid_out.astype(BF)
    emitted = matmul(resid_low, final_full) * token_inside
    emit_rim = with_halo(
        emitted.reshape(img_count, tile_rows, tile_cols, near_vals), (("row", 1), ("col", 2)), 1
    )
    out_latents = spread_near(emit_rim, tile_rows, tile_cols, patch_vals) * inside[..., None]

    lead = (0, 1)
    by_row = row_first()
    grad_emitted = (cot_near * token_inside).astype(BF)
    grad_final = weight_grad(resid_low, grad_emitted)
    grad_resid_out = matmul_back(grad_emitted, final_full)
    grad_down_low = grad_resid_out.astype(BF)
    bias_down_grad = column_sum(grad_down_low)
    grad_down_rows = images_gather(grad_down_low)
    every_lead = (0, 1, 2)
    whole_down = dot(activated, grad_down_rows, every_lead, every_lead)
    grad_hidden = gelu_pull(matmul_back(grad_down_rows, down_full))[0].astype(BF)
    whole_up = dot(mlp_in, grad_hidden, every_lead, every_lead)
    bias_up_grad = column_sum(grad_hidden)
    grad_mlp_in = images_scatter(matmul_back(grad_hidden, up_full))
    grad_from_mlp, gain_mlp_grad, shift_mlp_grad = mlp_norm_pull(grad_mlp_in)
    grad_resid_cross = grad_resid_out + grad_from_mlp

    grad_cross_low = grad_resid_cross.astype(BF)
    grad_cross_flat = grad_cross_low.reshape(all_tokens, D)
    whole_grads = {"cross_o": dot(cross_low, grad_cross_flat, (1,), (0,))}
    bias_cross_o_grad = column_sum(grad_cross_low)
    grad_cross_mixed = dot(cross_o_full, grad_cross_flat, (1,), (1,)).astype(BF)
    grad_cross_rows, grad_text, cross_head_grads = cross_attend_back(
        text_len, cross_rows, text_both, grad_cross_mixed.reshape(HEADS, HD, all_tokens),
        cross_total, own_cos, own_sin, cross_cols,
    )
    cross_head_grads = jnp.sum(cross_head_grads, axis=0)
    grad_cross_rows = grad_cross_rows.reshape(D, all_tokens)
    grad_cross_rows = moves.begin(
        grad_cross_rows,
        text=offload_sum(alone, grad_text.reshape(2 * D, img_count * text_count)),
    )
    whole_grads["cross_q"] = dot(cross_in.reshape(all_tokens, D), grad_cross_rows, (0,), (1,))
    bias_cross_q_grad = jnp.sum(grad_cross_rows.astype(F32), axis=1)
    grad_cross_in = dot(grad_cross_rows, cross_q_full, (0,), (1,))
    grad_from_cross, gain_cross_grad, shift_cross_grad = cross_norm_pull(
        grad_cross_in.reshape(img_count, tokens, D)
    )
    grad_resid_self = grad_resid_cross + grad_from_cross

    grad_out_rows = grad_resid_self.astype(BF)
    whole_grads["out"] = dot(attended_t, grad_out_rows, (0, 2), lead)
    bias_out_grad = column_sum(grad_out_rows)
    grad_attended = dot(out_full, grad_out_rows, (1,), (2,)).astype(BF)
    grad_attended = jnp.transpose(
        grad_attended.reshape(HEADS, HD, img_count, tokens), (0, 2, 1, 3)
    )
    grad_mixed_jobs = all_to_all(grad_attended.reshape(count, jobs, HD, tokens))
    grad_jobs, head_grads = attend_back(
        ext_jobs, qkv_jobs, grad_mixed_jobs, keep, total, every_cos, every_sin, head_cols, geo
    )
    grad_qkv_t = all_to_all(grad_jobs).reshape(HEADS, img_count, 3, HD, tokens)
    grad_qkv_t = jnp.transpose(grad_qkv_t, (2, 0, 3, 1, 4)).reshape(3 * D, img_count, tokens)
    head_grads = jnp.sum(head_grads, axis=0)

    for i, name in enumerate(("query", "key", "value")):
        whole_grads[name] = dot(normed, grad_qkv_t[i * D : (i + 1) * D], (0, 1), (1, 2))
    bias_qkv_grad = jnp.sum(grad_qkv_t.astype(F32), axis=(1, 2))
    grad_normed = dot(grad_qkv_t, qkv_full, (0,), (1,))
    grad_shift_rows = jnp.sum(grad_normed, axis=1)
    bias_shift_grad = jnp.sum(grad_shift_rows, axis=0)
    grad_from_self, gain_self_grad, shift_self_grad = self_norm_pull(grad_normed)
    grad_resid_in = grad_resid_self + grad_from_self
    grad_merged = grad_resid_in.astype(BF)
    whole_grads["skip"] = weight_grad(skip_in, grad_merged)
    bias_skip_grad = column_sum(grad_merged)
    grad_skip_normed = matmul_back(grad_merged, skip_full)
    grad_joined, skip_gain_grad, skip_shift_grad = skip_norm_pull(grad_skip_normed)
    grad_skip = grad_joined[..., D:].reshape(img_count, tile_rows, tile_cols, D)
    grad_embedded = grad_joined[..., :D].astype(BF)
    grad_embed_t = weight_grad(grad_embedded, near)
    bias_embed_grad = column_sum(grad_embedded)
    grad_near = matmul(grad_embedded, embed_t).reshape(
        img_count, tile_rows, tile_cols, near_vals
    )
    near_rim = with_halo(grad_near, (("row", 1), ("col", 2)), 1)
    grad_latents = spread_near(near_rim, tile_rows, tile_cols, patch_vals) * inside[..., None]

    moves.finish(*list(moves.running))
    shards = moves.done
    grad_text_lin, head_gain_ck_grad, head_shift_ck_grad = text_pull(shards["text"])
    grad_text_low = grad_text_lin.astype(BF)
    grad_cross_keys = images_sum(
        dot(
            text_wide, grad_text_low.reshape(text_width, img_count, text_count), (0, 1), (1, 2)
        ),
        BF,
    )
    grad_cross_bias = images_sum(jnp.sum(grad_text_low.astype(F32), axis=1), F32)

    def by_device(vector):
        return vector.reshape(count, -1)

    def rows_by_device(rows):
        return jnp.transpose(rows.reshape(3, count, shard), (1, 0, 2)).reshape(count, -1)

    bias_up_all = jnp.where(
        (jnp.arange(groups) == group_index)[None, :, None],
        bias_up_grad.reshape(count, 1, hid_part),
        0.0,
    ).reshape(-1)
    small_grads = jnp.concatenate(
        [
            by_device(grad_embed_t),
            by_device(grad_final),
            rows_by_device(jnp.stack([gain_self_grad, gain_cross_grad, gain_mlp_grad])),
            rows_by_device(jnp.stack([shift_self_grad, shift_cross_grad, shift_mlp_grad])),
            by_device(skip_gain_grad),
            by_device(skip_shift_grad),
            by_device(
                jnp.concatenate(
                    [head_grads[:, 0], head_grads[:, 2], cross_head_grads[:, 0], head_gain_ck_grad]
                )
            ),
            by_device(
                jnp.concatenate(
                    [head_grads[:, 1], head_grads[:, 3], cross_head_grads[:, 1], head_shift_ck_grad]
                )
            ),
            by_device(
                jnp.concatenate([bias_embed_grad, bias_skip_grad, bias_shift_grad, bias_qkv_grad])
            ),
            by_device(
                jnp.concatenate(
                    [
                        bias_out_grad, bias_cross_q_grad, bias_cross_o_grad, bias_up_all,
                        bias_down_grad,
                    ]
                )
            ),
        ],
        axis=1,
    )
    shift_share = jnp.broadcast_to(grad_shift_rows.reshape(1, -1), (count, img_count * D))
    small_grads = jnp.concatenate([small_grads, shift_share], axis=1).astype(BF)
    small_grads = jnp.pad(small_grads, ((0, 0), (0, padded_len - small_grads.shape[1])))
    small_got = all_to_all(small_grads.reshape(count, -1, 128))
    names = ("query", "key", "value", "skip", "out", "cross_q", "cross_o")
    packed = [whole_grads[name].astype(BF).reshape(count, -1, D) for name in names]
    packed_rows = sum(part.shape[1] for part in packed)
    fill = -packed_rows % (16 * groups)
    packed = jnp.pad(jnp.concatenate(packed, axis=1), ((0, 0), (0, fill), (0, 0)))
    up_rows = jnp.pad(
        whole_up.astype(BF).reshape(count, shard, -1), ((0, 0), (0, -shard % 16), (0, 0))
    )
    down_rows = whole_down.astype(BF).reshape(count, hid_part, D)
    packed, small_got = lax.optimization_barrier((packed, small_got))
    summed, up_sums, down_sums = sum_everywhere(
        packed, down_rows, up_rows, (groups, row_count, col_count)
    )
    summed = summed.astype(F32)
    total_of, at = {}, 0
    for name in names:
        rows = whole_grads[name].shape[0] // count
        total_of[name] = summed[at : at + rows]
        at += rows
    small_got = jnp.sum(small_got.astype(F32), axis=0).reshape(-1)
    small_sum = images_sum(small_got[:small_len], F32)
    total_parts = cuts(small_sum, (wide, wide) + small_widths)
    grad_shift = lax.dot_general(
        time_own.astype(F32),
        small_got[small_len : small_len + img_count * D].reshape(img_count, D),
        (((0,), (0,)), ((), ())),
        precision=lax.Precision.HIGHEST,
    )

    total_up = jnp.transpose(
        up_sums[:, :shard].reshape(groups, shard, count, hid_part), (1, 2, 0, 3)
    ).reshape(shard, FF)
    total_down = down_sums.reshape(hid_shard, D)
    return (
        out_latents,
        grad_latents,
        grad_skip,
        total_parts[0].reshape(shard, near_vals).T,
        total_of["skip"],
        images_sum(grad_shift, F32),
        jnp.concatenate([total_of[name] for name in ("query", "key", "value")], axis=1),
        total_of["out"],
        total_of["cross_q"],
        grad_cross_keys,
        total_of["cross_o"],
        total_up.astype(F32),
        total_down.astype(F32),
        total_parts[1].reshape(shard, near_vals),
        total_parts[2].reshape(3, shard),
        total_parts[3].reshape(3, shard),
        total_parts[4],
        total_parts[5],
        total_parts[6],
        total_parts[7],
        total_parts[8],
        total_parts[9],
        grad_cross_bias,
    )


def solution(mesh):
    tile = P("img", "row", "col", None)
    rows = P(GROUP, None)
    columns = P(None, GROUP)
    vector = P(GROUP)
    return jax.shard_map(
        body,
        mesh=mesh,
        in_specs=(
            tile, tile, P("img", None), P("img", None, None), P("img", None), P("img", None),
            columns, rows, rows, rows, rows, rows, columns, rows, rows, rows, rows,
            columns, columns, vector, vector, vector, vector, vector, vector, vector, tile,
        ),
        out_specs=(
            tile, tile, tile, columns, rows, rows, rows, rows, rows, columns, rows, rows, rows,
            rows, columns, columns, vector, vector, vector, vector, vector, vector, vector,
        ),
        check_vma=False,
    )
```

```python
import functools
import math
from typing import NamedTuple

import jax
import jax.numpy as jnp
import numpy as np
from jax import lax
from jax.experimental import pallas as pl
from jax.experimental.pallas import tpu as pltpu
from jax.sharding import PartitionSpec as P

D = 1408
HEADS = 16
HD = 88
FF = 6144
CLIP = 77
NORM_EPS = 1e-06
NEG_FILL = -1e30
STEPS = ((-1, -1), (-1, 0), (-1, 1), (0, -1), (0, 0), (0, 1), (1, -1), (1, 0), (1, 1))
GROUP = ("row", "col")
F32 = jnp.float32
BF = jnp.bfloat16
SCALE = 1.0 / math.sqrt(HD)
LOG2E = math.log2(math.e)
NT = (((1,), (1,)), ((), ()))
KEY_BLOCK = 256
QUERY_CHUNK = 1024


def with_halo(block, sides, width):
    for axis, dim in sides:
        count = lax.axis_size(axis)
        forward = [(i, i + 1) for i in range(count - 1)]
        backward = [(target, source) for source, target in forward]
        low = lax.ppermute(
            lax.slice_in_dim(block, block.shape[dim] - width, None, axis=dim), axis, forward
        )
        high = lax.ppermute(lax.slice_in_dim(block, 0, width, axis=dim), axis, backward)
        block = jnp.concatenate([low, block, high], axis=dim)
    return block


def dot(former, latter, former_dims, latter_dims):
    return lax.dot_general(
        former, latter, ((former_dims, latter_dims), ((), ())), preferred_element_type=F32
    )


def matmul(former, latter):
    return dot(former, latter, (former.ndim - 1,), (0,))


def matmul_back(former, latter):
    return dot(former, latter, (former.ndim - 1,), (1,))


def weight_grad(inputs, grads):
    lead = tuple(range(inputs.ndim - 1))
    return dot(inputs, grads, lead, lead)


def column_sum(grads):
    return jnp.sum(grads.astype(F32), axis=tuple(range(grads.ndim - 1)))


def layer_norm(values, scales, offsets):
    centre = values - jnp.mean(values, axis=-1, keepdims=True)
    spread = jnp.mean(centre * centre, axis=-1, keepdims=True)
    return centre * lax.rsqrt(spread + NORM_EPS) * scales + offsets


def angles_of(row_place, col_place):
    pair_index = np.arange(HD) // 2
    quarter = HD // 4
    within = np.where(pair_index < quarter, pair_index, pair_index - quarter).astype(np.float32)
    frequency = np.exp(np.float32(-math.log(10000.0)) * within / np.float32(quarter))
    by_row = jnp.asarray(pair_index < quarter)
    places = jnp.where(by_row[:, None], row_place[None, :], col_place[None, :])
    return places.astype(F32) * jnp.asarray(frequency.astype(np.float32))[:, None]


def gather_near(padded, tall, broad):
    return jnp.concatenate(
        [
            padded[..., 1 + step_row : 1 + step_row + tall, 1 + step_col : 1 + step_col + broad, :]
            for step_row, step_col in STEPS
        ],
        axis=-1,
    )


def spread_near(padded, tall, broad, channels):
    result = None
    for number, (step_row, step_col) in enumerate(STEPS):
        portion = padded[
            ...,
            1 - step_row : 1 - step_row + tall,
            1 - step_col : 1 - step_col + broad,
            number * channels : (number + 1) * channels,
        ]
        result = portion if result is None else result + portion
    return result


def cuts(vector, widths):
    ends = np.cumsum((0,) + widths)
    return [vector[..., ends[i] : ends[i + 1]] for i in range(len(widths))]


def swap_images(values, bit):
    count = lax.axis_size("img")
    return lax.ppermute(values, "img", [(i, i ^ bit) for i in range(count)])


def images_gather(values):
    blocks = values[None]
    while blocks.shape[0] < lax.axis_size("img"):
        blocks = jnp.concatenate([blocks, swap_images(blocks, blocks.shape[0])])
    return blocks


def images_scatter(parts):
    while parts.shape[0] > 1:
        half = parts.shape[0] // 2
        parts = parts[:half] + swap_images(parts[half:].astype(BF), half).astype(F32)
    return parts[0]


def images_sum(values, sent):
    bit = 1
    while bit < lax.axis_size("img"):
        values = values.astype(sent)
        values = values.astype(F32) + swap_images(values, bit).astype(F32)
        bit *= 2
    return values.astype(F32)


def exchange(values, axis, bit):
    if bit is None:
        return lax.psum_scatter(values, axis, scatter_dimension=0, tiled=True)
    size = lax.axis_size(axis)
    return lax.ppermute(values, axis, [(i, i ^ bit) for i in range(size)])


def halves(values, dim, bit):
    keep = lax.dynamic_index_in_dim(values, bit, dim, keepdims=False)
    return keep, lax.dynamic_index_in_dim(values, 1 - bit, dim, keepdims=False)


def core_features(values, dim, core):
    rows = lax.axis_size("row")
    block = values.shape[dim] // rows
    return jnp.concatenate(
        [
            lax.dynamic_slice_in_dim(values, (2 * i + core) * block, block, dim)
            for i in range(rows // 2)
        ],
        axis=dim,
    )


def row_first():
    rows, cols = lax.axis_size("row"), lax.axis_size("col")
    row_bits = [("row", 1 << i) for i in range(1, rows.bit_length() - 1)]
    return row_bits + [("col", 1 << i) for i in range(cols.bit_length() - 1)]


def shard_sum(order, after, inputs, grads, input_lead, grad_lead, feature):
    core = lax.axis_index("row") % 2
    give = dot(core_features(inputs, feature, 1 - core), grads, input_lead, grad_lead)
    (got,) = yield [give.astype(BF)], "row", 1
    keep = dot(core_features(inputs, feature, core), grads, input_lead, grad_lead)
    part = yield from scatter_sum(order, keep + got.astype(F32))
    part = yield from after(part)
    return part


def offload_sum(after, part):
    (got,) = yield [part.astype(BF)], GROUP, None
    part = yield from after(got.astype(F32))
    return part


def scatter_sum(order, part):
    dims = [d for d in reversed(row_first()) if d[0] == "row"]
    dims += [d for d in reversed(row_first()) if d[0] == "col"]
    width = part.shape[-1]
    part = part.reshape((2,) * len(dims) + (-1, width))
    for axis, bit in order:
        at = dims.index((axis, bit))
        keep, give = halves(part, at, lax.axis_index(axis) // bit % 2)
        del dims[at]
        (got,) = yield [give.astype(BF)], axis, bit
        part = keep + got.astype(F32)
    return part.reshape(-1, width)


def alone(part):
    return part
    yield


def all_images(part):
    bit, blocks = 1, part.astype(BF)[None]
    while bit < lax.axis_size("img"):
        (got,) = yield [blocks], "img", bit
        blocks = placed(blocks, got, lax.axis_index("img") // bit % 2, 0)
        blocks = blocks.reshape((-1,) + part.shape)
        bit *= 2
    return blocks


def placed(mine, other, bit, dim):
    first = lax.select(jnp.broadcast_to(bit == 0, mine.shape), mine, other)
    last = lax.select(jnp.broadcast_to(bit == 0, mine.shape), other, mine)
    return jnp.stack([first, last], axis=dim)


class Moves:
    def __init__(self):
        self.running = {}
        self.done = {}

    def begin(self, value, **makers):
        return self.launch(value, {name: (maker, next(maker)) for name, maker in makers.items()})

    def launch(self, value, wanted):
        if not wanted:
            return value
        gives = {name: request[0] for name, (_, request) in wanted.items()}
        value, gives = lax.optimization_barrier((value, gives))
        for name, (maker, (_, axis, bit)) in wanted.items():
            self.running[name] = (maker, [exchange(give, axis, bit) for give in gives[name]])
        return value

    def step(self, value, *names):
        names = [name for name in names if name in self.running]
        if not names:
            return value
        value, gots = lax.optimization_barrier(
            (value, {name: self.running[name][1] for name in names})
        )
        wanted = {}
        for name in names:
            maker = self.running.pop(name)[0]
            try:
                wanted[name] = (maker, maker.send(gots[name]))
            except StopIteration as stop:
                self.done[name] = stop.value
        return self.launch(value, wanted)

    def finish(self, *names):
        waiting = [name for name in names if name in self.running]
        while waiting:
            for name in waiting:
                maker, gots = self.running.pop(name)
                try:
                    gives, axis, bit = maker.send(gots)
                    self.running[name] = (maker, [exchange(give, axis, bit) for give in gives])
                except StopIteration as stop:
                    self.done[name] = stop.value
            waiting = [name for name in names if name in self.running]


def unit_rows(values):
    centre = values - jnp.mean(values, axis=0, keepdims=True)
    rstd = lax.rsqrt(jnp.mean(centre * centre, axis=0, keepdims=True) + NORM_EPS)
    return centre * rstd, rstd


def swap_pairs(values, back):
    rows = values.shape[0]
    even = lax.broadcasted_iota(jnp.int32, values.shape, 0) % 2 == 0
    up = pltpu.roll(values, rows - 1, 0)
    down = pltpu.roll(values, 1, 0)
    return jnp.where(even, up, -down) if back else jnp.where(even, -up, down)


def turn(values, cos, sin):
    return values * cos + swap_pairs(values, False) * sin


def turn_back(values, cos, sin):
    return values * cos + swap_pairs(values, True) * sin


def tiles(ref, part, count):
    return jnp.concatenate([ref[s, 0, part] for s in range(count)], axis=1)


def key_blocks(geo, ext_ref, job):
    count, tile_rows, tile_cols, col_tiles, block_tiles = geo
    rows = ext_ref[job, 0] // tile_rows
    groups = ext_ref[job, 1] // (block_tiles * tile_cols)

    def place(i):
        block = i // groups * (col_tiles // block_tiles) + i % groups
        return pl.multiple_of(block * KEY_BLOCK, KEY_BLOCK)

    return rows * groups, place


def attend_kernel(
    geo, ext_ref, qkv_ref, cos_ref, sin_ref, head_ref, out_ref, keep_ref, total_ref,
    q_s, kt_s, v_s, m_s, l_s,
):
    count = geo[0]
    cos, sin = cos_ref[...], sin_ref[...]
    unit, _ = unit_rows(tiles(qkv_ref, 0, count).astype(F32))
    q_s[...] = turn(unit * head_ref[:, 0:1] + head_ref[:, 1:2], cos, sin).astype(BF)
    unit, _ = unit_rows(tiles(qkv_ref, 1, count).astype(F32))
    kt_s[...] = turn(unit * head_ref[:, 2:3] + head_ref[:, 3:4], cos, sin).T.astype(BF)
    v_s[...] = tiles(qkv_ref, 2, count)
    block_count, place = key_blocks(geo, ext_ref, pl.program_id(0))
    width = q_s.shape[1]
    m_s[...] = jnp.full_like(m_s, NEG_FILL)
    l_s[...] = jnp.zeros_like(l_s)
    keep_ref[0] = jnp.zeros(keep_ref.shape[1:], F32)

    def key_step(i, carry):
        first = place(i)
        keys = kt_s[pl.ds(first, KEY_BLOCK), :]
        vals = v_s[:, pl.ds(first, KEY_BLOCK)]
        for part in range(width // QUERY_CHUNK):
            cut = slice(part * QUERY_CHUNK, (part + 1) * QUERY_CHUNK)
            scores = jnp.dot(keys, q_s[:, cut], preferred_element_type=F32)
            old = m_s[:, cut]
            new = jnp.maximum(old, jnp.max(scores, axis=0, keepdims=True))
            probs = jnp.exp2((scores - new) * (SCALE * LOG2E))
            factor = jnp.exp2((old - new) * (SCALE * LOG2E))
            m_s[:, cut] = new
            l_s[:, cut] = l_s[:, cut] * factor + jnp.sum(probs, axis=0, keepdims=True)
            keep_ref[0, :, cut] = keep_ref[0, :, cut] * factor + jnp.dot(
                vals, probs.astype(BF), preferred_element_type=F32
            )
        return carry

    lax.fori_loop(0, block_count, key_step, 0)
    total_ref[0] = m_s[...] * (SCALE * LOG2E) + jnp.log2(l_s[...])
    mixed = keep_ref[0] / l_s[...]
    keep_ref[0] = mixed
    low = mixed.astype(BF)
    tile = width // count
    for s in range(count):
        out_ref[s, 0] = low[:, s * tile : (s + 1) * tile]


def attend(ext_jobs, qkv, cos, sin, head, geo):
    count, jobs, _, _, tile = qkv.shape
    width = count * tile
    work = 4 * jobs * width * width * HD
    return pl.pallas_call(
        functools.partial(attend_kernel, geo),
        grid=(jobs,),
        in_specs=[
            pl.BlockSpec(memory_space=pltpu.SMEM),
            pl.BlockSpec((count, 1, 3, HD, tile), lambda j: (0, j, 0, 0, 0)),
            pl.BlockSpec((HD, width), lambda j: (0, 0)),
            pl.BlockSpec((HD, width), lambda j: (0, 0)),
            pl.BlockSpec((HD, 4), lambda j: (0, 0)),
        ],
        out_specs=[
            pl.BlockSpec((count, 1, HD, tile), lambda j: (0, j, 0, 0)),
            pl.BlockSpec((1, HD, width), lambda j: (j, 0, 0)),
            pl.BlockSpec((1, 1, width), lambda j: (j, 0, 0)),
        ],
        out_shape=[
            jax.ShapeDtypeStruct((count, jobs, HD, tile), BF),
            jax.ShapeDtypeStruct((jobs, HD, width), F32),
            jax.ShapeDtypeStruct((jobs, 1, width), F32),
        ],
        scratch_shapes=[
            pltpu.VMEM((HD, width), BF),
            pltpu.VMEM((width, HD), BF),
            pltpu.VMEM((HD, width), BF),
            pltpu.VMEM((1, width), F32),
            pltpu.VMEM((1, width), F32),
        ],
        compiler_params=pltpu.CompilerParams(vmem_limit_bytes=48 * 2**20),
        cost_estimate=pl.CostEstimate(
            flops=3 * work, bytes_accessed=6 * 2**20, transcendentals=jobs * width * width
        ),
    )(ext_jobs, qkv, cos, sin, head)


def attend_back_kernel(
    geo, ext_ref, qkv_ref, dout_ref, keep_ref, total_ref, cos_ref, sin_ref, head_ref,
    grad_ref, head_grad_ref, q_s, k_s, kt_s, vt_s, do_s, delta_s, dq_s, dk_s, dv_s,
):
    count = geo[0]
    cos, sin = cos_ref[...], sin_ref[...]
    unit, _ = unit_rows(tiles(qkv_ref, 0, count).astype(F32))
    q_s[...] = turn(unit * head_ref[:, 0:1] + head_ref[:, 1:2], cos, sin).astype(BF)
    unit, _ = unit_rows(tiles(qkv_ref, 1, count).astype(F32))
    keys = turn(unit * head_ref[:, 2:3] + head_ref[:, 3:4], cos, sin)
    k_s[...] = keys.astype(BF)
    kt_s[...] = keys.T.astype(BF)
    vt_s[...] = tiles(qkv_ref, 2, count).astype(F32).T.astype(BF)
    dout = jnp.concatenate([dout_ref[s, 0] for s in range(count)], axis=1)
    do_s[...] = dout
    delta_s[...] = jnp.sum(dout.astype(F32) * keep_ref[0], axis=0, keepdims=True)
    block_count, place = key_blocks(geo, ext_ref, pl.program_id(0))
    width = q_s.shape[1]
    dq_s[...] = jnp.zeros_like(dq_s)
    dk_s[...] = jnp.zeros_like(dk_s)
    dv_s[...] = jnp.zeros_like(dv_s)

    def key_step(i, carry):
        first = place(i)
        keys_t = kt_s[pl.ds(first, KEY_BLOCK), :]
        vals_t = vt_s[pl.ds(first, KEY_BLOCK), :]
        keys_n = k_s[:, pl.ds(first, KEY_BLOCK)]
        dk = jnp.zeros((HD, KEY_BLOCK), F32)
        dv = jnp.zeros((HD, KEY_BLOCK), F32)
        for part in range(width // QUERY_CHUNK):
            cut = slice(part * QUERY_CHUNK, (part + 1) * QUERY_CHUNK)
            queries = q_s[:, cut]
            douts = do_s[:, cut]
            scores = jnp.dot(keys_t, queries, preferred_element_type=F32)
            probs = jnp.exp2(scores * (SCALE * LOG2E) - total_ref[0, :, cut])
            dprob = jnp.dot(vals_t, douts, preferred_element_type=F32)
            dscore = (probs * (dprob - delta_s[:, cut])).astype(BF)
            dv = dv + lax.dot_general(douts, probs.astype(BF), NT, preferred_element_type=F32)
            dk = dk + lax.dot_general(queries, dscore, NT, preferred_element_type=F32)
            dq_s[:, cut] += jnp.dot(keys_n, dscore, preferred_element_type=F32)
        dk_s[:, pl.ds(first, KEY_BLOCK)] = dk
        dv_s[:, pl.ds(first, KEY_BLOCK)] = dv
        return carry

    lax.fori_loop(0, block_count, key_step, 0)
    tile = width // count

    def lift(part, turned, at):
        unit, rstd = unit_rows(tiles(qkv_ref, part, count).astype(F32))
        dy = turn_back(turned * SCALE, cos, sin)
        head_grad_ref[0, :, at : at + 1] = jnp.sum(dy * unit, axis=1, keepdims=True)
        head_grad_ref[0, :, at + 1 : at + 2] = jnp.sum(dy, axis=1, keepdims=True)
        dunit = dy * head_ref[:, at : at + 1]
        along = jnp.mean(dunit * unit, axis=0, keepdims=True)
        dx = (dunit - jnp.mean(dunit, axis=0, keepdims=True) - unit * along) * rstd
        low = dx.astype(BF)
        for s in range(count):
            grad_ref[s, 0, part] = low[:, s * tile : (s + 1) * tile]

    lift(0, dq_s[...], 0)
    lift(1, dk_s[...], 2)
    low = dv_s[...].astype(BF)
    for s in range(count):
        grad_ref[s, 0, 2] = low[:, s * tile : (s + 1) * tile]


def attend_back(ext_jobs, qkv, dout, keep, total, cos, sin, head, geo):
    count, jobs, _, _, tile = qkv.shape
    width = count * tile
    work = 10 * jobs * width * width * HD
    return pl.pallas_call(
        functools.partial(attend_back_kernel, geo),
        grid=(jobs,),
        in_specs=[
            pl.BlockSpec(memory_space=pltpu.SMEM),
            pl.BlockSpec((count, 1, 3, HD, tile), lambda j: (0, j, 0, 0, 0)),
            pl.BlockSpec((count, 1, HD, tile), lambda j: (0, j, 0, 0)),
            pl.BlockSpec((1, HD, width), lambda j: (j, 0, 0)),
            pl.BlockSpec((1, 1, width), lambda j: (j, 0, 0)),
            pl.BlockSpec((HD, width), lambda j: (0, 0)),
            pl.BlockSpec((HD, width), lambda j: (0, 0)),
            pl.BlockSpec((HD, 4), lambda j: (0, 0)),
        ],
        out_specs=[
            pl.BlockSpec((count, 1, 3, HD, tile), lambda j: (0, j, 0, 0, 0)),
            pl.BlockSpec((1, HD, 4), lambda j: (j, 0, 0)),
        ],
        out_shape=[
            jax.ShapeDtypeStruct((count, jobs, 3, HD, tile), BF),
            jax.ShapeDtypeStruct((jobs, HD, 4), F32),
        ],
        scratch_shapes=[
            pltpu.VMEM((HD, width), BF),
            pltpu.VMEM((HD, width), BF),
            pltpu.VMEM((width, HD), BF),
            pltpu.VMEM((width, HD), BF),
            pltpu.VMEM((HD, width), BF),
            pltpu.VMEM((1, width), F32),
            pltpu.VMEM((HD, width), F32),
            pltpu.VMEM((HD, width), F32),
            pltpu.VMEM((HD, width), F32),
        ],
        compiler_params=pltpu.CompilerParams(vmem_limit_bytes=56 * 2**20),
        cost_estimate=pl.CostEstimate(
            flops=3 * work, bytes_accessed=8 * 2**20, transcendentals=jobs * width * width
        ),
    )(ext_jobs, qkv, dout, keep, total, cos, sin, head)


TN = (((0,), (0,)), ((), ()))
CROSS_HEADS = 2


def text_scores(len_ref, keys, queries, image):
    scores = lax.dot_general(keys, queries, TN, preferred_element_type=F32) * (SCALE * LOG2E)
    place = lax.broadcasted_iota(jnp.int32, scores.shape, 0)
    live = (place < len_ref[image, 0]) | (
        (place >= CLIP) & (place < CLIP + len_ref[image, 1])
    )
    return jnp.where(live, scores, NEG_FILL)


def cross_kernel(images, len_ref, rows_ref, text_ref, cos_ref, sin_ref, head_ref, out_ref, total_ref):
    tile = rows_ref.shape[2] // images
    slots = text_ref.shape[3] // images
    for h in range(CROSS_HEADS):
        unit, _ = unit_rows(rows_ref[h])
        queries = turn(unit * head_ref[:, 0:1] + head_ref[:, 1:2], cos_ref[...], sin_ref[...])
        queries = queries.astype(BF)
        for i in range(images):
            own, slot = slice(i * tile, (i + 1) * tile), slice(i * slots, (i + 1) * slots)
            scores = text_scores(len_ref, text_ref[0, h, :, slot], queries[:, own], i)
            top = jnp.max(scores, axis=0, keepdims=True)
            probs = jnp.exp2(scores - top)
            weight = jnp.sum(probs, axis=0, keepdims=True)
            low = (probs / weight).astype(BF)
            mixed = jnp.dot(text_ref[1, h, :, slot], low, preferred_element_type=F32)
            out_ref[h, :, own] = mixed.astype(BF)
            total_ref[h, :, own] = top + jnp.log2(weight)


def cross_back_kernel(
    images, len_ref, rows_ref, text_ref, dout_ref, total_ref, cos_ref, sin_ref, head_ref,
    grad_ref, text_grad_ref, head_grad_ref,
):
    tile = rows_ref.shape[2] // images
    slots = text_ref.shape[3] // images
    cos, sin = cos_ref[...], sin_ref[...]
    gain_grad = jnp.zeros((HD, 1), F32)
    shift_grad = jnp.zeros((HD, 1), F32)
    for h in range(CROSS_HEADS):
        unit, rstd = unit_rows(rows_ref[h])
        queries = turn(unit * head_ref[:, 0:1] + head_ref[:, 1:2], cos, sin).astype(BF)
        turned = []
        for i in range(images):
            own, slot = slice(i * tile, (i + 1) * tile), slice(i * slots, (i + 1) * slots)
            keys = text_ref[0, h, :, slot]
            douts = dout_ref[h, :, own]
            scores = text_scores(len_ref, keys, queries[:, own], i)
            probs = jnp.exp2(scores - total_ref[h, :, own])
            dprob = lax.dot_general(
                text_ref[1, h, :, slot], douts, TN, preferred_element_type=F32
            )
            delta = jnp.sum(probs * dprob, axis=0, keepdims=True)
            dscore = (probs * (dprob - delta)).astype(BF)
            low = probs.astype(BF)
            dkeys = lax.dot_general(queries[:, own], dscore, NT, preferred_element_type=F32)
            text_grad_ref[0, h, :, slot] = (dkeys * SCALE).astype(BF)
            text_grad_ref[1, h, :, slot] = lax.dot_general(
                douts, low, NT, preferred_element_type=F32
            ).astype(BF)
            turned.append(jnp.dot(keys, dscore, preferred_element_type=F32))
        dy = turn_back(jnp.concatenate(turned, axis=1) * SCALE, cos, sin)
        gain_grad += jnp.sum(dy * unit, axis=1, keepdims=True)
        shift_grad += jnp.sum(dy, axis=1, keepdims=True)
        dunit = dy * head_ref[:, 0:1]
        along_unit = jnp.mean(dunit * unit, axis=0, keepdims=True)
        dx = (dunit - jnp.mean(dunit, axis=0, keepdims=True) - unit * along_unit) * rstd
        grad_ref[h] = dx.astype(BF)
    head_grad_ref[0, :, 0:1] = gain_grad
    head_grad_ref[0, :, 1:2] = shift_grad


def cross_specs(width, slots):
    return dict(
        smem=pl.BlockSpec(memory_space=pltpu.SMEM),
        rows=pl.BlockSpec((CROSS_HEADS, HD, width), lambda h: (h, 0, 0)),
        text=pl.BlockSpec((2, CROSS_HEADS, HD, slots), lambda h: (0, h, 0, 0)),
        table=pl.BlockSpec((HD, width), lambda h: (0, 0)),
        head=pl.BlockSpec((HD, 2), lambda h: (0, 0)),
        total=pl.BlockSpec((CROSS_HEADS, 1, width), lambda h: (h, 0, 0)),
        head_grad=pl.BlockSpec((1, HD, 2), lambda h: (h, 0, 0)),
    )


def cross_attend(lengths, rows, text, cos, sin, head):
    heads, _, width = rows.shape
    slots = text.shape[3]
    sp = cross_specs(width, slots)
    return pl.pallas_call(
        functools.partial(cross_kernel, lengths.shape[0]),
        grid=(heads // CROSS_HEADS,),
        in_specs=[sp["smem"], sp["rows"], sp["text"], sp["table"], sp["table"], sp["head"]],
        out_specs=[sp["rows"], sp["total"]],
        out_shape=[
            jax.ShapeDtypeStruct((heads, HD, width), BF),
            jax.ShapeDtypeStruct((heads, 1, width), F32),
        ],
        compiler_params=pltpu.CompilerParams(vmem_limit_bytes=32 * 2**20),
        cost_estimate=pl.CostEstimate(
            flops=2**32, bytes_accessed=10 * 2**20, transcendentals=heads * width * slots
        ),
    )(lengths, rows, text, cos, sin, head)


def cross_attend_back(lengths, rows, text, dout, total, cos, sin, head):
    heads, _, width = rows.shape
    slots = text.shape[3]
    sp = cross_specs(width, slots)
    return pl.pallas_call(
        functools.partial(cross_back_kernel, lengths.shape[0]),
        grid=(heads // CROSS_HEADS,),
        in_specs=[
            sp["smem"], sp["rows"], sp["text"], sp["rows"], sp["total"], sp["table"], sp["table"],
            sp["head"],
        ],
        out_specs=[sp["rows"], sp["text"], sp["head_grad"]],
        out_shape=[
            jax.ShapeDtypeStruct((heads, HD, width), BF),
            jax.ShapeDtypeStruct((2, heads, HD, slots), BF),
            jax.ShapeDtypeStruct((heads // CROSS_HEADS, HD, 2), F32),
        ],
        compiler_params=pltpu.CompilerParams(vmem_limit_bytes=32 * 2**20),
        cost_estimate=pl.CostEstimate(
            flops=2**33, bytes_accessed=16 * 2**20, transcendentals=heads * width * slots
        ),
    )(lengths, rows, text, dout, total, cos, sin, head)


MESH = pl.DeviceIdType.MESH
LAG = 3
ROW_SHARE = 5


class Kind(NamedTuple):
    operand: int
    first_row: int
    width: int
    height: int
    chunks: int
    stride: int
    order: tuple


def sum_plan(sizes, kind):
    groups, row_count, cols = sizes
    count, height = row_count * cols // 2, kind.height
    firsts = {"img": (0, groups), "row": (1, row_count), "col": (0, cols)}
    plan = []
    for axis, i in [
        (axis, i)
        for axis in kind.order
        for i in range(firsts[axis][0], firsts[axis][1].bit_length() - 1)
    ]:
        bit = 1 << i
        if axis == "img":
            height //= 2
        else:
            count //= 2
        plan.append((axis, bit, count, height))
    return plan


def sum_kernel(sizes, kinds, *refs):
    groups, row_count, cols = sizes
    number = 1 + max(kind.operand for kind in kinds)
    grads_refs, out_refs, scratch = refs[:number], refs[number : 2 * number], refs[2 * number :]
    first_count = row_count * cols // 2
    places = {axis: lax.axis_index(axis) for axis in ("img", "row", "col")}
    plans = [sum_plan(sizes, kind) for kind in kinds]
    image_stages = groups.bit_length() - 1
    held, own, sems = [], [], []
    at = 0
    for plan in plans:
        held.append(scratch[at : at + len(plan) + 1])
        own.append(scratch[at + len(plan) + 1])
        sems.append(scratch[at + len(plan) + 2 : at + len(plan) + 8])
        at += len(plan) + 8
    core = places["row"] % 2

    def device_of(place):
        return tuple(place[name] for name in ("img", "row", "col"))

    def partner(axis, bit):
        place = dict(places)
        part = place[axis] // bit % 2
        place[axis] = place[axis] + bit - 2 * bit * part
        return device_of(place)

    def other_images():
        for i in range(1, groups):
            place = dict(places)
            place["img"] = lax.rem(places["img"] + i, groups)
            yield i, device_of(place)

    def bit_of(axis, bit):
        return places[axis] // bit % 2

    def chunk_rows(k, chunk):
        return pl.multiple_of(kinds[k].first_row + chunk * kinds[k].height, 16)

    def first_copies(k, chunk):
        rows = pl.ds(chunk_rows(k, chunk), kinds[k].height)
        for i in range(row_count // 2):
            shards = pl.ds((2 * i + 1 - core) * cols, cols)
            yield pltpu.make_async_remote_copy(
                src_ref=grads_refs[kinds[k].operand].at[shards, rows],
                dst_ref=held[k][0].at[chunk, pl.ds(i * cols, cols)],
                send_sem=sems[k][0].at[0, chunk],
                recv_sem=sems[k][1].at[0, chunk],
                device_id=partner("row", 1),
                device_id_type=MESH,
            )

    def own_copies(k, chunk):
        rows = pl.ds(chunk_rows(k, chunk), kinds[k].height)
        for i in range(row_count // 2):
            shards = pl.ds((2 * i + core) * cols, cols)
            yield pltpu.make_async_copy(
                grads_refs[kinds[k].operand].at[shards, rows],
                own[k].at[lax.rem(chunk, 2), pl.ds(i * cols, cols)],
                sems[k][4].at[lax.rem(chunk, 2)],
            )

    def split(k, stage):
        axis, bit, count, rows = plans[k][stage]
        part = bit_of(axis, bit)
        if axis == "img":
            give = pl.ds(pl.multiple_of((1 - part) * rows, 16), rows)
            keep = pl.ds(pl.multiple_of(part * rows, 16), rows)
            return [((pl.ds(0, count), give), pl.ds(0, count))], lambda i: (i, keep)
        every = pl.ds(0, rows)
        if axis == "row":
            give = pl.ds((1 - part) * count, count)
            return [((give, every), pl.ds(0, count))], lambda i: (part * count + i, every)
        return (
            [((pl.ds(2 * i + 1 - part, 1), every), pl.ds(i, 1)) for i in range(count)],
            lambda i: (2 * i + part, every),
        )

    def stage_copies(k, stage, chunk):
        axis, bit, _, _ = plans[k][stage]
        for (shards, lines), target in split(k, stage)[0]:
            yield pltpu.make_async_remote_copy(
                src_ref=held[k][stage].at[chunk, shards, lines],
                dst_ref=held[k][stage + 1].at[chunk, target],
                send_sem=sems[k][0].at[stage + 1, chunk],
                recv_sem=sems[k][1].at[stage + 1, chunk],
                device_id=partner(axis, bit),
                device_id_type=MESH,
            )

    def whole(k, stage, chunk):
        buffer = held[k][stage].at[chunk]
        return pltpu.make_async_remote_copy(
            src_ref=buffer,
            dst_ref=buffer,
            send_sem=sems[k][0].at[stage, chunk],
            recv_sem=sems[k][1].at[stage, chunk],
            device_id=partner("row", 1),
            device_id_type=MESH,
        )

    def home(k, chunk):
        rows = plans[k][-1][3]
        out_ref = out_refs[kinds[k].operand]
        if "img" not in kinds[k].order:
            return out_ref.at[places["img"], pl.ds(chunk_rows(k, chunk), rows)]
        place = 0
        for i in range(image_stages):
            place = place + bit_of("img", 1 << i) * (1 << (image_stages - 1 - i))
        return out_ref.at[pl.ds(pl.multiple_of(chunk_rows(k, chunk) + place * rows, 16), rows)]

    def spread_copies(k, chunk):
        for i, other in other_images():
            yield pltpu.make_async_remote_copy(
                src_ref=held[k][-1].at[chunk, 0],
                dst_ref=home(k, chunk),
                send_sem=sems[k][2].at[i, chunk],
                recv_sem=sems[k][3].at[i, chunk],
                device_id=other,
                device_id_type=MESH,
            )

    def home_copy(k, chunk):
        return pltpu.make_async_copy(
            held[k][-1].at[chunk, 0], home(k, chunk), sems[k][5].at[chunk]
        )

    def start(copies):
        for copy in copies:
            copy.start()

    def begin(k, chunk):
        start(first_copies(k, chunk))
        start(own_copies(k, chunk))

    barrier = pltpu.get_barrier_semaphore()
    near = [partner("row", 1)] + [partner(a, b) for a, b, _, _ in plans[0] if a != "img"]
    near += [other for _, other in other_images()]
    for other in near:
        pl.semaphore_signal(barrier, inc=1, device_id=other, device_id_type=MESH)
    pl.semaphore_wait(barrier, len(near))

    for k in range(len(kinds)):
        begin(k, 0)

    def advance(k, stage, chunk):
        if stage == 0:

            @pl.when(chunk + 1 < kinds[k].chunks)
            def _():
                begin(k, chunk + 1)

        buffer = held[k][stage]
        whole(k, stage, chunk).wait_recv()
        if stage == 0:
            count = first_count
            for copy in own_copies(k, chunk):
                copy.wait()

            def mine(i):
                return own[k][lax.rem(chunk, 2), i]
        else:
            count = plans[k][stage - 1][2]
            kept = split(k, stage - 1)[1]

            def mine(i):
                shard, lines = kept(i)
                return held[k][stage - 1][chunk, shard, lines]

        def add(i, carry):
            both = buffer[chunk, i].astype(F32) + mine(i).astype(F32)
            buffer[chunk, i] = both.astype(BF)
            return carry

        lax.fori_loop(0, count, add, 0)
        if stage < len(plans[k]):
            start(stage_copies(k, stage, chunk))
        else:
            start(spread_copies(k, chunk))
            home_copy(k, chunk).start()

    def time_step(t, carry):
        for stage in range(max(len(plan) for plan in plans), -1, -1):
            for k, kind in enumerate(kinds):
                if stage <= len(plans[k]):
                    since = t - LAG * stage
                    chunk = since // kind.stride
                    due = jnp.logical_and(since >= 0, since % kind.stride == 0)

                    @pl.when(jnp.logical_and(due, chunk < kind.chunks))
                    def _(k=k, stage=stage, chunk=chunk):
                        advance(k, stage, chunk)

        return carry

    last = max(k.stride * k.chunks + LAG * len(plan) for k, plan in zip(kinds, plans))
    lax.fori_loop(0, last, time_step, 0)

    for k, kind in enumerate(kinds):

        def drain(chunk, carry, k=k):
            for stage in range(len(plans[k]) + 1):
                whole(k, stage, chunk).wait_send()
            for copy in spread_copies(k, chunk):
                copy.wait()
            home_copy(k, chunk).wait()
            return carry

        lax.fori_loop(0, kind.chunks, drain, 0)


def sum_everywhere(projections, down, up, sizes):
    groups, row_count, cols = sizes
    first_count = row_count * cols // 2
    height = 16 * groups
    chunks = projections.shape[1] // height
    late = max(1, chunks * ROW_SHARE // 22)
    early = chunks - late
    kinds = [
        Kind(0, 0, D, height, early, 1, ("img", "row", "col")),
        Kind(0, early * height, D, height, late, 3, ("row", "img", "col")),
        Kind(1, 0, up.shape[2], 16, up.shape[1] // 16, 3, ("row", "col")),
        Kind(2, 0, D, 16, down.shape[1] // 16, 1, ("col", "row")),
    ]
    scratch = []
    for kind in kinds:
        plan = sum_plan(sizes, kind)
        shapes = [(first_count, kind.height)] + [(c, h) for _, _, c, h in plan]
        scratch += [pltpu.VMEM((kind.chunks, c, h, kind.width), BF) for c, h in shapes]
        scratch.append(pltpu.VMEM((2, first_count, kind.height, kind.width), BF))
        stage_sems = pltpu.SemaphoreType.DMA((len(plan) + 1, kind.chunks))
        spread_sems = pltpu.SemaphoreType.DMA((groups, kind.chunks))
        scratch += [
            stage_sems, stage_sems, spread_sems, spread_sems,
            pltpu.SemaphoreType.DMA((2,)), pltpu.SemaphoreType.DMA((kind.chunks,)),
        ]
    space = pl.BlockSpec(memory_space=pl.ANY)
    return pl.pallas_call(
        functools.partial(sum_kernel, sizes, kinds),
        out_shape=[
            jax.ShapeDtypeStruct(projections.shape[1:], BF),
            jax.ShapeDtypeStruct((groups,) + up.shape[1:], BF),
            jax.ShapeDtypeStruct((groups,) + down.shape[1:], BF),
        ],
        in_specs=[space] * 3,
        out_specs=[space] * 3,
        scratch_shapes=scratch,
        compiler_params=pltpu.CompilerParams(
            collective_id=1, has_side_effects=True, vmem_limit_bytes=58 * 2**20
        ),
        cost_estimate=pl.CostEstimate(flops=2**28, bytes_accessed=2**28, transcendentals=0),
    )(projections, up, down)


def all_to_all(values):
    return lax.all_to_all(values, GROUP, split_axis=0, concat_axis=0, tiled=True)


def body(
    latents, skip, temb, text, text_len, extent, embed_weight, skip_weight, shift_weight,
    qkv_weight, out_weight, cross_query, cross_keys, cross_out, up_weight, down_weight,
    final_weight, norm_gain, norm_shift, skip_gain, skip_shift, head_gain, head_shift,
    front_biases, all_biases, cross_bias, cotangent,
):
    img_count, tile_rows, tile_cols, patch_vals = latents.shape
    tokens = tile_rows * tile_cols
    near_vals = 9 * patch_vals
    row_count = lax.axis_size("row")
    col_count = lax.axis_size("col")
    count = row_count * col_count
    groups = lax.axis_size("img")
    jobs = img_count * HEADS // count
    row_index = lax.axis_index("row")
    col_index = lax.axis_index("col")
    group_index = lax.axis_index("img")
    device = row_index * col_count + col_index
    shard = D // count
    hid_shard = FF // count
    hid_part = hid_shard // groups

    small_widths = (
        norm_gain.size, norm_shift.size, skip_gain.size, skip_shift.size,
        head_gain.size, head_shift.size, front_biases.size, all_biases.size,
    )
    small = jnp.concatenate(
        [
            embed_weight.T.reshape(-1), final_weight.reshape(-1), norm_gain.reshape(-1),
            norm_shift.reshape(-1), skip_gain, skip_shift, head_gain, head_shift,
            front_biases, all_biases,
        ]
    )
    small_len = small.size
    padded_len = -(-(small_len + img_count * D) // 2048) * 2048
    time_act = jax.nn.silu(temb.astype(F32)).astype(BF)
    time_own = lax.dynamic_slice_in_dim(time_act, device * shard, shard, 1)
    shift_share = matmul(time_own, shift_weight).astype(BF).reshape(-1)
    small = jnp.pad(jnp.concatenate([small, shift_share]), (0, padded_len - small_len - shift_share.size))
    small_all = all_to_all(jnp.broadcast_to(small.reshape(1, -1, 128), (count, padded_len // 128, 128)))
    small_all = small_all.reshape(count, padded_len)
    def beside(values, parts):
        return jnp.concatenate(jnp.split(values, parts, axis=0), axis=1)

    def below(values, parts):
        width = values.shape[1] // parts
        blocks = [values[:, i * width : (i + 1) * width] for i in range(parts)]
        return jnp.stack([b.reshape(count, -1, width) for b in blocks], axis=1).reshape(-1, width)

    first_all = lax.all_gather(
        jnp.concatenate([beside(skip_weight, 2), qkv_weight], axis=1), GROUP, axis=0, tiled=True
    )
    skip_full = below(first_all[:, : 2 * D], 2)
    qkv_full = first_all[:, 2 * D :]
    folds = hid_part // shard
    fold_rows = hid_part // folds
    up_part = lax.dynamic_index_in_dim(
        up_weight.reshape(shard, count, groups, hid_part), group_index, 2, keepdims=False
    ).reshape(shard, count * hid_part)
    down_part = lax.dynamic_index_in_dim(
        down_weight.reshape(groups, hid_part, D), group_index, 0, keepdims=False
    )
    third = jnp.concatenate(
        [jnp.pad(up_part, ((0, fold_rows - shard), (0, 0))), beside(down_part, folds)], axis=1
    )

    wide = shard * near_vals
    embed_t = small_all[:, :wide].reshape(D, near_vals)
    final_full = small_all[:, wide : 2 * wide].reshape(D, near_vals)
    vectors = cuts(small_all[:, 2 * wide : small_len].astype(F32), small_widths)
    gain_rows = jnp.transpose(vectors[0].reshape(count, 3, shard), (1, 0, 2)).reshape(3, D)
    offset_rows = jnp.transpose(vectors[1].reshape(count, 3, shard), (1, 0, 2)).reshape(3, D)
    skip_gains, skip_offsets = vectors[2].reshape(-1), vectors[3].reshape(-1)
    head_gains, head_offsets = vectors[4].reshape(4, HD), vectors[5].reshape(4, HD)
    bias_embed, bias_skip, bias_shift, bias_qkv = cuts(vectors[6].reshape(-1), (D, D, D, 3 * D))
    bias_out, bias_cross_q, bias_cross_o, bias_up, bias_down = cuts(
        vectors[7].reshape(-1), (D, D, D, FF, D)
    )
    bias_up_part = lax.dynamic_index_in_dim(
        bias_up.reshape(count, groups, hid_part), group_index, 1, keepdims=False
    ).reshape(-1)

    local_rows = row_index * tile_rows + jnp.arange(tile_rows, dtype=jnp.int32)
    local_cols = col_index * tile_cols + jnp.arange(tile_cols, dtype=jnp.int32)
    inside = (
        (local_rows[None, :, None] < extent[:, 0, None, None])
        & (local_cols[None, None, :] < extent[:, 1, None, None])
    ).astype(F32)
    token_inside = inside.reshape(img_count, tokens, 1)
    own_angle = angles_of(
        jnp.tile(jnp.repeat(local_rows, tile_cols), img_count),
        jnp.tile(jnp.tile(local_cols, tile_rows), img_count),
    )
    own_cos, own_sin = jnp.cos(own_angle), jnp.sin(own_angle)
    every = np.arange(count * tokens)
    every_row = every // tokens // col_count * tile_rows + every % tokens // tile_cols
    every_col = every // tokens % col_count * tile_cols + every % tile_cols
    every_angle = angles_of(jnp.asarray(every_row), jnp.asarray(every_col))
    every_cos, every_sin = jnp.cos(every_angle), jnp.sin(every_angle)
    job_images = (device * jobs + jnp.arange(jobs, dtype=jnp.int32)) % img_count
    ext_jobs = jnp.take(extent, job_images, axis=0)
    geo = (count, tile_rows, tile_cols, col_count, KEY_BLOCK // tokens)

    def gelu_tanh(values):
        return jax.nn.gelu(values, approximate=True)

    text_width = cross_keys.shape[1]
    text_count = -(-text.shape[1] // 128) * 128
    text_wide = jnp.pad(text, ((0, 0), (0, text_count - text.shape[1]), (0, 0)))
    is_key = device * text_width + jnp.arange(text_width, dtype=jnp.int32) < D

    def text_norm(values, scales, offsets):
        per_head = values.reshape(text_width // HD, HD, -1)
        centre = per_head - jnp.mean(per_head, axis=1, keepdims=True)
        spread = jnp.mean(centre * centre, axis=1, keepdims=True)
        unit = centre * lax.rsqrt(spread + NORM_EPS) * scales[:, None] + offsets[:, None]
        return jnp.where(is_key[:, None], unit.reshape(values.shape), values)

    text_part = dot(cross_keys, text_wide, (0,), (2,)).reshape(text_width, -1)
    text_part = text_part + cross_bias.astype(F32)[:, None]
    text_normed, text_pull = jax.vjp(text_norm, text_part, head_gains[3], head_offsets[3])
    moves = Moves()
    even_group = group_index % 2 == 0
    second_all = lax.all_gather(
        jnp.concatenate(
            [
                out_weight,
                lax.select(jnp.broadcast_to(even_group, cross_out.shape), cross_query, cross_out),
                beside(text_normed.astype(BF), 2),
            ],
            axis=1,
        ),
        GROUP,
        axis=0,
        tiled=True,
    )
    out_full, cross_mine = second_all[:, :D], second_all[:, D : 2 * D]
    cross_other = exchange(cross_mine, "img", 1)
    choose = jnp.broadcast_to(even_group, cross_mine.shape)
    cross_q_full = lax.select(choose, cross_mine, cross_other)
    cross_o_full = lax.select(choose, cross_other, cross_mine)
    text_both = below(second_all[:, 2 * D :], 2).reshape(2, HEADS, HD, img_count * text_count)
    third_all = lax.all_gather(third, GROUP, axis=0, tiled=True)
    third_rows = third_all.reshape(count, fold_rows, -1)
    up_full = third_rows[:, :shard, : count * hid_part].reshape(D, count * hid_part)
    down_full = below(third_all[:, count * hid_part :], folds)
    shift_sums = small_all[:, small_len : small_len + img_count * D].astype(F32)
    shift_rows = jnp.sum(shift_sums, axis=0).reshape(img_count, D) + bias_shift

    lat_masked = (latents * inside[..., None]).astype(BF)
    cot_masked = (cotangent * inside[..., None]).astype(BF)
    rims = with_halo(
        jnp.concatenate([lat_masked, cot_masked], axis=-1), (("row", 1), ("col", 2)), 1
    )
    rims = rims.astype(F32)
    near = gather_near(rims[..., :patch_vals], tile_rows, tile_cols)
    near = near.reshape(img_count, tokens, near_vals).astype(BF)
    cot_near = gather_near(rims[..., patch_vals:], tile_rows, tile_cols)
    cot_near = cot_near.reshape(img_count, tokens, near_vals)
    embedded = matmul_back(near, embed_t) + bias_embed
    joined_full = jnp.concatenate(
        [embedded, skip.reshape(img_count, tokens, D).astype(F32)], axis=-1
    )
    skip_normed, skip_norm_pull = jax.vjp(layer_norm, joined_full, skip_gains, skip_offsets)
    skip_in = skip_normed.astype(BF)
    resid_in = matmul(skip_in, skip_full) + bias_skip
    self_norm, self_norm_pull = jax.vjp(layer_norm, resid_in, gain_rows[0], offset_rows[0])
    normed = (self_norm + shift_rows[:, None, :]).astype(BF)

    qkv_t = dot(qkv_full, normed, (0,), (2,)) + bias_qkv[:, None, None]
    qkv_t = qkv_t.astype(BF).reshape(3, HEADS, HD, img_count, tokens)
    qkv_jobs = all_to_all(
        jnp.transpose(qkv_t, (1, 3, 0, 2, 4)).reshape(count, jobs, 3, HD, tokens)
    )
    head_cols = jnp.stack([head_gains[0], head_offsets[0], head_gains[1], head_offsets[1]], axis=1)
    mixed_jobs, keep, total = attend(ext_jobs, qkv_jobs, every_cos, every_sin, head_cols, geo)
    mixed = all_to_all(mixed_jobs).reshape(HEADS, img_count, HD, tokens)
    attended_t = jnp.transpose(mixed, (1, 0, 2, 3)).reshape(img_count, D, tokens)
    resid_self = resid_in + dot(attended_t, out_full, (1,), (0,)) + bias_out

    cross_norm, cross_norm_pull = jax.vjp(layer_norm, resid_self, gain_rows[1], offset_rows[1])
    cross_in = cross_norm.astype(BF)
    all_tokens = img_count * tokens
    cross_rows = dot(cross_q_full, cross_in.reshape(all_tokens, D), (0,), (1,))
    cross_rows = (cross_rows + bias_cross_q[:, None]).reshape(HEADS, HD, all_tokens)
    cross_cols = jnp.stack([head_gains[2], head_offsets[2]], axis=1)
    cross_mixed, cross_total = cross_attend(
        text_len, cross_rows, text_both, own_cos, own_sin, cross_cols
    )
    cross_low = cross_mixed.reshape(D, all_tokens)
    cross_out_rows = dot(cross_low, cross_o_full, (0,), (0,)).reshape(img_count, tokens, D)
    resid_cross = resid_self + cross_out_rows + bias_cross_o

    mlp_norm, mlp_norm_pull = jax.vjp(layer_norm, resid_cross, gain_rows[2], offset_rows[2])
    mlp_in = images_gather(mlp_norm.astype(BF))
    hidden = matmul(mlp_in, up_full) + bias_up_part
    gelu_out, gelu_pull = jax.vjp(gelu_tanh, hidden)
    activated = gelu_out.astype(BF)
    resid_out = resid_cross + images_scatter(matmul(activated, down_full)) + bias_down
    resid_low = resid_out.astype(BF)
    emitted = matmul(resid_low, final_full) * token_inside
    emit_rim = with_halo(
        emitted.reshape(img_count, tile_rows, tile_cols, near_vals), (("row", 1), ("col", 2)), 1
    )
    out_latents = spread_near(emit_rim, tile_rows, tile_cols, patch_vals) * inside[..., None]

    lead = (0, 1)
    by_row = row_first()
    grad_emitted = (cot_near * token_inside).astype(BF)
    grad_final = weight_grad(resid_low, grad_emitted)
    grad_resid_out = matmul_back(grad_emitted, final_full)
    grad_down_low = grad_resid_out.astype(BF)
    bias_down_grad = column_sum(grad_down_low)
    grad_down_rows = images_gather(grad_down_low)
    every_lead = (0, 1, 2)
    whole_down = dot(activated, grad_down_rows, every_lead, every_lead)
    grad_hidden = gelu_pull(matmul_back(grad_down_rows, down_full))[0].astype(BF)
    whole_up = dot(mlp_in, grad_hidden, every_lead, every_lead)
    bias_up_grad = column_sum(grad_hidden)
    grad_mlp_in = images_scatter(matmul_back(grad_hidden, up_full))
    grad_from_mlp, gain_mlp_grad, shift_mlp_grad = mlp_norm_pull(grad_mlp_in)
    grad_resid_cross = grad_resid_out + grad_from_mlp

    grad_cross_low = grad_resid_cross.astype(BF)
    grad_cross_flat = grad_cross_low.reshape(all_tokens, D)
    whole_grads = {"cross_o": dot(cross_low, grad_cross_flat, (1,), (0,))}
    bias_cross_o_grad = column_sum(grad_cross_low)
    grad_cross_mixed = dot(cross_o_full, grad_cross_flat, (1,), (1,)).astype(BF)
    grad_cross_rows, grad_text, cross_head_grads = cross_attend_back(
        text_len, cross_rows, text_both, grad_cross_mixed.reshape(HEADS, HD, all_tokens),
        cross_total, own_cos, own_sin, cross_cols,
    )
    cross_head_grads = jnp.sum(cross_head_grads, axis=0)
    grad_cross_rows = grad_cross_rows.reshape(D, all_tokens)
    grad_cross_rows = moves.begin(
        grad_cross_rows,
        text=offload_sum(alone, grad_text.reshape(2 * D, img_count * text_count)),
    )
    whole_grads["cross_q"] = dot(cross_in.reshape(all_tokens, D), grad_cross_rows, (0,), (1,))
    bias_cross_q_grad = jnp.sum(grad_cross_rows.astype(F32), axis=1)
    grad_cross_in = dot(grad_cross_rows, cross_q_full, (0,), (1,))
    grad_from_cross, gain_cross_grad, shift_cross_grad = cross_norm_pull(
        grad_cross_in.reshape(img_count, tokens, D)
    )
    grad_resid_self = grad_resid_cross + grad_from_cross

    grad_out_rows = grad_resid_self.astype(BF)
    whole_grads["out"] = dot(attended_t, grad_out_rows, (0, 2), lead)
    bias_out_grad = column_sum(grad_out_rows)
    grad_attended = dot(out_full, grad_out_rows, (1,), (2,)).astype(BF)
    grad_attended = jnp.transpose(
        grad_attended.reshape(HEADS, HD, img_count, tokens), (0, 2, 1, 3)
    )
    grad_mixed_jobs = all_to_all(grad_attended.reshape(count, jobs, HD, tokens))
    grad_jobs, head_grads = attend_back(
        ext_jobs, qkv_jobs, grad_mixed_jobs, keep, total, every_cos, every_sin, head_cols, geo
    )
    grad_qkv_t = all_to_all(grad_jobs).reshape(HEADS, img_count, 3, HD, tokens)
    grad_qkv_t = jnp.transpose(grad_qkv_t, (2, 0, 3, 1, 4)).reshape(3 * D, img_count, tokens)
    head_grads = jnp.sum(head_grads, axis=0)

    for i, name in enumerate(("query", "key", "value")):
        whole_grads[name] = dot(normed, grad_qkv_t[i * D : (i + 1) * D], (0, 1), (1, 2))
    bias_qkv_grad = jnp.sum(grad_qkv_t.astype(F32), axis=(1, 2))
    grad_normed = dot(grad_qkv_t, qkv_full, (0,), (1,))
    grad_shift_rows = jnp.sum(grad_normed, axis=1)
    bias_shift_grad = jnp.sum(grad_shift_rows, axis=0)
    grad_from_self, gain_self_grad, shift_self_grad = self_norm_pull(grad_normed)
    grad_resid_in = grad_resid_self + grad_from_self
    grad_merged = grad_resid_in.astype(BF)
    bias_skip_grad = column_sum(grad_merged)
    grad_skip_normed = matmul_back(grad_merged, skip_full)
    grad_joined, skip_gain_grad, skip_shift_grad = skip_norm_pull(grad_skip_normed)
    grad_skip = grad_joined[..., D:].reshape(img_count, tile_rows, tile_cols, D)
    grad_embedded = grad_joined[..., :D].astype(BF)
    grad_embed_t = weight_grad(grad_embedded, near)
    bias_embed_grad = column_sum(grad_embedded)
    grad_near = matmul(grad_embedded, embed_t).reshape(
        img_count, tile_rows, tile_cols, near_vals
    )
    near_rim = with_halo(grad_near, (("row", 1), ("col", 2)), 1)
    grad_latents = spread_near(near_rim, tile_rows, tile_cols, patch_vals) * inside[..., None]

    moves.finish(*list(moves.running))
    shards = moves.done
    grad_text_lin, head_gain_ck_grad, head_shift_ck_grad = text_pull(shards["text"])
    grad_text_low = grad_text_lin.astype(BF)
    grad_cross_keys = images_sum(
        dot(
            text_wide, grad_text_low.reshape(text_width, img_count, text_count), (0, 1), (1, 2)
        ),
        BF,
    )
    grad_cross_bias = images_sum(jnp.sum(grad_text_low.astype(F32), axis=1), F32)

    def by_device(vector):
        return vector.reshape(count, -1)

    def rows_by_device(rows):
        return jnp.transpose(rows.reshape(3, count, shard), (1, 0, 2)).reshape(count, -1)

    bias_up_all = jnp.where(
        (jnp.arange(groups) == group_index)[None, :, None],
        bias_up_grad.reshape(count, 1, hid_part),
        0.0,
    ).reshape(-1)
    small_grads = jnp.concatenate(
        [
            by_device(grad_embed_t),
            by_device(grad_final),
            rows_by_device(jnp.stack([gain_self_grad, gain_cross_grad, gain_mlp_grad])),
            rows_by_device(jnp.stack([shift_self_grad, shift_cross_grad, shift_mlp_grad])),
            by_device(skip_gain_grad),
            by_device(skip_shift_grad),
            by_device(
                jnp.concatenate(
                    [head_grads[:, 0], head_grads[:, 2], cross_head_grads[:, 0], head_gain_ck_grad]
                )
            ),
            by_device(
                jnp.concatenate(
                    [head_grads[:, 1], head_grads[:, 3], cross_head_grads[:, 1], head_shift_ck_grad]
                )
            ),
            by_device(
                jnp.concatenate([bias_embed_grad, bias_skip_grad, bias_shift_grad, bias_qkv_grad])
            ),
            by_device(
                jnp.concatenate(
                    [
                        bias_out_grad, bias_cross_q_grad, bias_cross_o_grad, bias_up_all,
                        bias_down_grad,
                    ]
                )
            ),
        ],
        axis=1,
    )
    shift_share = jnp.broadcast_to(grad_shift_rows.reshape(1, -1), (count, img_count * D))
    small_grads = jnp.concatenate([small_grads, shift_share], axis=1).astype(BF)
    small_grads = jnp.pad(small_grads, ((0, 0), (0, padded_len - small_grads.shape[1])))
    skip_late, small_grads = lax.optimization_barrier((skip_in, small_grads))
    whole_grads["skip"] = weight_grad(skip_late, grad_merged)
    small_got = all_to_all(small_grads.reshape(count, -1, 128))
    names = ("query", "key", "value", "skip", "out", "cross_q", "cross_o")
    packed = [whole_grads[name].astype(BF).reshape(count, -1, D) for name in names]
    packed_rows = sum(part.shape[1] for part in packed)
    fill = -packed_rows % (16 * groups)
    packed = jnp.pad(jnp.concatenate(packed, axis=1), ((0, 0), (0, fill), (0, 0)))
    up_rows = jnp.pad(
        whole_up.astype(BF).reshape(count, shard, -1), ((0, 0), (0, -shard % 16), (0, 0))
    )
    down_rows = whole_down.astype(BF).reshape(count, hid_part, D)
    packed, small_got = lax.optimization_barrier((packed, small_got))
    summed, up_sums, down_sums = sum_everywhere(
        packed, down_rows, up_rows, (groups, row_count, col_count)
    )
    summed = summed.astype(F32)
    total_of, at = {}, 0
    for name in names:
        rows = whole_grads[name].shape[0] // count
        total_of[name] = summed[at : at + rows]
        at += rows
    small_got = jnp.sum(small_got.astype(F32), axis=0).reshape(-1)
    small_sum = images_sum(small_got[:small_len], F32)
    total_parts = cuts(small_sum, (wide, wide) + small_widths)
    grad_shift = lax.dot_general(
        time_own.astype(F32),
        small_got[small_len : small_len + img_count * D].reshape(img_count, D),
        (((0,), (0,)), ((), ())),
        precision=lax.Precision.HIGHEST,
    )

    total_up = jnp.transpose(
        up_sums[:, :shard].reshape(groups, shard, count, hid_part), (1, 2, 0, 3)
    ).reshape(shard, FF)
    total_down = down_sums.reshape(hid_shard, D)
    return (
        out_latents,
        grad_latents,
        grad_skip,
        total_parts[0].reshape(shard, near_vals).T,
        total_of["skip"],
        images_sum(grad_shift, F32),
        jnp.concatenate([total_of[name] for name in ("query", "key", "value")], axis=1),
        total_of["out"],
        total_of["cross_q"],
        grad_cross_keys,
        total_of["cross_o"],
        total_up.astype(F32),
        total_down.astype(F32),
        total_parts[1].reshape(shard, near_vals),
        total_parts[2].reshape(3, shard),
        total_parts[3].reshape(3, shard),
        total_parts[4],
        total_parts[5],
        total_parts[6],
        total_parts[7],
        total_parts[8],
        total_parts[9],
        grad_cross_bias,
    )


def solution(mesh):
    tile = P("img", "row", "col", None)
    rows = P(GROUP, None)
    columns = P(None, GROUP)
    vector = P(GROUP)
    return jax.shard_map(
        body,
        mesh=mesh,
        in_specs=(
            tile, tile, P("img", None), P("img", None, None), P("img", None), P("img", None),
            columns, rows, rows, rows, rows, rows, columns, rows, rows, rows, rows,
            columns, columns, vector, vector, vector, vector, vector, vector, vector, tile,
        ),
        out_specs=(
            tile, tile, tile, columns, rows, rows, rows, rows, rows, columns, rows, rows, rows,
            rows, columns, columns, vector, vector, vector, vector, vector, vector, vector,
        ),
        check_vma=False,
    )
```
